32 devices in a mesh: grp: 2 (over y), row: 8 (over z, x), sub: 2 (over core).
Axes of the slice: x: 2, y: 2, z: 4, core: 2. Of those that a mesh axis runs over, the one named last changes fastest.
Arguments:
- pair_rep: bfloat16 [64, 32, 128], P(('grp', 'row'), 'sub'), parts along dimension 0, may hold values from -6 to 6
- norm_gain: float32 [128], replicated, may hold values from 0.1 to 1.9
- norm_bias: float32 [128], replicated, may hold values from -3 to 3
- w_a_proj: bfloat16 [128, 128], replicated, may hold values from -0.5 to 0.5
- w_a_gate: bfloat16 [128, 128], replicated, may hold values from -0.5 to 0.5
- w_b_proj: bfloat16 [128, 128], replicated, may hold values from -0.5 to 0.5
- w_b_gate: bfloat16 [128, 128], replicated, may hold values from -0.5 to 0.5
- w_gate: bfloat16 [128, 128], replicated, may hold values from -0.5 to 0.5
- out_gain: float32 [128], replicated, may hold values from 0.1 to 1.9
- out_bias: float32 [128], replicated, may hold values from -3 to 3
- w_out: bfloat16 [128, 128], replicated, may hold values from -0.5 to 0.5
Outputs:
- update: bfloat16 [64, 32, 128], P(('grp', 'row'), 'sub'), parts along dimension 0
The draws below stay inside these ranges and needn't reach their ends.
There are 2 independent parts, one for each index of `grp`. The reference program is written for one: setup_inputs(seed, part) draws one part's arguments, and reference() takes and returns one part's arrays. A program takes and returns all parts, laid end to end along the dimension named above; an argument that names none is the same for every part. Nothing has to cross between parts.
All inputs are finite; a program needn't handle non-finite values.
Results may differ from the reference program's by a relative error of at most 0.012.
Values may be sent and summed in bfloat16 or wider, within the bound.
No kernel may reach another device: no remote copies, remote signals or barrier semaphores. Data moves between devices by JAX's collectives and lax.ppermute only.
A program may use at most 64 MiB of HBM per device.

```python
import jax
import jax.numpy as jnp
from jax import lax

C = 128
H = 128
ROWS_DEV = 4
TOKENS = 32
N_ROW = 8


def block_levels(stream_key, dims, pieces, least, high):
    def one(position, blocks):
        heights = jax.random.uniform(jax.random.fold_in(jax.random.fold_in(stream_key, 6), position), (blocks,), jnp.float32, least / len(pieces), high / len(pieces))
        return jnp.repeat(jnp.exp(heights), dims[position] // blocks).reshape((-1,) + (1,) * (len(dims) - position - 1))

    level = one(*pieces[0])
    for cut in pieces[1:]:
        level = level * one(*cut)
    return level


def bell_draw(rng, shape, deviation, most, split=(), dtype=jnp.bfloat16):
    level = block_levels(rng, shape, split, -0.22, 0.18) if split else 1.0
    entries = jax.random.normal(rng, shape, jnp.float32) * deviation * level
    return jnp.minimum(jnp.maximum(entries, -most), most).astype(dtype)


def setup_inputs(seed: int = 0, part: int = 0) -> dict:
    key_list = jax.random.split(jax.random.key(seed), 12)
    part_keys = jax.random.split(jax.random.fold_in(key_list[11], part), 12)
    pair_rep = bell_draw(part_keys[0], (TOKENS, TOKENS, C), 1.0, 6.0, ((0, 8), (1, 2)))
    norm_gain = jnp.clip(1.0 + 0.18 * jax.random.normal(key_list[1], (C,), jnp.float32), 0.1, 1.9)
    norm_bias = bell_draw(key_list[2], (C,), 0.5, 3.0, (), jnp.float32)
    w_a_proj = bell_draw(key_list[3], (C, H), C ** -0.5, 0.5)
    w_a_gate = bell_draw(key_list[4], (C, H), C ** -0.5, 0.5)
    w_b_proj = bell_draw(key_list[5], (C, H), C ** -0.5, 0.5)
    w_b_gate = bell_draw(key_list[6], (C, H), C ** -0.5, 0.5)
    w_gate = bell_draw(key_list[7], (C, C), C ** -0.5, 0.5)
    out_gain = jnp.clip(1.0 + 0.18 * jax.random.normal(key_list[8], (H,), jnp.float32), 0.1, 1.9)
    out_bias = bell_draw(key_list[9], (H,), 0.5, 3.0, (), jnp.float32)
    w_out = bell_draw(key_list[10], (H, C), H ** -0.5, 0.5)
    return dict(pair_rep=pair_rep, norm_gain=norm_gain, norm_bias=norm_bias, w_a_proj=w_a_proj, w_a_gate=w_a_gate, w_b_proj=w_b_proj, w_b_gate=w_b_gate, w_gate=w_gate, out_gain=out_gain, out_bias=out_bias, w_out=w_out)


EPSILON = 1e-05

def layer_norm(values, gain, shift, axis):
    centred = values - lax.optimization_barrier(jnp.mean(values, axis=axis, keepdims=True))
    variance = lax.optimization_barrier(jnp.mean(centred * centred, axis=axis, keepdims=True))
    return centred * lax.rsqrt(variance + EPSILON) * gain + shift

def reference(pair_rep, norm_gain, norm_bias, w_a_proj, w_a_gate, w_b_proj, w_b_gate, w_gate, out_gain, out_bias, w_out):
    w_inner = jnp.concatenate([w_a_proj, w_a_gate, w_b_proj, w_b_gate], axis=1)

    def project(block):
        normed = layer_norm(block.astype(jnp.float32), norm_gain, norm_bias, -1).astype(jnp.bfloat16)
        flat_rows = normed.reshape(-1, C)
        inner = jnp.dot(flat_rows, w_inner, preferred_element_type=jnp.float32)
        left_act = (jax.nn.sigmoid(inner[:, H:2 * H]) * inner[:, :H]).astype(jnp.bfloat16)
        right_act = (jax.nn.sigmoid(inner[:, 3 * H:4 * H]) * inner[:, 2 * H:3 * H]).astype(jnp.bfloat16)
        gating = jax.nn.sigmoid(jnp.dot(flat_rows, w_gate, preferred_element_type=jnp.float32)).astype(jnp.bfloat16)
        return (left_act.reshape(ROWS_DEV, TOKENS, H), right_act.reshape(ROWS_DEV, TOKENS, H), gating.reshape(ROWS_DEV, TOKENS, C))
    blocks = pair_rep.reshape(N_ROW, ROWS_DEV, TOKENS, C)
    left_act, right_act, gating = lax.map(project, blocks)
    left_t = jnp.transpose(left_act.reshape(TOKENS, TOKENS, H), (2, 0, 1))
    right_t = jnp.transpose(right_act.reshape(TOKENS, TOKENS, H), (2, 0, 1))

    def channel(operands):
        left_one, right_one = operands
        return jnp.dot(left_one, right_one.T, preferred_element_type=jnp.float32).astype(jnp.bfloat16)
    triangle = lax.map(channel, (left_t, right_t))
    tri_rows = jnp.transpose(triangle, (1, 2, 0)).reshape(N_ROW, ROWS_DEV, TOKENS, H)

    def finish(operands):
        tri_block, gate_block = operands
        normed = layer_norm(tri_block.astype(jnp.float32), out_gain, out_bias, -1).astype(jnp.bfloat16)
        mixed = jnp.dot(normed.reshape(-1, H), w_out, preferred_element_type=jnp.float32)
        result = gate_block.reshape(-1, C).astype(jnp.float32) * mixed
        return result.astype(jnp.bfloat16).reshape(ROWS_DEV, TOKENS, C)
    return lax.map(finish, (tri_rows, gating)).reshape(TOKENS, TOKENS, C)
```

```python
import functools

import jax
import jax.numpy as jnp
from jax import lax
from jax.experimental import pallas as pl
from jax.experimental.pallas import tpu as pltpu
from jax.sharding import PartitionSpec as P

EPSILON = 1e-05
GATHER_BYTES = 2 * 1024 * 1024


def layer_norm(values, gain, shift, axis):
    centred = values - jnp.mean(values, axis=axis, keepdims=True)
    variance = jnp.mean(centred * centred, axis=axis, keepdims=True)
    return centred * lax.rsqrt(variance + EPSILON) * gain + shift


def gated(rows, w_proj, w_gate):
    proj = jnp.dot(rows, w_proj, preferred_element_type=jnp.float32)
    gate = jnp.dot(rows, w_gate, preferred_element_type=jnp.float32)
    return (jax.nn.sigmoid(gate) * proj).astype(jnp.bfloat16).astype(jnp.float32)


def triangle_kernel(
    n_sub,
    blocks_ref,
    norm_gain_ref,
    norm_bias_ref,
    w_a_proj_ref,
    w_a_gate_ref,
    w_b_proj_ref,
    w_b_gate_ref,
    w_gate_ref,
    out_gain_ref,
    out_bias_ref,
    w_out_ref,
    update_ref,
):
    n_blocks, rows, cols, width = blocks_ref.shape
    hidden = w_out_ref.shape[0]
    row = lax.axis_index("row")
    sub = lax.axis_index("sub")
    right_blocks = n_blocks // n_sub
    right_rows = right_blocks // n_sub
    gain, bias = norm_gain_ref[...], norm_bias_ref[...]

    def normed(values):
        flat = values.reshape(-1, width).astype(jnp.float32)
        return layer_norm(flat, gain, bias, -1).astype(jnp.bfloat16)

    right_in = normed(blocks_ref[pl.ds(sub * right_blocks, right_blocks)])
    right = gated(right_in, w_b_proj_ref[...], w_b_gate_ref[...])
    right = right.reshape(right_rows, n_sub, rows, cols, hidden)
    left_in = normed(blocks_ref[pl.ds(row * n_sub, n_sub)])
    left = gated(left_in, w_a_proj_ref[...], w_a_gate_ref[...])
    left = left.reshape(n_sub, rows, cols, hidden)
    own_in = normed(blocks_ref[row * n_sub + sub])
    gating = jax.nn.sigmoid(jnp.dot(own_in, w_gate_ref[...], preferred_element_type=jnp.float32))
    gating = gating.astype(jnp.bfloat16).astype(jnp.float32)

    sums = []
    for i in range(rows):
        products = right[:, 0] * left[0, i]
        for part in range(1, n_sub):
            products = products + right[:, part] * left[part, i]
        sums.append(jnp.sum(products, axis=2).reshape(right_rows * rows, hidden))
    triangle = jnp.concatenate(sums, axis=0).astype(jnp.bfloat16).astype(jnp.float32)
    hidden_normed = layer_norm(triangle, out_gain_ref[...], out_bias_ref[...], -1)
    mixed = jnp.dot(
        hidden_normed.astype(jnp.bfloat16), w_out_ref[...], preferred_element_type=jnp.float32
    )
    update_ref[...] = (gating * mixed).astype(jnp.bfloat16).reshape(update_ref.shape)


def gather_rows(
    n_sub,
    pair_rep,
    norm_gain,
    norm_bias,
    w_a_proj,
    w_a_gate,
    w_b_proj,
    w_b_gate,
    w_gate,
    out_gain,
    out_bias,
    w_out,
):
    blocks = lax.all_gather(pair_rep, ("row", "sub"), axis=0, tiled=False)
    return pl.pallas_call(
        functools.partial(triangle_kernel, n_sub),
        out_shape=jax.ShapeDtypeStruct(pair_rep.shape, pair_rep.dtype),
    )(
        blocks,
        norm_gain[None],
        norm_bias[None],
        w_a_proj,
        w_a_gate,
        w_b_proj,
        w_b_gate,
        w_gate,
        out_gain[None],
        out_bias[None],
        w_out,
    )


def exchange_channels(
    pair_rep,
    norm_gain,
    norm_bias,
    w_a_proj,
    w_a_gate,
    w_b_proj,
    w_b_gate,
    w_gate,
    out_gain,
    out_bias,
    w_out,
):
    hidden = w_a_proj.shape[1]
    w_inner = jnp.concatenate([w_a_proj, w_a_gate, w_b_proj, w_b_gate], axis=1)
    normed = layer_norm(pair_rep.astype(jnp.float32), norm_gain, norm_bias, -1).astype(jnp.bfloat16)
    inner = jnp.einsum("rkc,cm->mrk", normed, w_inner, preferred_element_type=jnp.float32)
    left_local = (jax.nn.sigmoid(inner[hidden : 2 * hidden]) * inner[:hidden]).astype(jnp.bfloat16)
    right_local = (
        jax.nn.sigmoid(inner[3 * hidden : 4 * hidden]) * inner[2 * hidden : 3 * hidden]
    ).astype(jnp.bfloat16)
    gating = jax.nn.sigmoid(
        jnp.einsum("rkc,cd->rkd", normed, w_gate, preferred_element_type=jnp.float32)
    ).astype(jnp.bfloat16)
    left_chan, right_chan = (
        lax.all_to_all(left_local, "row", split_axis=0, concat_axis=1, tiled=True),
        lax.all_to_all(right_local, "row", split_axis=0, concat_axis=1, tiled=True),
    )
    left_rows = lax.all_to_all(left_chan, "sub", split_axis=1, concat_axis=2, tiled=True)
    triangle = jnp.einsum(
        "hik,hjk->hij",
        left_rows,
        lax.all_gather(right_chan, "sub", axis=2, tiled=True),
        preferred_element_type=jnp.float32,
    ).astype(jnp.bfloat16)
    regrouped = lax.all_to_all(
        lax.all_to_all(triangle, "sub", split_axis=2, concat_axis=1, tiled=True),
        "row",
        split_axis=1,
        concat_axis=0,
        tiled=True,
    )
    hidden_normed = layer_norm(
        regrouped.astype(jnp.float32), out_gain[:, None, None], out_bias[:, None, None], 0
    ).astype(jnp.bfloat16)
    mixed = jnp.einsum("hrj,hc->rjc", hidden_normed, w_out, preferred_element_type=jnp.float32)
    return (gating.astype(jnp.float32) * mixed).astype(jnp.bfloat16)


def solution(mesh):
    n_row, n_sub = mesh.shape["row"], mesh.shape["sub"]

    def per_device(pair_rep, *weights):
        gathered = n_row * n_sub * pair_rep.size * pair_rep.dtype.itemsize
        if gathered <= GATHER_BYTES:
            return gather_rows(n_sub, pair_rep, *weights)
        return exchange_channels(pair_rep, *weights)

    in_specs = (P(("grp", "row"), "sub", None), P(), P(), P(), P(), P(), P(), P(), P(), P(), P())
    out_specs = P(("grp", "row"), "sub", None)
    return jax.shard_map(
        per_device, mesh=mesh, in_specs=in_specs, out_specs=out_specs, check_vma=False
    )
```

```python
import functools

import jax
import jax.numpy as jnp
from jax import lax
from jax.experimental import pallas as pl
from jax.experimental.pallas import tpu as pltpu
from jax.sharding import PartitionSpec as P

EPSILON = 1e-05
GATHER_BYTES = 2 * 1024 * 1024


def layer_norm(values, gain, shift, axis):
    centred = values - jnp.mean(values, axis=axis, keepdims=True)
    variance = jnp.mean(centred * centred, axis=axis, keepdims=True)
    return centred * lax.rsqrt(variance + EPSILON) * gain + shift


def gated(rows, w_proj, w_gate):
    proj = jnp.dot(rows, w_proj, preferred_element_type=jnp.float32)
    gate = jnp.dot(rows, w_gate, preferred_element_type=jnp.float32)
    return (jax.nn.sigmoid(gate) * proj).astype(jnp.bfloat16).astype(jnp.float32)


def triangle_kernel(n_row, n_sub, *refs):
    own_ref, other_refs, refs = refs[0], refs[1:n_sub], refs[n_sub:]
    block_refs, refs = refs[:n_row], refs[n_row:]
    (
        norm_gain_ref,
        norm_bias_ref,
        w_a_proj_ref,
        w_a_gate_ref,
        w_b_proj_ref,
        w_b_gate_ref,
        w_gate_ref,
        out_gain_ref,
        out_bias_ref,
        w_out_ref,
        update_ref,
        left_ref,
        right_ref,
    ) = refs
    rows, cols, width = own_ref.shape
    hidden = w_out_ref.shape[0]
    span = n_row // n_sub
    row = lax.axis_index("row")
    sub = lax.axis_index("sub")
    gain, bias = norm_gain_ref[...], norm_bias_ref[...]

    def normed(values):
        flat = values.reshape(-1, width).astype(jnp.float32)
        return layer_norm(flat, gain, bias, -1).astype(jnp.bfloat16)

    for step in range(n_row):
        source_row, source_sub = step // n_sub, step % n_sub
        place = (lax.rem(row + source_row, span)) * n_sub + lax.rem(row // span + source_sub, n_sub)
        right_ref[pl.ds(place, 1)] = block_refs[step][...][None]
    left_ref[pl.ds(sub, 1)] = own_ref[...][None]
    for step in range(1, n_sub):
        left_ref[pl.ds(lax.rem(sub + step, n_sub), 1)] = other_refs[step - 1][...][None]

    right = gated(normed(right_ref[...]), w_b_proj_ref[...], w_b_gate_ref[...])
    right = right.reshape(span, n_sub, rows, cols, hidden)
    left = gated(normed(left_ref[...]), w_a_proj_ref[...], w_a_gate_ref[...])
    left = left.reshape(n_sub, rows, cols, hidden)
    own_in = normed(own_ref[...])
    gating = jax.nn.sigmoid(jnp.dot(own_in, w_gate_ref[...], preferred_element_type=jnp.float32))
    gating = gating.astype(jnp.bfloat16).astype(jnp.float32)

    sums = []
    for i in range(rows):
        products = right[:, 0] * left[0, i]
        for part in range(1, n_sub):
            products = products + right[:, part] * left[part, i]
        sums.append(jnp.sum(products, axis=2).reshape(span * rows, hidden))
    triangle = jnp.concatenate(sums, axis=0).astype(jnp.bfloat16).astype(jnp.float32)
    hidden_normed = layer_norm(triangle, out_gain_ref[...], out_bias_ref[...], -1)
    mixed = jnp.dot(
        hidden_normed.astype(jnp.bfloat16), w_out_ref[...], preferred_element_type=jnp.float32
    )
    update_ref[...] = (gating * mixed).astype(jnp.bfloat16).reshape(update_ref.shape)


def send_rows(
    n_row,
    n_sub,
    pair_rep,
    norm_gain,
    norm_bias,
    w_a_proj,
    w_a_gate,
    w_b_proj,
    w_b_gate,
    w_gate,
    out_gain,
    out_bias,
    w_out,
):
    span = n_row // n_sub
    devices = [(row, sub) for row in range(n_row) for sub in range(n_sub)]

    def receive(source):
        pairs = [(source(row, sub), (row, sub)) for row, sub in devices]
        pairs = [(a[0] * n_sub + a[1], b[0] * n_sub + b[1]) for a, b in pairs]
        return lax.ppermute(pair_rep, ("row", "sub"), pairs)

    others = [
        receive(lambda row, sub: (row, (sub + step) % n_sub)) for step in range(1, n_sub)
    ]
    blocks = [
        receive(
            lambda row, sub: (
                sub * span + (row + step // n_sub) % span,
                (row // span + step % n_sub) % n_sub,
            )
        )
        for step in range(n_row)
    ]
    return pl.pallas_call(
        functools.partial(triangle_kernel, n_row, n_sub),
        out_shape=jax.ShapeDtypeStruct(pair_rep.shape, pair_rep.dtype),
        scratch_shapes=[
            pltpu.VMEM((n_sub,) + pair_rep.shape, pair_rep.dtype),
            pltpu.VMEM((n_row,) + pair_rep.shape, pair_rep.dtype),
        ],
    )(
        pair_rep,
        *others,
        *blocks,
        norm_gain[None],
        norm_bias[None],
        w_a_proj,
        w_a_gate,
        w_b_proj,
        w_b_gate,
        w_gate,
        out_gain[None],
        out_bias[None],
        w_out,
    )


def exchange_channels(
    pair_rep,
    norm_gain,
    norm_bias,
    w_a_proj,
    w_a_gate,
    w_b_proj,
    w_b_gate,
    w_gate,
    out_gain,
    out_bias,
    w_out,
):
    hidden = w_a_proj.shape[1]
    w_inner = jnp.concatenate([w_a_proj, w_a_gate, w_b_proj, w_b_gate], axis=1)
    normed = layer_norm(pair_rep.astype(jnp.float32), norm_gain, norm_bias, -1).astype(jnp.bfloat16)
    inner = jnp.einsum("rkc,cm->mrk", normed, w_inner, preferred_element_type=jnp.float32)
    left_local = (jax.nn.sigmoid(inner[hidden : 2 * hidden]) * inner[:hidden]).astype(jnp.bfloat16)
    right_local = (
        jax.nn.sigmoid(inner[3 * hidden : 4 * hidden]) * inner[2 * hidden : 3 * hidden]
    ).astype(jnp.bfloat16)
    gating = jax.nn.sigmoid(
        jnp.einsum("rkc,cd->rkd", normed, w_gate, preferred_element_type=jnp.float32)
    ).astype(jnp.bfloat16)
    left_chan, right_chan = (
        lax.all_to_all(left_local, "row", split_axis=0, concat_axis=1, tiled=True),
        lax.all_to_all(right_local, "row", split_axis=0, concat_axis=1, tiled=True),
    )
    left_rows = lax.all_to_all(left_chan, "sub", split_axis=1, concat_axis=2, tiled=True)
    triangle = jnp.einsum(
        "hik,hjk->hij",
        left_rows,
        lax.all_gather(right_chan, "sub", axis=2, tiled=True),
        preferred_element_type=jnp.float32,
    ).astype(jnp.bfloat16)
    regrouped = lax.all_to_all(
        lax.all_to_all(triangle, "sub", split_axis=2, concat_axis=1, tiled=True),
        "row",
        split_axis=1,
        concat_axis=0,
        tiled=True,
    )
    hidden_normed = layer_norm(
        regrouped.astype(jnp.float32), out_gain[:, None, None], out_bias[:, None, None], 0
    ).astype(jnp.bfloat16)
    mixed = jnp.einsum("hrj,hc->rjc", hidden_normed, w_out, preferred_element_type=jnp.float32)
    return (gating.astype(jnp.float32) * mixed).astype(jnp.bfloat16)


def solution(mesh):
    n_row, n_sub = mesh.shape["row"], mesh.shape["sub"]

    def per_device(pair_rep, *weights):
        gathered = n_row * n_sub * pair_rep.size * pair_rep.dtype.itemsize
        if gathered <= GATHER_BYTES:
            return send_rows(n_row, n_sub, pair_rep, *weights)
        return exchange_channels(pair_rep, *weights)

    in_specs = (P(("grp", "row"), "sub", None), P(), P(), P(), P(), P(), P(), P(), P(), P(), P())
    out_specs = P(("grp", "row"), "sub", None)
    return jax.shard_map(
        per_device, mesh=mesh, in_specs=in_specs, out_specs=out_specs, check_vma=False
    )
```

```python
import functools

import jax
import jax.numpy as jnp
from jax import lax
from jax.experimental import pallas as pl
from jax.experimental.pallas import tpu as pltpu
from jax.sharding import PartitionSpec as P

EPSILON = 1e-05
GATHER_BYTES = 2 * 1024 * 1024


def layer_norm(values, gain, shift, axis):
    centred = values - jnp.mean(values, axis=axis, keepdims=True)
    variance = jnp.mean(centred * centred, axis=axis, keepdims=True)
    return centred * lax.rsqrt(variance + EPSILON) * gain + shift


def gated(rows, w_proj, w_gate):
    proj = jnp.dot(rows, w_proj, preferred_element_type=jnp.float32)
    gate = jnp.dot(rows, w_gate, preferred_element_type=jnp.float32)
    return (jax.nn.sigmoid(gate) * proj).astype(jnp.bfloat16).astype(jnp.float32)


def triangle_kernel(n_row, n_sub, *refs):
    (
        blocks_ref,
        norm_gain_ref,
        norm_bias_ref,
        w_a_proj_ref,
        w_a_gate_ref,
        w_b_proj_ref,
        w_b_gate_ref,
        w_gate_ref,
        out_gain_ref,
        out_bias_ref,
        w_out_ref,
        update_ref,
        left_ref,
        right_ref,
    ) = refs
    _, rows, cols, width = blocks_ref.shape
    hidden = w_out_ref.shape[0]
    span = n_row // n_sub
    row = lax.axis_index("row")
    sub = lax.axis_index("sub")
    gain, bias = norm_gain_ref[...], norm_bias_ref[...]

    def normed(values):
        flat = values.reshape(-1, width).astype(jnp.float32)
        return layer_norm(flat, gain, bias, -1).astype(jnp.bfloat16)

    def block(other_row, other_sub):
        difference = (row ^ other_row) * n_sub + (sub ^ other_sub)
        return blocks_ref[pl.ds(place_of(difference, n_row * n_sub), 1)]

    def place_of(difference, total):
        place, weight = 0, 1
        while weight < total:
            place = place * 2 + difference % 2
            difference = difference // 2
            weight *= 2
        return place

    for step in range(n_row):
        right_ref[step : step + 1] = block(sub * span + step // n_sub, step % n_sub)
    for step in range(n_sub):
        left_ref[step : step + 1] = block(row, step)

    right = gated(normed(right_ref[...]), w_b_proj_ref[...], w_b_gate_ref[...])
    right = right.reshape(span, n_sub, rows, cols, hidden)
    left = gated(normed(left_ref[...]), w_a_proj_ref[...], w_a_gate_ref[...])
    left = left.reshape(n_sub, rows, cols, hidden)
    own_in = normed(blocks_ref[0])
    gating = jax.nn.sigmoid(jnp.dot(own_in, w_gate_ref[...], preferred_element_type=jnp.float32))
    gating = gating.astype(jnp.bfloat16).astype(jnp.float32)

    sums = []
    for i in range(rows):
        products = right[:, 0] * left[0, i]
        for part in range(1, n_sub):
            products = products + right[:, part] * left[part, i]
        sums.append(jnp.sum(products, axis=2).reshape(span * rows, hidden))
    triangle = jnp.concatenate(sums, axis=0).astype(jnp.bfloat16).astype(jnp.float32)
    hidden_normed = layer_norm(triangle, out_gain_ref[...], out_bias_ref[...], -1)
    mixed = jnp.dot(
        hidden_normed.astype(jnp.bfloat16), w_out_ref[...], preferred_element_type=jnp.float32
    )
    update_ref[...] = (gating * mixed).astype(jnp.bfloat16).reshape(update_ref.shape)


def double_rows(
    n_row,
    n_sub,
    pair_rep,
    norm_gain,
    norm_bias,
    w_a_proj,
    w_a_gate,
    w_b_proj,
    w_b_gate,
    w_gate,
    out_gain,
    out_bias,
    w_out,
):
    total = n_row * n_sub
    blocks = pair_rep[None]
    bit = total // 2
    while bit:
        received = lax.ppermute(blocks, ("row", "sub"), [(place, place ^ bit) for place in range(total)])
        blocks = jnp.concatenate([blocks, received], axis=0)
        bit //= 2
    return pl.pallas_call(
        functools.partial(triangle_kernel, n_row, n_sub),
        out_shape=jax.ShapeDtypeStruct(pair_rep.shape, pair_rep.dtype),
        scratch_shapes=[
            pltpu.VMEM((n_sub,) + pair_rep.shape, pair_rep.dtype),
            pltpu.VMEM((n_row,) + pair_rep.shape, pair_rep.dtype),
        ],
    )(
        blocks,
        norm_gain[None],
        norm_bias[None],
        w_a_proj,
        w_a_gate,
        w_b_proj,
        w_b_gate,
        w_gate,
        out_gain[None],
        out_bias[None],
        w_out,
    )


def exchange_channels(
    pair_rep,
    norm_gain,
    norm_bias,
    w_a_proj,
    w_a_gate,
    w_b_proj,
    w_b_gate,
    w_gate,
    out_gain,
    out_bias,
    w_out,
):
    hidden = w_a_proj.shape[1]
    w_inner = jnp.concatenate([w_a_proj, w_a_gate, w_b_proj, w_b_gate], axis=1)
    normed = layer_norm(pair_rep.astype(jnp.float32), norm_gain, norm_bias, -1).astype(jnp.bfloat16)
    inner = jnp.einsum("rkc,cm->mrk", normed, w_inner, preferred_element_type=jnp.float32)
    left_local = (jax.nn.sigmoid(inner[hidden : 2 * hidden]) * inner[:hidden]).astype(jnp.bfloat16)
    right_local = (
        jax.nn.sigmoid(inner[3 * hidden : 4 * hidden]) * inner[2 * hidden : 3 * hidden]
    ).astype(jnp.bfloat16)
    gating = jax.nn.sigmoid(
        jnp.einsum("rkc,cd->rkd", normed, w_gate, preferred_element_type=jnp.float32)
    ).astype(jnp.bfloat16)
    left_chan, right_chan = (
        lax.all_to_all(left_local, "row", split_axis=0, concat_axis=1, tiled=True),
        lax.all_to_all(right_local, "row", split_axis=0, concat_axis=1, tiled=True),
    )
    left_rows = lax.all_to_all(left_chan, "sub", split_axis=1, concat_axis=2, tiled=True)
    triangle = jnp.einsum(
        "hik,hjk->hij",
        left_rows,
        lax.all_gather(right_chan, "sub", axis=2, tiled=True),
        preferred_element_type=jnp.float32,
    ).astype(jnp.bfloat16)
    regrouped = lax.all_to_all(
        lax.all_to_all(triangle, "sub", split_axis=2, concat_axis=1, tiled=True),
        "row",
        split_axis=1,
        concat_axis=0,
        tiled=True,
    )
    hidden_normed = layer_norm(
        regrouped.astype(jnp.float32), out_gain[:, None, None], out_bias[:, None, None], 0
    ).astype(jnp.bfloat16)
    mixed = jnp.einsum("hrj,hc->rjc", hidden_normed, w_out, preferred_element_type=jnp.float32)
    return (gating.astype(jnp.float32) * mixed).astype(jnp.bfloat16)


def solution(mesh):
    n_row, n_sub = mesh.shape["row"], mesh.shape["sub"]

    def per_device(pair_rep, *weights):
        gathered = n_row * n_sub * pair_rep.size * pair_rep.dtype.itemsize
        doubles = (n_row * n_sub) & (n_row * n_sub - 1) == 0
        if doubles and gathered <= GATHER_BYTES:
            return double_rows(n_row, n_sub, pair_rep, *weights)
        return exchange_channels(pair_rep, *weights)

    in_specs = (P(("grp", "row"), "sub", None), P(), P(), P(), P(), P(), P(), P(), P(), P(), P())
    out_specs = P(("grp", "row"), "sub", None)
    return jax.shard_map(
        per_device, mesh=mesh, in_specs=in_specs, out_specs=out_specs, check_vma=False
    )
```

```python
import functools

import jax
import jax.numpy as jnp
from jax import lax
from jax.experimental import pallas as pl
from jax.experimental.pallas import tpu as pltpu
from jax.sharding import PartitionSpec as P

EPSILON = 1e-05
GATHER_BYTES = 2 * 1024 * 1024


def layer_norm(values, gain, shift, axis):
    centred = values - jnp.mean(values, axis=axis, keepdims=True)
    variance = jnp.mean(centred * centred, axis=axis, keepdims=True)
    return centred * lax.rsqrt(variance + EPSILON) * gain + shift


def gated(rows, w_proj, w_gate):
    proj = jnp.dot(rows, w_proj, preferred_element_type=jnp.float32)
    gate = jnp.dot(rows, w_gate, preferred_element_type=jnp.float32)
    return (jax.nn.sigmoid(gate) * proj).astype(jnp.bfloat16).astype(jnp.float32)


def triangle_kernel(span, *refs):
    own_ref, sent_refs, refs = refs[0], refs[1 : 2 * span + 1], refs[2 * span + 1 :]
    (
        norm_gain_ref,
        norm_bias_ref,
        w_a_proj_ref,
        w_a_gate_ref,
        w_b_proj_ref,
        w_b_gate_ref,
        w_gate_ref,
        out_gain_ref,
        out_bias_ref,
        w_out_ref,
        update_ref,
        left_ref,
        right_ref,
    ) = refs
    _, rows, cols, width = own_ref.shape
    hidden = w_out_ref.shape[0]
    row = lax.axis_index("row")
    sub = lax.axis_index("sub")
    gain, bias = norm_gain_ref[...], norm_bias_ref[...]

    def normed(values):
        flat = values.reshape(-1, width).astype(jnp.float32)
        return layer_norm(flat, gain, bias, -1).astype(jnp.bfloat16)

    left_ref[pl.ds(sub, 1)] = own_ref[0:1]
    left_ref[pl.ds(1 - sub, 1)] = own_ref[1:2]
    for step in range(span):
        up_ref, down_ref = sent_refs[step::span]
        place = lax.rem((1 - step) % span + span - lax.rem(row, span), span)
        source = sub * span + place
        first = jnp.where(source == row, sub, jnp.where(row // span == sub, 0, 1))
        pair = jnp.where(source == row, own_ref[...], up_ref[...] + down_ref[...])
        right_ref[pl.ds(place * 2 + first, 1)] = pair[0:1]
        right_ref[pl.ds(place * 2 + 1 - first, 1)] = pair[1:2]

    right = gated(normed(right_ref[...]), w_b_proj_ref[...], w_b_gate_ref[...])
    right = right.reshape(span, 2, rows, cols, hidden)
    left = gated(normed(left_ref[...]), w_a_proj_ref[...], w_a_gate_ref[...])
    left = left.reshape(2, rows, cols, hidden)
    own_in = normed(own_ref[0])
    gating = jax.nn.sigmoid(jnp.dot(own_in, w_gate_ref[...], preferred_element_type=jnp.float32))
    gating = gating.astype(jnp.bfloat16).astype(jnp.float32)

    sums = []
    for i in range(rows):
        products = right[:, 0] * left[0, i] + right[:, 1] * left[1, i]
        sums.append(jnp.sum(products, axis=2).reshape(span * rows, hidden))
    triangle = jnp.concatenate(sums, axis=0).astype(jnp.bfloat16).astype(jnp.float32)
    hidden_normed = layer_norm(triangle, out_gain_ref[...], out_bias_ref[...], -1)
    mixed = jnp.dot(
        hidden_normed.astype(jnp.bfloat16), w_out_ref[...], preferred_element_type=jnp.float32
    )
    update_ref[...] = (gating * mixed).astype(jnp.bfloat16).reshape(update_ref.shape)


def send_one_way(
    n_row,
    pair_rep,
    norm_gain,
    norm_bias,
    w_a_proj,
    w_a_gate,
    w_b_proj,
    w_b_gate,
    w_gate,
    out_gain,
    out_bias,
    w_out,
):
    span = n_row // 2
    axes = ("row", "sub")
    swaps = [(2 * row + sub, 2 * row + 1 - sub) for row in range(n_row) for sub in range(2)]
    pair = jnp.stack([pair_rep, lax.ppermute(pair_rep, axes, swaps)])

    def routes(step, down):
        found = []
        for row in range(n_row):
            for sub in range(2):
                source = sub * span + (step - row) % span
                if source != row and (source > row) == down:
                    sender = 0 if row // span == sub else 1
                    found.append((2 * source + sender, 2 * row + sub))
        return found

    sent = [
        lax.ppermute(pair, axes, routes((1 - step) % span, down))
        for down in (False, True)
        for step in range(span)
    ]
    return pl.pallas_call(
        functools.partial(triangle_kernel, span),
        out_shape=jax.ShapeDtypeStruct(pair_rep.shape, pair_rep.dtype),
        scratch_shapes=[
            pltpu.VMEM((2,) + pair_rep.shape, pair_rep.dtype),
            pltpu.VMEM((n_row,) + pair_rep.shape, pair_rep.dtype),
        ],
    )(
        pair,
        *sent,
        norm_gain[None],
        norm_bias[None],
        w_a_proj,
        w_a_gate,
        w_b_proj,
        w_b_gate,
        w_gate,
        out_gain[None],
        out_bias[None],
        w_out,
    )


def exchange_channels(
    pair_rep,
    norm_gain,
    norm_bias,
    w_a_proj,
    w_a_gate,
    w_b_proj,
    w_b_gate,
    w_gate,
    out_gain,
    out_bias,
    w_out,
):
    hidden = w_a_proj.shape[1]
    w_inner = jnp.concatenate([w_a_proj, w_a_gate, w_b_proj, w_b_gate], axis=1)
    normed = layer_norm(pair_rep.astype(jnp.float32), norm_gain, norm_bias, -1).astype(jnp.bfloat16)
    inner = jnp.einsum("rkc,cm->mrk", normed, w_inner, preferred_element_type=jnp.float32)
    left_local = (jax.nn.sigmoid(inner[hidden : 2 * hidden]) * inner[:hidden]).astype(jnp.bfloat16)
    right_local = (
        jax.nn.sigmoid(inner[3 * hidden : 4 * hidden]) * inner[2 * hidden : 3 * hidden]
    ).astype(jnp.bfloat16)
    gating = jax.nn.sigmoid(
        jnp.einsum("rkc,cd->rkd", normed, w_gate, preferred_element_type=jnp.float32)
    ).astype(jnp.bfloat16)
    left_chan, right_chan = (
        lax.all_to_all(left_local, "row", split_axis=0, concat_axis=1, tiled=True),
        lax.all_to_all(right_local, "row", split_axis=0, concat_axis=1, tiled=True),
    )
    left_rows = lax.all_to_all(left_chan, "sub", split_axis=1, concat_axis=2, tiled=True)
    triangle = jnp.einsum(
        "hik,hjk->hij",
        left_rows,
        lax.all_gather(right_chan, "sub", axis=2, tiled=True),
        preferred_element_type=jnp.float32,
    ).astype(jnp.bfloat16)
    regrouped = lax.all_to_all(
        lax.all_to_all(triangle, "sub", split_axis=2, concat_axis=1, tiled=True),
        "row",
        split_axis=1,
        concat_axis=0,
        tiled=True,
    )
    hidden_normed = layer_norm(
        regrouped.astype(jnp.float32), out_gain[:, None, None], out_bias[:, None, None], 0
    ).astype(jnp.bfloat16)
    mixed = jnp.einsum("hrj,hc->rjc", hidden_normed, w_out, preferred_element_type=jnp.float32)
    return (gating.astype(jnp.float32) * mixed).astype(jnp.bfloat16)


def solution(mesh):
    n_row, n_sub = mesh.shape["row"], mesh.shape["sub"]

    def per_device(pair_rep, *weights):
        gathered = n_row * n_sub * pair_rep.size * pair_rep.dtype.itemsize
        if n_sub == 2 and n_row % 2 == 0 and gathered <= GATHER_BYTES:
            return send_one_way(n_row, pair_rep, *weights)
        return exchange_channels(pair_rep, *weights)

    in_specs = (P(("grp", "row"), "sub", None), P(), P(), P(), P(), P(), P(), P(), P(), P(), P())
    out_specs = P(("grp", "row"), "sub", None)
    return jax.shard_map(
        per_device, mesh=mesh, in_specs=in_specs, out_specs=out_specs, check_vma=False
    )
```

```python
import functools

import jax
import jax.numpy as jnp
from jax import lax
from jax.experimental import pallas as pl
from jax.experimental.pallas import tpu as pltpu
from jax.sharding import PartitionSpec as P

EPSILON = 1e-05
GATHER_BYTES = 2 * 1024 * 1024


def layer_norm(values, gain, shift, axis):
    centred = values - jnp.mean(values, axis=axis, keepdims=True)
    variance = jnp.mean(centred * centred, axis=axis, keepdims=True)
    return centred * lax.rsqrt(variance + EPSILON) * gain + shift


def gated(rows, w_proj, w_gate):
    proj = jnp.dot(rows, w_proj, preferred_element_type=jnp.float32)
    gate = jnp.dot(rows, w_gate, preferred_element_type=jnp.float32)
    return (jax.nn.sigmoid(gate) * proj).astype(jnp.bfloat16).astype(jnp.float32)


def triangle_kernel(span, *refs):
    (
        own_ref,
        other_ref,
        norm_gain_ref,
        norm_bias_ref,
        w_a_proj_ref,
        w_a_gate_ref,
        w_b_proj_ref,
        w_b_gate_ref,
        w_gate_ref,
        out_gain_ref,
        out_bias_ref,
        w_out_ref,
        update_ref,
        left_ref,
        right_ref,
    ) = refs
    _, rows, cols, width = own_ref.shape
    hidden = w_out_ref.shape[0]
    row = lax.axis_index("row")
    sub = lax.axis_index("sub")
    gain, bias = norm_gain_ref[...], norm_bias_ref[...]

    def normed(values):
        flat = values.reshape(-1, width).astype(jnp.float32)
        return layer_norm(flat, gain, bias, -1).astype(jnp.bfloat16)

    for step, ref in enumerate((own_ref, other_ref)):
        half = sub ^ step
        left_ref[pl.ds(half, 1)] = ref[pl.ds(row, 1)]
        right_ref[:, pl.ds(half, 1)] = ref[pl.ds(sub * span, span)][:, None]

    right = gated(normed(right_ref[...]), w_b_proj_ref[...], w_b_gate_ref[...])
    right = right.reshape(span, 2, rows, cols, hidden)
    left = gated(normed(left_ref[...]), w_a_proj_ref[...], w_a_gate_ref[...])
    left = left.reshape(2, rows, cols, hidden)
    own_in = normed(own_ref[row])
    gating = jax.nn.sigmoid(jnp.dot(own_in, w_gate_ref[...], preferred_element_type=jnp.float32))
    gating = gating.astype(jnp.bfloat16).astype(jnp.float32)

    sums = []
    for i in range(rows):
        products = right[:, 0] * left[0, i] + right[:, 1] * left[1, i]
        sums.append(jnp.sum(products, axis=2).reshape(span * rows, hidden))
    triangle = jnp.concatenate(sums, axis=0).astype(jnp.bfloat16).astype(jnp.float32)
    hidden_normed = layer_norm(triangle, out_gain_ref[...], out_bias_ref[...], -1)
    mixed = jnp.dot(
        hidden_normed.astype(jnp.bfloat16), w_out_ref[...], preferred_element_type=jnp.float32
    )
    update_ref[...] = (gating * mixed).astype(jnp.bfloat16).reshape(update_ref.shape)


def gather_rows(
    n_row,
    pair_rep,
    norm_gain,
    norm_bias,
    w_a_proj,
    w_a_gate,
    w_b_proj,
    w_b_gate,
    w_gate,
    out_gain,
    out_bias,
    w_out,
):
    span = n_row // 2
    own = lax.all_gather(pair_rep, "row")
    other = lax.ppermute(own, "sub", [(0, 1), (1, 0)])
    return pl.pallas_call(
        functools.partial(triangle_kernel, span),
        out_shape=jax.ShapeDtypeStruct(pair_rep.shape, pair_rep.dtype),
        scratch_shapes=[
            pltpu.VMEM((2,) + pair_rep.shape, pair_rep.dtype),
            pltpu.VMEM((span, 2) + pair_rep.shape, pair_rep.dtype),
        ],
    )(
        own,
        other,
        norm_gain[None],
        norm_bias[None],
        w_a_proj,
        w_a_gate,
        w_b_proj,
        w_b_gate,
        w_gate,
        out_gain[None],
        out_bias[None],
        w_out,
    )


def exchange_channels(
    pair_rep,
    norm_gain,
    norm_bias,
    w_a_proj,
    w_a_gate,
    w_b_proj,
    w_b_gate,
    w_gate,
    out_gain,
    out_bias,
    w_out,
):
    hidden = w_a_proj.shape[1]
    w_inner = jnp.concatenate([w_a_proj, w_a_gate, w_b_proj, w_b_gate], axis=1)
    normed = layer_norm(pair_rep.astype(jnp.float32), norm_gain, norm_bias, -1).astype(jnp.bfloat16)
    inner = jnp.einsum("rkc,cm->mrk", normed, w_inner, preferred_element_type=jnp.float32)
    left_local = (jax.nn.sigmoid(inner[hidden : 2 * hidden]) * inner[:hidden]).astype(jnp.bfloat16)
    right_local = (
        jax.nn.sigmoid(inner[3 * hidden : 4 * hidden]) * inner[2 * hidden : 3 * hidden]
    ).astype(jnp.bfloat16)
    gating = jax.nn.sigmoid(
        jnp.einsum("rkc,cd->rkd", normed, w_gate, preferred_element_type=jnp.float32)
    ).astype(jnp.bfloat16)
    left_chan, right_chan = (
        lax.all_to_all(left_local, "row", split_axis=0, concat_axis=1, tiled=True),
        lax.all_to_all(right_local, "row", split_axis=0, concat_axis=1, tiled=True),
    )
    left_rows = lax.all_to_all(left_chan, "sub", split_axis=1, concat_axis=2, tiled=True)
    triangle = jnp.einsum(
        "hik,hjk->hij",
        left_rows,
        lax.all_gather(right_chan, "sub", axis=2, tiled=True),
        preferred_element_type=jnp.float32,
    ).astype(jnp.bfloat16)
    regrouped = lax.all_to_all(
        lax.all_to_all(triangle, "sub", split_axis=2, concat_axis=1, tiled=True),
        "row",
        split_axis=1,
        concat_axis=0,
        tiled=True,
    )
    hidden_normed = layer_norm(
        regrouped.astype(jnp.float32), out_gain[:, None, None], out_bias[:, None, None], 0
    ).astype(jnp.bfloat16)
    mixed = jnp.einsum("hrj,hc->rjc", hidden_normed, w_out, preferred_element_type=jnp.float32)
    return (gating.astype(jnp.float32) * mixed).astype(jnp.bfloat16)


def solution(mesh):
    n_row, n_sub = mesh.shape["row"], mesh.shape["sub"]

    def per_device(pair_rep, *weights):
        gathered = n_row * n_sub * pair_rep.size * pair_rep.dtype.itemsize
        if n_sub == 2 and n_row % 2 == 0 and gathered <= GATHER_BYTES:
            return gather_rows(n_row, pair_rep, *weights)
        return exchange_channels(pair_rep, *weights)

    in_specs = (P(("grp", "row"), "sub", None), P(), P(), P(), P(), P(), P(), P(), P(), P(), P())
    out_specs = P(("grp", "row"), "sub", None)
    return jax.shard_map(
        per_device, mesh=mesh, in_specs=in_specs, out_specs=out_specs, check_vma=False
    )
```

```python
import functools

import jax
import jax.numpy as jnp
from jax import lax
from jax.experimental import pallas as pl
from jax.experimental.pallas import tpu as pltpu
from jax.sharding import PartitionSpec as P

EPSILON = 1e-05
GATHER_BYTES = 2 * 1024 * 1024


def layer_norm(values, gain, shift, axis):
    centred = values - jnp.mean(values, axis=axis, keepdims=True)
    variance = jnp.mean(centred * centred, axis=axis, keepdims=True)
    return centred * lax.rsqrt(variance + EPSILON) * gain + shift


def gated(rows, w_proj, w_gate):
    proj = jnp.dot(rows, w_proj, preferred_element_type=jnp.float32)
    gate = jnp.dot(rows, w_gate, preferred_element_type=jnp.float32)
    return (jax.nn.sigmoid(gate) * proj).astype(jnp.bfloat16).astype(jnp.float32)


def copy_kernel(source_ref, target_ref):
    target_ref[...] = source_ref[...]


def flat_normed(values, gain, bias):
    flat = values.reshape(-1, values.shape[-1]).astype(jnp.float32)
    return layer_norm(flat, gain, bias, -1).astype(jnp.bfloat16)


def first_kernel(
    span,
    pair_ref,
    first_ref,
    second_ref,
    norm_gain_ref,
    norm_bias_ref,
    w_a_proj_ref,
    w_a_gate_ref,
    w_b_proj_ref,
    w_b_gate_ref,
    w_gate_ref,
    left_ref,
    right_ref,
    gating_ref,
):
    gain, bias = norm_gain_ref[...], norm_bias_ref[...]
    crossed = jnp.where(lax.axis_index("row") // span == lax.axis_index("sub"), 0, 1)
    for half, place in ((0, crossed), (1, 1 - crossed)):
        rows = flat_normed(pair_ref[place], gain, bias)
        left = gated(rows, w_a_proj_ref[...], w_a_gate_ref[...])
        left_ref[half] = left.astype(jnp.bfloat16).reshape(left_ref.shape[1:])
    rows = flat_normed(pair_ref[0], gain, bias)
    gating = jax.nn.sigmoid(jnp.dot(rows, w_gate_ref[...], preferred_element_type=jnp.float32))
    gating_ref[...] = gating.astype(jnp.bfloat16).reshape(gating_ref.shape)
    for place, ref in enumerate((first_ref, second_ref)):
        rows = flat_normed(ref[...], gain, bias)
        right = gated(rows, w_b_proj_ref[...], w_b_gate_ref[...])
        right_ref[place] = right.astype(jnp.bfloat16).reshape(right_ref.shape[1:])


def last_kernel(
    span,
    last_ref,
    left_ref,
    right_ref,
    gating_ref,
    norm_gain_ref,
    norm_bias_ref,
    w_b_proj_ref,
    w_b_gate_ref,
    out_gain_ref,
    out_bias_ref,
    w_out_ref,
    update_ref,
    placed_ref,
):
    _, _, rows, cols, width = last_ref.shape
    hidden = w_out_ref.shape[0]
    last = flat_normed(last_ref[...], norm_gain_ref[...], norm_bias_ref[...])
    last = gated(last, w_b_proj_ref[...], w_b_gate_ref[...]).reshape(2, 2, rows, cols, hidden)
    base = lax.rem(lax.axis_index("row"), span)
    for step in range(2):
        placed_ref[pl.ds(base ^ (2 * step), 1)] = right_ref[step : step + 1].astype(jnp.float32)
        placed_ref[pl.ds(base ^ (2 * step + 1), 1)] = last[step : step + 1]
    right = placed_ref[...]
    left = left_ref[...].astype(jnp.float32)
    sums = []
    for i in range(rows):
        products = right[:, 0] * left[0, i] + right[:, 1] * left[1, i]
        sums.append(jnp.sum(products, axis=2).reshape(span * rows, hidden))
    triangle = jnp.concatenate(sums, axis=0).astype(jnp.bfloat16).astype(jnp.float32)
    hidden_normed = layer_norm(triangle, out_gain_ref[...], out_bias_ref[...], -1)
    mixed = jnp.dot(
        hidden_normed.astype(jnp.bfloat16), w_out_ref[...], preferred_element_type=jnp.float32
    )
    gating = gating_ref[...].reshape(mixed.shape).astype(jnp.float32)
    update_ref[...] = (gating * mixed).astype(jnp.bfloat16).reshape(update_ref.shape)


def swap_rows(
    n_row,
    pair_rep,
    norm_gain,
    norm_bias,
    w_a_proj,
    w_a_gate,
    w_b_proj,
    w_b_gate,
    w_gate,
    out_gain,
    out_bias,
    w_out,
):
    span = n_row // 2
    block = pair_rep.shape
    like = lambda *lead: jax.ShapeDtypeStruct(lead + block, pair_rep.dtype)
    cost = pl.CostEstimate(flops=10**8, bytes_accessed=10**6, transcendentals=0)

    def swap(values, partner):
        devices = [(row, sub) for row in range(n_row) for sub in range(2)]
        partners = [partner(row, sub) for row, sub in devices]
        pairs = [(2 * a + b, 2 * c + d) for (a, b), (c, d) in zip(devices, partners)]
        return lax.ppermute(values, ("row", "sub"), pairs)

    def across(row, sub):
        return (row, sub) if row // span == sub else (row ^ span, 1 - sub)

    other = swap(pair_rep, lambda row, sub: (row, 1 - sub))
    own = pl.pallas_call(copy_kernel, out_shape=like(), cost_estimate=cost)(pair_rep)
    pair = jnp.stack([own, other])
    first = swap(pair, across)
    second = swap(first, lambda row, sub: (row ^ 2, sub))
    last = swap(jnp.stack([first, second]), lambda row, sub: (row ^ 1, sub))
    left, right, gating = pl.pallas_call(
        functools.partial(first_kernel, span),
        out_shape=(like(2), like(2, 2), like()),
        cost_estimate=cost,
    )(
        pair,
        first,
        second,
        norm_gain[None],
        norm_bias[None],
        w_a_proj,
        w_a_gate,
        w_b_proj,
        w_b_gate,
        w_gate,
    )
    return pl.pallas_call(
        functools.partial(last_kernel, span),
        out_shape=like(),
        scratch_shapes=[pltpu.VMEM((span, 2) + block, jnp.float32)],
    )(
        last,
        left,
        right,
        gating,
        norm_gain[None],
        norm_bias[None],
        w_b_proj,
        w_b_gate,
        out_gain[None],
        out_bias[None],
        w_out,
    )


def exchange_channels(
    pair_rep,
    norm_gain,
    norm_bias,
    w_a_proj,
    w_a_gate,
    w_b_proj,
    w_b_gate,
    w_gate,
    out_gain,
    out_bias,
    w_out,
):
    hidden = w_a_proj.shape[1]
    w_inner = jnp.concatenate([w_a_proj, w_a_gate, w_b_proj, w_b_gate], axis=1)
    normed = layer_norm(pair_rep.astype(jnp.float32), norm_gain, norm_bias, -1).astype(jnp.bfloat16)
    inner = jnp.einsum("rkc,cm->mrk", normed, w_inner, preferred_element_type=jnp.float32)
    left_local = (jax.nn.sigmoid(inner[hidden : 2 * hidden]) * inner[:hidden]).astype(jnp.bfloat16)
    right_local = (
        jax.nn.sigmoid(inner[3 * hidden : 4 * hidden]) * inner[2 * hidden : 3 * hidden]
    ).astype(jnp.bfloat16)
    gating = jax.nn.sigmoid(
        jnp.einsum("rkc,cd->rkd", normed, w_gate, preferred_element_type=jnp.float32)
    ).astype(jnp.bfloat16)
    left_chan, right_chan = (
        lax.all_to_all(left_local, "row", split_axis=0, concat_axis=1, tiled=True),
        lax.all_to_all(right_local, "row", split_axis=0, concat_axis=1, tiled=True),
    )
    left_rows = lax.all_to_all(left_chan, "sub", split_axis=1, concat_axis=2, tiled=True)
    triangle = jnp.einsum(
        "hik,hjk->hij",
        left_rows,
        lax.all_gather(right_chan, "sub", axis=2, tiled=True),
        preferred_element_type=jnp.float32,
    ).astype(jnp.bfloat16)
    regrouped = lax.all_to_all(
        lax.all_to_all(triangle, "sub", split_axis=2, concat_axis=1, tiled=True),
        "row",
        split_axis=1,
        concat_axis=0,
        tiled=True,
    )
    hidden_normed = layer_norm(
        regrouped.astype(jnp.float32), out_gain[:, None, None], out_bias[:, None, None], 0
    ).astype(jnp.bfloat16)
    mixed = jnp.einsum("hrj,hc->rjc", hidden_normed, w_out, preferred_element_type=jnp.float32)
    return (gating.astype(jnp.float32) * mixed).astype(jnp.bfloat16)


def solution(mesh):
    n_row, n_sub = mesh.shape["row"], mesh.shape["sub"]

    def per_device(pair_rep, *weights):
        gathered = n_row * n_sub * pair_rep.size * pair_rep.dtype.itemsize
        if n_sub == 2 and n_row == 8 and gathered <= GATHER_BYTES:
            return swap_rows(n_row, pair_rep, *weights)
        return exchange_channels(pair_rep, *weights)

    in_specs = (P(("grp", "row"), "sub", None), P(), P(), P(), P(), P(), P(), P(), P(), P(), P())
    out_specs = P(("grp", "row"), "sub", None)
    return jax.shard_map(
        per_device, mesh=mesh, in_specs=in_specs, out_specs=out_specs, check_vma=False
    )
```

```python
import functools

import jax
import jax.numpy as jnp
from jax import lax
from jax.experimental import pallas as pl
from jax.experimental.pallas import tpu as pltpu
from jax.sharding import PartitionSpec as P

EPSILON = 1e-05
GATHER_BYTES = 2 * 1024 * 1024
KERNEL_BYTES = 4 * 1024 * 1024


def layer_norm(values, gain, shift, axis):
    centred = values - jnp.mean(values, axis=axis, keepdims=True)
    variance = jnp.mean(centred * centred, axis=axis, keepdims=True)
    return centred * lax.rsqrt(variance + EPSILON) * gain + shift


def gated(rows, w_proj, w_gate):
    proj = jnp.dot(rows, w_proj, preferred_element_type=jnp.float32)
    gate = jnp.dot(rows, w_gate, preferred_element_type=jnp.float32)
    return (jax.nn.sigmoid(gate) * proj).astype(jnp.bfloat16).astype(jnp.float32)


def copy_kernel(source_ref, target_ref):
    target_ref[...] = source_ref[...]


def flat_normed(values, gain, bias):
    flat = values.reshape(-1, values.shape[-1]).astype(jnp.float32)
    return layer_norm(flat, gain, bias, -1).astype(jnp.bfloat16)


def first_kernel(
    span,
    pair_ref,
    first_ref,
    second_ref,
    norm_gain_ref,
    norm_bias_ref,
    w_a_proj_ref,
    w_a_gate_ref,
    w_b_proj_ref,
    w_b_gate_ref,
    w_gate_ref,
    left_ref,
    right_ref,
    gating_ref,
):
    gain, bias = norm_gain_ref[...], norm_bias_ref[...]
    crossed = jnp.where(lax.axis_index("row") // span == lax.axis_index("sub"), 0, 1)
    for half, place in ((0, crossed), (1, 1 - crossed)):
        rows = flat_normed(pair_ref[place], gain, bias)
        left = gated(rows, w_a_proj_ref[...], w_a_gate_ref[...])
        left_ref[half] = left.astype(jnp.bfloat16).reshape(left_ref.shape[1:])
    rows = flat_normed(pair_ref[0], gain, bias)
    gating = jax.nn.sigmoid(jnp.dot(rows, w_gate_ref[...], preferred_element_type=jnp.float32))
    gating_ref[...] = gating.astype(jnp.bfloat16).reshape(gating_ref.shape)
    for place, ref in enumerate((first_ref, second_ref)):
        rows = flat_normed(ref[...], gain, bias)
        right = gated(rows, w_b_proj_ref[...], w_b_gate_ref[...])
        right_ref[place] = right.astype(jnp.bfloat16).reshape(right_ref.shape[1:])


def last_kernel(
    span,
    last_ref,
    left_ref,
    right_ref,
    gating_ref,
    norm_gain_ref,
    norm_bias_ref,
    w_b_proj_ref,
    w_b_gate_ref,
    out_gain_ref,
    out_bias_ref,
    w_out_ref,
    update_ref,
    placed_ref,
):
    _, _, rows, cols, width = last_ref.shape
    hidden = w_out_ref.shape[0]
    last = flat_normed(last_ref[...], norm_gain_ref[...], norm_bias_ref[...])
    last = gated(last, w_b_proj_ref[...], w_b_gate_ref[...]).reshape(2, 2, rows, cols, hidden)
    base = lax.rem(lax.axis_index("row"), span)
    for step in range(2):
        placed_ref[pl.ds(base ^ (2 * step), 1)] = right_ref[step : step + 1].astype(jnp.float32)
        placed_ref[pl.ds(base ^ (2 * step + 1), 1)] = last[step : step + 1]
    right = placed_ref[...]
    left = left_ref[...].astype(jnp.float32)
    sums = []
    for i in range(rows):
        products = right[:, 0] * left[0, i] + right[:, 1] * left[1, i]
        sums.append(jnp.sum(products, axis=2).reshape(span * rows, hidden))
    triangle = jnp.concatenate(sums, axis=0).astype(jnp.bfloat16).astype(jnp.float32)
    hidden_normed = layer_norm(triangle, out_gain_ref[...], out_bias_ref[...], -1)
    mixed = jnp.dot(
        hidden_normed.astype(jnp.bfloat16), w_out_ref[...], preferred_element_type=jnp.float32
    )
    gating = gating_ref[...].reshape(mixed.shape).astype(jnp.float32)
    update_ref[...] = (gating * mixed).astype(jnp.bfloat16).reshape(update_ref.shape)


def swap_rows(
    n_row,
    pair_rep,
    norm_gain,
    norm_bias,
    w_a_proj,
    w_a_gate,
    w_b_proj,
    w_b_gate,
    w_gate,
    out_gain,
    out_bias,
    w_out,
):
    span = n_row // 2
    block = pair_rep.shape
    like = lambda *lead: jax.ShapeDtypeStruct(lead + block, pair_rep.dtype)
    params = pltpu.CompilerParams(vmem_limit_bytes=KERNEL_BYTES)
    cost = pl.CostEstimate(flops=10**8, bytes_accessed=10**6, transcendentals=0)

    def swap(values, partner):
        devices = [(row, sub) for row in range(n_row) for sub in range(2)]
        partners = [partner(row, sub) for row, sub in devices]
        pairs = [(2 * a + b, 2 * c + d) for (a, b), (c, d) in zip(devices, partners)]
        return lax.ppermute(values, ("row", "sub"), pairs)

    other = swap(pair_rep, lambda row, sub: (row, 1 - sub))
    own = pl.pallas_call(copy_kernel, out_shape=like(), cost_estimate=cost, compiler_params=params)(pair_rep)
    pair = jnp.stack([own, other])
    across = swap(pair, lambda row, sub: (row ^ span, 1 - sub))
    crossed = lax.axis_index("row") // span != lax.axis_index("sub")
    first = jnp.where(crossed, across, pair)
    second = swap(first, lambda row, sub: (row ^ 2, sub))
    last = swap(jnp.stack([first, second]), lambda row, sub: (row ^ 1, sub))
    left, right, gating = pl.pallas_call(
        functools.partial(first_kernel, span),
        out_shape=(like(2), like(2, 2), like()),
        cost_estimate=cost,
        compiler_params=params,
    )(
        pair,
        first,
        second,
        norm_gain[None],
        norm_bias[None],
        w_a_proj,
        w_a_gate,
        w_b_proj,
        w_b_gate,
        w_gate,
    )
    return pl.pallas_call(
        functools.partial(last_kernel, span),
        out_shape=like(),
        scratch_shapes=[pltpu.VMEM((span, 2) + block, jnp.float32)],
        compiler_params=params,
    )(
        last,
        left,
        right,
        gating,
        norm_gain[None],
        norm_bias[None],
        w_b_proj,
        w_b_gate,
        out_gain[None],
        out_bias[None],
        w_out,
    )


def exchange_channels(
    pair_rep,
    norm_gain,
    norm_bias,
    w_a_proj,
    w_a_gate,
    w_b_proj,
    w_b_gate,
    w_gate,
    out_gain,
    out_bias,
    w_out,
):
    hidden = w_a_proj.shape[1]
    w_inner = jnp.concatenate([w_a_proj, w_a_gate, w_b_proj, w_b_gate], axis=1)
    normed = layer_norm(pair_rep.astype(jnp.float32), norm_gain, norm_bias, -1).astype(jnp.bfloat16)
    inner = jnp.einsum("rkc,cm->mrk", normed, w_inner, preferred_element_type=jnp.float32)
    left_local = (jax.nn.sigmoid(inner[hidden : 2 * hidden]) * inner[:hidden]).astype(jnp.bfloat16)
    right_local = (
        jax.nn.sigmoid(inner[3 * hidden : 4 * hidden]) * inner[2 * hidden : 3 * hidden]
    ).astype(jnp.bfloat16)
    gating = jax.nn.sigmoid(
        jnp.einsum("rkc,cd->rkd", normed, w_gate, preferred_element_type=jnp.float32)
    ).astype(jnp.bfloat16)
    left_chan, right_chan = (
        lax.all_to_all(left_local, "row", split_axis=0, concat_axis=1, tiled=True),
        lax.all_to_all(right_local, "row", split_axis=0, concat_axis=1, tiled=True),
    )
    left_rows = lax.all_to_all(left_chan, "sub", split_axis=1, concat_axis=2, tiled=True)
    triangle = jnp.einsum(
        "hik,hjk->hij",
        left_rows,
        lax.all_gather(right_chan, "sub", axis=2, tiled=True),
        preferred_element_type=jnp.float32,
    ).astype(jnp.bfloat16)
    regrouped = lax.all_to_all(
        lax.all_to_all(triangle, "sub", split_axis=2, concat_axis=1, tiled=True),
        "row",
        split_axis=1,
        concat_axis=0,
        tiled=True,
    )
    hidden_normed = layer_norm(
        regrouped.astype(jnp.float32), out_gain[:, None, None], out_bias[:, None, None], 0
    ).astype(jnp.bfloat16)
    mixed = jnp.einsum("hrj,hc->rjc", hidden_normed, w_out, preferred_element_type=jnp.float32)
    return (gating.astype(jnp.float32) * mixed).astype(jnp.bfloat16)


def solution(mesh):
    n_row, n_sub = mesh.shape["row"], mesh.shape["sub"]

    def per_device(pair_rep, *weights):
        gathered = n_row * n_sub * pair_rep.size * pair_rep.dtype.itemsize
        if n_sub == 2 and n_row == 8 and gathered <= GATHER_BYTES:
            return swap_rows(n_row, pair_rep, *weights)
        return exchange_channels(pair_rep, *weights)

    in_specs = (P(("grp", "row"), "sub", None), P(), P(), P(), P(), P(), P(), P(), P(), P(), P())
    out_specs = P(("grp", "row"), "sub", None)
    return jax.shard_map(
        per_device, mesh=mesh, in_specs=in_specs, out_specs=out_specs, check_vma=False
    )
```

```python
import functools

import jax
import jax.numpy as jnp
from jax import lax
from jax.experimental import pallas as pl
from jax.experimental.pallas import tpu as pltpu
from jax.sharding import PartitionSpec as P

EPSILON = 1e-05
GATHER_BYTES = 2 * 1024 * 1024
KERNEL_BYTES = 4 * 1024 * 1024


def layer_norm(values, gain, shift, axis):
    centred = values - jnp.mean(values, axis=axis, keepdims=True)
    variance = jnp.mean(centred * centred, axis=axis, keepdims=True)
    return centred * lax.rsqrt(variance + EPSILON) * gain + shift


def gated(rows, w_proj, w_gate):
    proj = jnp.dot(rows, w_proj, preferred_element_type=jnp.float32)
    gate = jnp.dot(rows, w_gate, preferred_element_type=jnp.float32)
    return (jax.nn.sigmoid(gate) * proj).astype(jnp.bfloat16).astype(jnp.float32)


def copy_kernel(source_ref, target_ref):
    target_ref[...] = source_ref[...]


def flat_normed(values, gain, bias):
    flat = values.reshape(-1, values.shape[-1]).astype(jnp.float32)
    return layer_norm(flat, gain, bias, -1).astype(jnp.bfloat16)


def finish(left, right, gating, out_gain_ref, out_bias_ref, w_out_ref):
    sums = []
    for block in range(right.shape[0]):
        for row in range(left.shape[1]):
            products = right[block, 0] * left[0, row] + right[block, 1] * left[1, row]
            sums.append(jnp.sum(products, axis=1))
    triangle = jnp.concatenate(sums, axis=0).astype(jnp.bfloat16).astype(jnp.float32)
    hidden_normed = layer_norm(triangle, out_gain_ref[...], out_bias_ref[...], -1)
    mixed = jnp.dot(
        hidden_normed.astype(jnp.bfloat16), w_out_ref[...], preferred_element_type=jnp.float32
    )
    return gating * mixed.reshape(gating.shape)


def first_kernel(
    span,
    own_ref,
    swapped_ref,
    first_ref,
    second_ref,
    norm_gain_ref,
    norm_bias_ref,
    w_a_proj_ref,
    w_a_gate_ref,
    w_b_proj_ref,
    w_b_gate_ref,
    w_gate_ref,
    out_gain_ref,
    out_bias_ref,
    w_out_ref,
    left_ref,
    gating_ref,
    update_ref,
):
    rows, cols, width = own_ref.shape
    gain, bias = norm_gain_ref[...], norm_bias_ref[...]
    row = lax.axis_index("row")
    crossed = jnp.where(row // span == lax.axis_index("sub"), 0, 1)
    own = flat_normed(own_ref[...], gain, bias)
    other = flat_normed(swapped_ref[0], gain, bias)
    for values, place in ((own, crossed), (other, 1 - crossed)):
        left = gated(values, w_a_proj_ref[...], w_a_gate_ref[...])
        left_ref[pl.ds(place, 1)] = left.astype(jnp.bfloat16).reshape(1, rows, cols, -1)
    gating = jax.nn.sigmoid(jnp.dot(own, w_gate_ref[...], preferred_element_type=jnp.float32))
    gating = gating.astype(jnp.bfloat16).astype(jnp.float32).reshape(rows, cols, width)
    for place in range(span):
        part = gating[:, place * rows : (place + 1) * rows]
        gating_ref[place] = part.reshape(rows * rows, width)
    right = []
    for ref in (first_ref, second_ref):
        values = flat_normed(ref[...], gain, bias)
        right.append(gated(values, w_b_proj_ref[...], w_b_gate_ref[...]).reshape(2, rows, cols, -1))
    base = lax.rem(row, span)
    gating = jnp.stack([gating_ref[base], gating_ref[base ^ 2]])
    left = left_ref[...].astype(jnp.float32)
    update_ref[...] = finish(left, jnp.stack(right), gating, out_gain_ref, out_bias_ref, w_out_ref)


def last_kernel(
    span,
    last_ref,
    left_ref,
    gating_ref,
    first_ref,
    norm_gain_ref,
    norm_bias_ref,
    w_b_proj_ref,
    w_b_gate_ref,
    out_gain_ref,
    out_bias_ref,
    w_out_ref,
    update_ref,
    placed_ref,
):
    _, _, rows, cols, width = last_ref.shape
    base = lax.rem(lax.axis_index("row"), span)
    values = flat_normed(last_ref[...], norm_gain_ref[...], norm_bias_ref[...])
    right = gated(values, w_b_proj_ref[...], w_b_gate_ref[...]).reshape(2, 2, rows, cols, -1)
    gating = jnp.stack([gating_ref[base ^ 1], gating_ref[base ^ 3]])
    left = left_ref[...].astype(jnp.float32)
    last = finish(left, right, gating, out_gain_ref, out_bias_ref, w_out_ref)
    for step in range(2):
        placed_ref[pl.ds(base ^ (2 * step), 1)] = first_ref[step : step + 1]
        placed_ref[pl.ds(base ^ (2 * step + 1), 1)] = last[step : step + 1]
    for row in range(rows):
        parts = [placed_ref[place, row * rows : (row + 1) * rows] for place in range(span)]
        update_ref[row] = jnp.concatenate(parts, axis=0).astype(jnp.bfloat16)


def swap_rows(
    n_row,
    pair_rep,
    norm_gain,
    norm_bias,
    w_a_proj,
    w_a_gate,
    w_b_proj,
    w_b_gate,
    w_gate,
    out_gain,
    out_bias,
    w_out,
):
    span = n_row // 2
    block = pair_rep.shape
    rows, _, width = block
    params = pltpu.CompilerParams(vmem_limit_bytes=KERNEL_BYTES)
    cost = pl.CostEstimate(flops=10**8, bytes_accessed=10**6, transcendentals=0)

    def swap(values, partner):
        devices = [(row, sub) for row in range(n_row) for sub in range(2)]
        partners = [partner(row, sub) for row, sub in devices]
        pairs = [(2 * a + b, 2 * c + d) for (a, b), (c, d) in zip(devices, partners)]
        return lax.ppermute(values, ("row", "sub"), pairs)

    far = swap(pair_rep, lambda row, sub: (row ^ span, 1 - sub))
    own = pl.pallas_call(
        copy_kernel,
        out_shape=jax.ShapeDtypeStruct(block, pair_rep.dtype),
        cost_estimate=cost,
        compiler_params=params,
    )(pair_rep)
    swapped = swap(jnp.stack([own, far]), lambda row, sub: (row, 1 - sub))
    crossed = lax.axis_index("row") // span != lax.axis_index("sub")
    first = jnp.where(crossed, jnp.stack([far, swapped[1]]), jnp.stack([own, swapped[0]]))
    second = swap(first, lambda row, sub: (row ^ 2, sub))
    last = swap(jnp.stack([first, second]), lambda row, sub: (row ^ 1, sub))
    norm = (norm_gain[None], norm_bias[None])
    out = (out_gain[None], out_bias[None], w_out)
    left, gating, update = pl.pallas_call(
        functools.partial(first_kernel, span),
        out_shape=(
            jax.ShapeDtypeStruct((2,) + block, jnp.bfloat16),
            jax.ShapeDtypeStruct((span, rows * rows, width), jnp.float32),
            jax.ShapeDtypeStruct((2, rows * rows, width), jnp.float32),
        ),
        cost_estimate=cost,
        compiler_params=params,
    )(own, swapped, first, second, *norm, w_a_proj, w_a_gate, w_b_proj, w_b_gate, w_gate, *out)
    return pl.pallas_call(
        functools.partial(last_kernel, span),
        out_shape=jax.ShapeDtypeStruct(block, pair_rep.dtype),
        scratch_shapes=[pltpu.VMEM((span, rows * rows, width), jnp.float32)],
        compiler_params=params,
    )(last, left, gating, update, *norm, w_b_proj, w_b_gate, *out)


def exchange_channels(
    pair_rep,
    norm_gain,
    norm_bias,
    w_a_proj,
    w_a_gate,
    w_b_proj,
    w_b_gate,
    w_gate,
    out_gain,
    out_bias,
    w_out,
):
    hidden = w_a_proj.shape[1]
    w_inner = jnp.concatenate([w_a_proj, w_a_gate, w_b_proj, w_b_gate], axis=1)
    normed = layer_norm(pair_rep.astype(jnp.float32), norm_gain, norm_bias, -1).astype(jnp.bfloat16)
    inner = jnp.einsum("rkc,cm->mrk", normed, w_inner, preferred_element_type=jnp.float32)
    left_local = (jax.nn.sigmoid(inner[hidden : 2 * hidden]) * inner[:hidden]).astype(jnp.bfloat16)
    right_local = (
        jax.nn.sigmoid(inner[3 * hidden : 4 * hidden]) * inner[2 * hidden : 3 * hidden]
    ).astype(jnp.bfloat16)
    gating = jax.nn.sigmoid(
        jnp.einsum("rkc,cd->rkd", normed, w_gate, preferred_element_type=jnp.float32)
    ).astype(jnp.bfloat16)
    left_chan, right_chan = (
        lax.all_to_all(left_local, "row", split_axis=0, concat_axis=1, tiled=True),
        lax.all_to_all(right_local, "row", split_axis=0, concat_axis=1, tiled=True),
    )
    left_rows = lax.all_to_all(left_chan, "sub", split_axis=1, concat_axis=2, tiled=True)
    triangle = jnp.einsum(
        "hik,hjk->hij",
        left_rows,
        lax.all_gather(right_chan, "sub", axis=2, tiled=True),
        preferred_element_type=jnp.float32,
    ).astype(jnp.bfloat16)
    regrouped = lax.all_to_all(
        lax.all_to_all(triangle, "sub", split_axis=2, concat_axis=1, tiled=True),
        "row",
        split_axis=1,
        concat_axis=0,
        tiled=True,
    )
    hidden_normed = layer_norm(
        regrouped.astype(jnp.float32), out_gain[:, None, None], out_bias[:, None, None], 0
    ).astype(jnp.bfloat16)
    mixed = jnp.einsum("hrj,hc->rjc", hidden_normed, w_out, preferred_element_type=jnp.float32)
    return (gating.astype(jnp.float32) * mixed).astype(jnp.bfloat16)


def solution(mesh):
    n_row, n_sub = mesh.shape["row"], mesh.shape["sub"]

    def per_device(pair_rep, *weights):
        rows, cols, _ = pair_rep.shape
        gathered = n_row * n_sub * pair_rep.size * pair_rep.dtype.itemsize
        if n_sub == 2 and n_row == 8 and cols == n_row // 2 * rows and gathered <= GATHER_BYTES:
            return swap_rows(n_row, pair_rep, *weights)
        return exchange_channels(pair_rep, *weights)

    in_specs = (P(("grp", "row"), "sub", None), P(), P(), P(), P(), P(), P(), P(), P(), P(), P())
    out_specs = P(("grp", "row"), "sub", None)
    return jax.shard_map(
        per_device, mesh=mesh, in_specs=in_specs, out_specs=out_specs, check_vma=False
    )
```

```python
import functools

import jax
import jax.numpy as jnp
from jax import lax
from jax.experimental import pallas as pl
from jax.experimental.pallas import tpu as pltpu
from jax.sharding import PartitionSpec as P

EPSILON = 1e-05
GATHER_BYTES = 2 * 1024 * 1024
KERNEL_BYTES = 4 * 1024 * 1024
STEPS = (1, 2, 3)


def layer_norm(values, gain, shift, axis):
    centred = values - jnp.mean(values, axis=axis, keepdims=True)
    variance = jnp.mean(centred * centred, axis=axis, keepdims=True)
    return centred * lax.rsqrt(variance + EPSILON) * gain + shift


def gated(rows, w_proj, w_gate):
    proj = jnp.dot(rows, w_proj, preferred_element_type=jnp.float32)
    gate = jnp.dot(rows, w_gate, preferred_element_type=jnp.float32)
    return (jax.nn.sigmoid(gate) * proj).astype(jnp.bfloat16).astype(jnp.float32)


def copy_kernel(source_ref, target_ref):
    target_ref[...] = source_ref[...]


def flat_normed(values, gain, bias):
    flat = values.reshape(-1, values.shape[-1]).astype(jnp.float32)
    return layer_norm(flat, gain, bias, -1).astype(jnp.bfloat16)


def finish(left, right, gating, out_gain_ref, out_bias_ref, w_out_ref):
    sums = []
    for block in right:
        for row in range(left.shape[1]):
            products = block[0] * left[0, row] + block[1] * left[1, row]
            sums.append(jnp.sum(products, axis=1))
    triangle = jnp.concatenate(sums, axis=0).astype(jnp.bfloat16).astype(jnp.float32)
    hidden_normed = layer_norm(triangle, out_gain_ref[...], out_bias_ref[...], -1)
    mixed = jnp.dot(
        hidden_normed.astype(jnp.bfloat16), w_out_ref[...], preferred_element_type=jnp.float32
    )
    return gating * mixed.reshape(gating.shape)


def first_kernel(
    span,
    steps,
    own_ref,
    far_ref,
    swapped_ref,
    near_ref,
    norm_gain_ref,
    norm_bias_ref,
    w_a_proj_ref,
    w_a_gate_ref,
    w_b_proj_ref,
    w_b_gate_ref,
    w_gate_ref,
    out_gain_ref,
    out_bias_ref,
    w_out_ref,
    left_ref,
    gating_ref,
    update_ref,
):
    rows, cols, width = own_ref.shape
    gain, bias = norm_gain_ref[...], norm_bias_ref[...]
    row = lax.axis_index("row")
    crossed = row // span != lax.axis_index("sub")
    own = flat_normed(own_ref[...], gain, bias)
    other = flat_normed(swapped_ref[0], gain, bias)
    for values, place in ((own, jnp.where(crossed, 0, 1)), (other, jnp.where(crossed, 1, 0))):
        left = gated(values, w_a_proj_ref[...], w_a_gate_ref[...])
        left_ref[pl.ds(place, 1)] = left.astype(jnp.bfloat16).reshape(1, rows, cols, -1)
    gating = jax.nn.sigmoid(jnp.dot(own, w_gate_ref[...], preferred_element_type=jnp.float32))
    gating = gating.astype(jnp.bfloat16).astype(jnp.float32).reshape(rows, cols, width)
    for place in range(span):
        part = gating[:, place * rows : (place + 1) * rows]
        gating_ref[place] = part.reshape(rows * rows, width)
    right = []
    for half in (1, 0):
        here = swapped_ref[0] if half else own_ref[...]
        across = swapped_ref[1] if half else far_ref[...]
        right.append(jnp.where(crossed, across, here))
    right = jnp.stack([jnp.stack(right), near_ref[...]])
    right = gated(flat_normed(right, gain, bias), w_b_proj_ref[...], w_b_gate_ref[...])
    right = right.reshape(2, 2, rows, cols, -1)
    base = lax.rem(row, span)
    gating = jnp.stack([gating_ref[base], gating_ref[base ^ steps[0]]])
    left = left_ref[...].astype(jnp.float32)
    update_ref[...] = finish(left, right, gating, out_gain_ref, out_bias_ref, w_out_ref)


def last_kernel(
    span,
    steps,
    second_ref,
    third_ref,
    left_ref,
    gating_ref,
    first_ref,
    norm_gain_ref,
    norm_bias_ref,
    w_b_proj_ref,
    w_b_gate_ref,
    out_gain_ref,
    out_bias_ref,
    w_out_ref,
    update_ref,
    placed_ref,
):
    _, rows, cols, width = second_ref.shape
    base = lax.rem(lax.axis_index("row"), span)
    gain, bias = norm_gain_ref[...], norm_bias_ref[...]
    right = jnp.stack([second_ref[...], third_ref[...]])
    right = gated(flat_normed(right, gain, bias), w_b_proj_ref[...], w_b_gate_ref[...])
    right = right.reshape(2, 2, rows, cols, -1)
    gating = jnp.stack([gating_ref[base ^ steps[1]], gating_ref[base ^ steps[2]]])
    left = left_ref[...].astype(jnp.float32)
    last = finish(left, right, gating, out_gain_ref, out_bias_ref, w_out_ref)
    placed_ref[pl.ds(base, 1)] = first_ref[0:1]
    placed_ref[pl.ds(base ^ steps[0], 1)] = first_ref[1:2]
    placed_ref[pl.ds(base ^ steps[1], 1)] = last[0:1]
    placed_ref[pl.ds(base ^ steps[2], 1)] = last[1:2]
    for row in range(rows):
        parts = [placed_ref[place, row * rows : (row + 1) * rows] for place in range(span)]
        update_ref[row] = jnp.concatenate(parts, axis=0).astype(jnp.bfloat16)


def swap_rows(
    n_row,
    pair_rep,
    norm_gain,
    norm_bias,
    w_a_proj,
    w_a_gate,
    w_b_proj,
    w_b_gate,
    w_gate,
    out_gain,
    out_bias,
    w_out,
):
    span = n_row // 2
    block = pair_rep.shape
    rows, _, width = block
    params = pltpu.CompilerParams(vmem_limit_bytes=KERNEL_BYTES)
    cost = pl.CostEstimate(flops=10**8, bytes_accessed=10**6, transcendentals=0)

    def swap(values, partner):
        devices = [(row, sub) for row in range(n_row) for sub in range(2)]
        partners = [partner(row, sub) for row, sub in devices]
        pairs = [(2 * a + b, 2 * c + d) for (a, b), (c, d) in zip(devices, partners)]
        return lax.ppermute(values, ("row", "sub"), pairs)

    far = swap(pair_rep, lambda row, sub: (row ^ span, 1 - sub))
    own = pl.pallas_call(
        copy_kernel,
        out_shape=jax.ShapeDtypeStruct(block, pair_rep.dtype),
        cost_estimate=cost,
        compiler_params=params,
    )(pair_rep)
    swapped = swap(jnp.stack([own, far]), lambda row, sub: (row, 1 - sub))
    crossed = lax.axis_index("row") // span != lax.axis_index("sub")
    message = jnp.where(crossed, jnp.stack([own, swapped[0]]), jnp.stack([far, swapped[1]]))
    near, second, third = [
        swap(message, lambda row, sub: (row ^ step, 1 - sub)) for step in STEPS
    ]
    norm = (norm_gain[None], norm_bias[None])
    out = (out_gain[None], out_bias[None], w_out)
    left, gating, update = pl.pallas_call(
        functools.partial(first_kernel, span, STEPS),
        out_shape=(
            jax.ShapeDtypeStruct((2,) + block, jnp.bfloat16),
            jax.ShapeDtypeStruct((span, rows * rows, width), jnp.float32),
            jax.ShapeDtypeStruct((2, rows * rows, width), jnp.float32),
        ),
        cost_estimate=cost,
        compiler_params=params,
    )(own, far, swapped, near, *norm, w_a_proj, w_a_gate, w_b_proj, w_b_gate, w_gate, *out)
    return pl.pallas_call(
        functools.partial(last_kernel, span, STEPS),
        out_shape=jax.ShapeDtypeStruct(block, pair_rep.dtype),
        scratch_shapes=[pltpu.VMEM((span, rows * rows, width), jnp.float32)],
        compiler_params=params,
    )(second, third, left, gating, update, *norm, w_b_proj, w_b_gate, *out)


def exchange_channels(
    pair_rep,
    norm_gain,
    norm_bias,
    w_a_proj,
    w_a_gate,
    w_b_proj,
    w_b_gate,
    w_gate,
    out_gain,
    out_bias,
    w_out,
):
    hidden = w_a_proj.shape[1]
    w_inner = jnp.concatenate([w_a_proj, w_a_gate, w_b_proj, w_b_gate], axis=1)
    normed = layer_norm(pair_rep.astype(jnp.float32), norm_gain, norm_bias, -1).astype(jnp.bfloat16)
    inner = jnp.einsum("rkc,cm->mrk", normed, w_inner, preferred_element_type=jnp.float32)
    left_local = (jax.nn.sigmoid(inner[hidden : 2 * hidden]) * inner[:hidden]).astype(jnp.bfloat16)
    right_local = (
        jax.nn.sigmoid(inner[3 * hidden : 4 * hidden]) * inner[2 * hidden : 3 * hidden]
    ).astype(jnp.bfloat16)
    gating = jax.nn.sigmoid(
        jnp.einsum("rkc,cd->rkd", normed, w_gate, preferred_element_type=jnp.float32)
    ).astype(jnp.bfloat16)
    left_chan, right_chan = (
        lax.all_to_all(left_local, "row", split_axis=0, concat_axis=1, tiled=True),
        lax.all_to_all(right_local, "row", split_axis=0, concat_axis=1, tiled=True),
    )
    left_rows = lax.all_to_all(left_chan, "sub", split_axis=1, concat_axis=2, tiled=True)
    triangle = jnp.einsum(
        "hik,hjk->hij",
        left_rows,
        lax.all_gather(right_chan, "sub", axis=2, tiled=True),
        preferred_element_type=jnp.float32,
    ).astype(jnp.bfloat16)
    regrouped = lax.all_to_all(
        lax.all_to_all(triangle, "sub", split_axis=2, concat_axis=1, tiled=True),
        "row",
        split_axis=1,
        concat_axis=0,
        tiled=True,
    )
    hidden_normed = layer_norm(
        regrouped.astype(jnp.float32), out_gain[:, None, None], out_bias[:, None, None], 0
    ).astype(jnp.bfloat16)
    mixed = jnp.einsum("hrj,hc->rjc", hidden_normed, w_out, preferred_element_type=jnp.float32)
    return (gating.astype(jnp.float32) * mixed).astype(jnp.bfloat16)


def solution(mesh):
    n_row, n_sub = mesh.shape["row"], mesh.shape["sub"]

    def per_device(pair_rep, *weights):
        rows, cols, _ = pair_rep.shape
        gathered = n_row * n_sub * pair_rep.size * pair_rep.dtype.itemsize
        if n_sub == 2 and n_row == 8 and cols == n_row // 2 * rows and gathered <= GATHER_BYTES:
            return swap_rows(n_row, pair_rep, *weights)
        return exchange_channels(pair_rep, *weights)

    in_specs = (P(("grp", "row"), "sub", None), P(), P(), P(), P(), P(), P(), P(), P(), P(), P())
    out_specs = P(("grp", "row"), "sub", None)
    return jax.shard_map(
        per_device, mesh=mesh, in_specs=in_specs, out_specs=out_specs, check_vma=False
    )
```

```python
import functools

import jax
import jax.numpy as jnp
from jax import lax
from jax.experimental import pallas as pl
from jax.experimental.pallas import tpu as pltpu
from jax.sharding import PartitionSpec as P

EPSILON = 1e-05
GATHER_BYTES = 2 * 1024 * 1024
KERNEL_BYTES = 4 * 1024 * 1024


def layer_norm(values, gain, shift, axis):
    centred = values - jnp.mean(values, axis=axis, keepdims=True)
    variance = jnp.mean(centred * centred, axis=axis, keepdims=True)
    return centred * lax.rsqrt(variance + EPSILON) * gain + shift


def gated(rows, w_proj, w_gate):
    proj = jnp.dot(rows, w_proj, preferred_element_type=jnp.float32)
    gate = jnp.dot(rows, w_gate, preferred_element_type=jnp.float32)
    return (jax.nn.sigmoid(gate) * proj).astype(jnp.bfloat16).astype(jnp.float32)


def copy_kernel(source_ref, target_ref):
    target_ref[...] = source_ref[...]


def flat_normed(values, gain, bias):
    flat = values.reshape(-1, values.shape[-1]).astype(jnp.float32)
    return layer_norm(flat, gain, bias, -1).astype(jnp.bfloat16)


def finish(left, right, gating, out_gain_ref, out_bias_ref, w_out_ref):
    sums = []
    for block in right:
        for row in range(left.shape[1]):
            products = block[0] * left[0, row] + block[1] * left[1, row]
            sums.append(jnp.sum(products, axis=1))
    triangle = jnp.concatenate(sums, axis=0).astype(jnp.bfloat16).astype(jnp.float32)
    hidden_normed = layer_norm(triangle, out_gain_ref[...], out_bias_ref[...], -1)
    mixed = jnp.dot(
        hidden_normed.astype(jnp.bfloat16), w_out_ref[...], preferred_element_type=jnp.float32
    )
    return gating * mixed.reshape(gating.shape)


def first_kernel(
    own_ref,
    other_ref,
    norm_gain_ref,
    norm_bias_ref,
    w_a_proj_ref,
    w_a_gate_ref,
    w_b_proj_ref,
    w_b_gate_ref,
    w_gate_ref,
    out_gain_ref,
    out_bias_ref,
    w_out_ref,
    left_ref,
    gating_ref,
):
    rows, cols, width = own_ref.shape
    gain, bias = norm_gain_ref[...], norm_bias_ref[...]
    sub = lax.axis_index("sub")
    own = flat_normed(own_ref[...], gain, bias)
    other = flat_normed(other_ref[...], gain, bias)
    for values, place in ((own, sub), (other, 1 - sub)):
        left = gated(values, w_a_proj_ref[...], w_a_gate_ref[...])
        left_ref[pl.ds(place, 1)] = left.astype(jnp.bfloat16).reshape(1, rows, cols, -1)
    gating = jax.nn.sigmoid(jnp.dot(own, w_gate_ref[...], preferred_element_type=jnp.float32))
    gating = gating.astype(jnp.bfloat16).astype(jnp.float32).reshape(rows, cols, width)
    for place in range(cols // rows):
        part = gating[:, place * rows : (place + 1) * rows]
        gating_ref[place] = part.reshape(rows * rows, width)


def last_kernel(
    span,
    blocks_ref,
    left_ref,
    gating_ref,
    norm_gain_ref,
    norm_bias_ref,
    w_b_proj_ref,
    w_b_gate_ref,
    out_gain_ref,
    out_bias_ref,
    w_out_ref,
    update_ref,
):
    _, rows, cols, width = blocks_ref.shape
    gain, bias = norm_gain_ref[...], norm_bias_ref[...]
    right = gated(flat_normed(blocks_ref[...], gain, bias), w_b_proj_ref[...], w_b_gate_ref[...])
    right = right.reshape(span, 2, rows, cols, -1)
    crossed = lax.axis_index("row") // span != lax.axis_index("sub")
    first = left_ref[jnp.where(crossed, 1, 0)]
    second = left_ref[jnp.where(crossed, 0, 1)]
    left = jnp.stack([first, second]).astype(jnp.float32)
    update = finish(left, right, gating_ref[...], out_gain_ref, out_bias_ref, w_out_ref)
    for row in range(rows):
        parts = [update[place, row * rows : (row + 1) * rows] for place in range(span)]
        update_ref[row] = jnp.concatenate(parts, axis=0).astype(jnp.bfloat16)


def gather_span(
    n_row,
    pair_rep,
    norm_gain,
    norm_bias,
    w_a_proj,
    w_a_gate,
    w_b_proj,
    w_b_gate,
    w_gate,
    out_gain,
    out_bias,
    w_out,
):
    span = n_row // 2
    block = pair_rep.shape
    rows, _, width = block
    axes = ("row", "sub")
    params = pltpu.CompilerParams(vmem_limit_bytes=KERNEL_BYTES)
    cost = pl.CostEstimate(flops=10**8, bytes_accessed=10**6, transcendentals=0)

    def swap(values, partner):
        devices = [(row, sub) for row in range(n_row) for sub in range(2)]
        partners = [partner(row, sub) for row, sub in devices]
        pairs = [(2 * a + b, 2 * c + d) for (a, b), (c, d) in zip(devices, partners)]
        return lax.ppermute(values, axes, pairs)

    far = swap(pair_rep, lambda row, sub: (row ^ span, 1 - sub))
    own = pl.pallas_call(
        copy_kernel,
        out_shape=jax.ShapeDtypeStruct(block, pair_rep.dtype),
        cost_estimate=cost,
        compiler_params=params,
    )(pair_rep)
    other = swap(own, lambda row, sub: (row, 1 - sub))
    lower = lax.axis_index("row") // span == 0
    spans = jnp.stack([jnp.where(lower, own, far), jnp.where(lower, far, own)])
    messages = jnp.broadcast_to(spans, (span, 2) + block).reshape((n_row,) + block)
    groups = [list(range(n_row)), list(range(n_row, 2 * n_row))]
    blocks = lax.all_to_all(
        messages, axes, split_axis=0, concat_axis=0, axis_index_groups=groups, tiled=True
    )
    norm = (norm_gain[None], norm_bias[None])
    out = (out_gain[None], out_bias[None], w_out)
    left, gating = pl.pallas_call(
        first_kernel,
        out_shape=(
            jax.ShapeDtypeStruct((2,) + block, jnp.bfloat16),
            jax.ShapeDtypeStruct((span, rows * rows, width), jnp.float32),
        ),
        cost_estimate=cost,
        compiler_params=params,
    )(own, other, *norm, w_a_proj, w_a_gate, w_b_proj, w_b_gate, w_gate, *out)
    return pl.pallas_call(
        functools.partial(last_kernel, span),
        out_shape=jax.ShapeDtypeStruct(block, pair_rep.dtype),
        compiler_params=params,
    )(blocks, left, gating, *norm, w_b_proj, w_b_gate, *out)


def exchange_channels(
    pair_rep,
    norm_gain,
    norm_bias,
    w_a_proj,
    w_a_gate,
    w_b_proj,
    w_b_gate,
    w_gate,
    out_gain,
    out_bias,
    w_out,
):
    hidden = w_a_proj.shape[1]
    w_inner = jnp.concatenate([w_a_proj, w_a_gate, w_b_proj, w_b_gate], axis=1)
    normed = layer_norm(pair_rep.astype(jnp.float32), norm_gain, norm_bias, -1).astype(jnp.bfloat16)
    inner = jnp.einsum("rkc,cm->mrk", normed, w_inner, preferred_element_type=jnp.float32)
    left_local = (jax.nn.sigmoid(inner[hidden : 2 * hidden]) * inner[:hidden]).astype(jnp.bfloat16)
    right_local = (
        jax.nn.sigmoid(inner[3 * hidden : 4 * hidden]) * inner[2 * hidden : 3 * hidden]
    ).astype(jnp.bfloat16)
    gating = jax.nn.sigmoid(
        jnp.einsum("rkc,cd->rkd", normed, w_gate, preferred_element_type=jnp.float32)
    ).astype(jnp.bfloat16)
    left_chan, right_chan = (
        lax.all_to_all(left_local, "row", split_axis=0, concat_axis=1, tiled=True),
        lax.all_to_all(right_local, "row", split_axis=0, concat_axis=1, tiled=True),
    )
    left_rows = lax.all_to_all(left_chan, "sub", split_axis=1, concat_axis=2, tiled=True)
    triangle = jnp.einsum(
        "hik,hjk->hij",
        left_rows,
        lax.all_gather(right_chan, "sub", axis=2, tiled=True),
        preferred_element_type=jnp.float32,
    ).astype(jnp.bfloat16)
    regrouped = lax.all_to_all(
        lax.all_to_all(triangle, "sub", split_axis=2, concat_axis=1, tiled=True),
        "row",
        split_axis=1,
        concat_axis=0,
        tiled=True,
    )
    hidden_normed = layer_norm(
        regrouped.astype(jnp.float32), out_gain[:, None, None], out_bias[:, None, None], 0
    ).astype(jnp.bfloat16)
    mixed = jnp.einsum("hrj,hc->rjc", hidden_normed, w_out, preferred_element_type=jnp.float32)
    return (gating.astype(jnp.float32) * mixed).astype(jnp.bfloat16)


def solution(mesh):
    n_row, n_sub = mesh.shape["row"], mesh.shape["sub"]

    def per_device(pair_rep, *weights):
        rows, cols, _ = pair_rep.shape
        gathered = n_row * n_sub * pair_rep.size * pair_rep.dtype.itemsize
        if n_sub == 2 and n_row == 8 and cols == n_row // 2 * rows and gathered <= GATHER_BYTES:
            return gather_span(n_row, pair_rep, *weights)
        return exchange_channels(pair_rep, *weights)

    in_specs = (P(("grp", "row"), "sub", None), P(), P(), P(), P(), P(), P(), P(), P(), P(), P())
    out_specs = P(("grp", "row"), "sub", None)
    return jax.shard_map(
        per_device, mesh=mesh, in_specs=in_specs, out_specs=out_specs, check_vma=False
    )
```

```python
import functools

import jax
import jax.numpy as jnp
from jax import lax
from jax.experimental import pallas as pl
from jax.experimental.pallas import tpu as pltpu
from jax.sharding import PartitionSpec as P

EPSILON = 1e-05
GATHER_BYTES = 2 * 1024 * 1024
KERNEL_BYTES = 4 * 1024 * 1024
ROUTES = (
    (4, 11, 1, 12, 3, 15, 0, 8, 5, 10, 2, 13, 6, 9, 7, 14),
    (7, 14, 4, 8, 1, 13, 2, 15, 0, 12, 6, 10, 5, 11, 3, 9),
    (3, 12, 6, 15, 5, 10, 4, 13, 7, 8, 1, 9, 2, 14, 0, 11),
    (1, 9, 3, 10, 6, 8, 7, 11, 2, 15, 5, 14, 0, 12, 4, 13),
)


def layer_norm(values, gain, shift, axis):
    centred = values - jnp.mean(values, axis=axis, keepdims=True)
    variance = jnp.mean(centred * centred, axis=axis, keepdims=True)
    return centred * lax.rsqrt(variance + EPSILON) * gain + shift


def gated(rows, w_proj, w_gate):
    proj = jnp.dot(rows, w_proj, preferred_element_type=jnp.float32)
    gate = jnp.dot(rows, w_gate, preferred_element_type=jnp.float32)
    return (jax.nn.sigmoid(gate) * proj).astype(jnp.bfloat16).astype(jnp.float32)


def lookup(values, bits):
    word = sum(value << (bits * place) for place, value in enumerate(values))
    word = jnp.int32(word - (1 << 32) if word >> 31 else word)
    device = lax.axis_index("row") * 2 + lax.axis_index("sub")
    return lax.shift_right_logical(word, device * bits) & ((1 << bits) - 1)


def place_of(sources, span):
    place = lookup([source // 2 % span for source in sources], 2)
    return place, lookup([source % 2 for source in sources], 1)


def load_kernel(pair_ref, norm_gain_ref, norm_bias_ref, out_gain_ref, out_bias_ref, own_ref, vectors_ref):
    own_ref[...] = pair_ref[...]
    for place, ref in enumerate((norm_gain_ref, norm_bias_ref, out_gain_ref, out_bias_ref)):
        vectors_ref[place : place + 1] = ref[...]


def flat_normed(values, vectors_ref):
    flat = values.reshape(-1, values.shape[-1]).astype(jnp.float32)
    return layer_norm(flat, vectors_ref[0:1], vectors_ref[1:2], -1).astype(jnp.bfloat16)


def finish(left_ref, blocks, places, gating_ref, vectors_ref, w_out_ref):
    sums, gates = [], []
    for block, (place, half) in zip(blocks, places):
        left = left_ref[half].astype(jnp.float32), left_ref[1 - half].astype(jnp.float32)
        for row in range(left_ref.shape[1]):
            products = block[0] * left[0][row] + block[1] * left[1][row]
            sums.append(jnp.sum(products, axis=1))
        gates.append(gating_ref[place])
    triangle = jnp.concatenate(sums, axis=0).astype(jnp.bfloat16).astype(jnp.float32)
    hidden_normed = layer_norm(triangle, vectors_ref[2:3], vectors_ref[3:4], -1)
    mixed = jnp.dot(
        hidden_normed.astype(jnp.bfloat16), w_out_ref[...], preferred_element_type=jnp.float32
    )
    return (jnp.concatenate(gates, axis=0) * mixed).reshape(len(gates), -1, mixed.shape[-1])


def first_kernel(
    span,
    routes,
    own_ref,
    other_ref,
    block_ref,
    vectors_ref,
    w_a_proj_ref,
    w_a_gate_ref,
    w_b_proj_ref,
    w_b_gate_ref,
    w_gate_ref,
    w_out_ref,
    left_ref,
    gating_ref,
    update_ref,
):
    rows, cols, width = own_ref.shape
    sub = lax.axis_index("sub")
    own = flat_normed(own_ref[...], vectors_ref)
    other = flat_normed(other_ref[...], vectors_ref)
    for values, half in ((own, sub), (other, 1 - sub)):
        left = gated(values, w_a_proj_ref[...], w_a_gate_ref[...])
        left_ref[pl.ds(half, 1)] = left.astype(jnp.bfloat16).reshape(1, rows, cols, -1)
    gating = jax.nn.sigmoid(jnp.dot(own, w_gate_ref[...], preferred_element_type=jnp.float32))
    gating = gating.astype(jnp.bfloat16).astype(jnp.float32).reshape(rows, cols, width)
    for place in range(span):
        part = gating[:, place * rows : (place + 1) * rows]
        gating_ref[place] = part.reshape(rows * rows, width)
    right = gated(flat_normed(block_ref[...], vectors_ref), w_b_proj_ref[...], w_b_gate_ref[...])
    right = right.reshape(1, 2, rows, cols, -1)
    places = [place_of(routes[0], span)]
    update_ref[...] = finish(left_ref, right, places, gating_ref, vectors_ref, w_out_ref)


def last_kernel(span, routes, *refs):
    block_refs = refs[: span - 1][::-1]
    (
        left_ref,
        gating_ref,
        first_ref,
        vectors_ref,
        w_b_proj_ref,
        w_b_gate_ref,
        w_out_ref,
        update_ref,
        placed_ref,
    ) = refs[span - 1 :]
    _, rows, cols, width = block_refs[0].shape
    right = jnp.stack([ref[...] for ref in block_refs])
    right = gated(flat_normed(right, vectors_ref), w_b_proj_ref[...], w_b_gate_ref[...])
    right = right.reshape(span - 1, 2, rows, cols, -1)
    places = [place_of(sources, span) for sources in routes]
    last = finish(left_ref, right, places[1:], gating_ref, vectors_ref, w_out_ref)
    placed_ref[pl.ds(places[0][0], 1)] = first_ref[...]
    for step in range(span - 1):
        placed_ref[pl.ds(places[step + 1][0], 1)] = last[step : step + 1]
    for row in range(rows):
        parts = [placed_ref[place, row * rows : (row + 1) * rows] for place in range(span)]
        update_ref[row] = jnp.concatenate(parts, axis=0).astype(jnp.bfloat16)


def gather_span(
    routes,
    pair_rep,
    norm_gain,
    norm_bias,
    w_a_proj,
    w_a_gate,
    w_b_proj,
    w_b_gate,
    w_gate,
    out_gain,
    out_bias,
    w_out,
):
    span = len(routes)
    block = pair_rep.shape
    rows, _, width = block
    params = pltpu.CompilerParams(vmem_limit_bytes=KERNEL_BYTES)
    cost = pl.CostEstimate(flops=10**8, bytes_accessed=10**6, transcendentals=0)

    def receive(values, sources):
        pairs = [(source, device) for device, source in enumerate(sources)]
        return lax.ppermute(values, ("row", "sub"), pairs)

    other = receive(pair_rep, [device ^ 1 for device in range(4 * span)])
    own, vectors = pl.pallas_call(
        load_kernel,
        out_shape=(
            jax.ShapeDtypeStruct(block, pair_rep.dtype),
            jax.ShapeDtypeStruct((4, width), jnp.float32),
        ),
        cost_estimate=cost,
        compiler_params=params,
    )(pair_rep, norm_gain[None], norm_bias[None], out_gain[None], out_bias[None])
    pair = jnp.stack([own, other])
    blocks = [receive(pair, sources) for sources in routes]
    left, gating, update = pl.pallas_call(
        functools.partial(first_kernel, span, routes),
        out_shape=(
            jax.ShapeDtypeStruct((2,) + block, jnp.bfloat16),
            jax.ShapeDtypeStruct((span, rows * rows, width), jnp.float32),
            jax.ShapeDtypeStruct((1, rows * rows, width), jnp.float32),
        ),
        cost_estimate=cost,
        compiler_params=params,
    )(own, other, blocks[0], vectors, w_a_proj, w_a_gate, w_b_proj, w_b_gate, w_gate, w_out)
    return pl.pallas_call(
        functools.partial(last_kernel, span, routes),
        out_shape=jax.ShapeDtypeStruct(block, pair_rep.dtype),
        scratch_shapes=[pltpu.VMEM((span, rows * rows, width), jnp.float32)],
        compiler_params=params,
    )(*blocks[:0:-1], left, gating, update, vectors, w_b_proj, w_b_gate, w_out)


def exchange_channels(
    pair_rep,
    norm_gain,
    norm_bias,
    w_a_proj,
    w_a_gate,
    w_b_proj,
    w_b_gate,
    w_gate,
    out_gain,
    out_bias,
    w_out,
):
    hidden = w_a_proj.shape[1]
    w_inner = jnp.concatenate([w_a_proj, w_a_gate, w_b_proj, w_b_gate], axis=1)
    normed = layer_norm(pair_rep.astype(jnp.float32), norm_gain, norm_bias, -1).astype(jnp.bfloat16)
    inner = jnp.einsum("rkc,cm->mrk", normed, w_inner, preferred_element_type=jnp.float32)
    left_local = (jax.nn.sigmoid(inner[hidden : 2 * hidden]) * inner[:hidden]).astype(jnp.bfloat16)
    right_local = (
        jax.nn.sigmoid(inner[3 * hidden : 4 * hidden]) * inner[2 * hidden : 3 * hidden]
    ).astype(jnp.bfloat16)
    gating = jax.nn.sigmoid(
        jnp.einsum("rkc,cd->rkd", normed, w_gate, preferred_element_type=jnp.float32)
    ).astype(jnp.bfloat16)
    left_chan, right_chan = (
        lax.all_to_all(left_local, "row", split_axis=0, concat_axis=1, tiled=True),
        lax.all_to_all(right_local, "row", split_axis=0, concat_axis=1, tiled=True),
    )
    left_rows = lax.all_to_all(left_chan, "sub", split_axis=1, concat_axis=2, tiled=True)
    triangle = jnp.einsum(
        "hik,hjk->hij",
        left_rows,
        lax.all_gather(right_chan, "sub", axis=2, tiled=True),
        preferred_element_type=jnp.float32,
    ).astype(jnp.bfloat16)
    regrouped = lax.all_to_all(
        lax.all_to_all(triangle, "sub", split_axis=2, concat_axis=1, tiled=True),
        "row",
        split_axis=1,
        concat_axis=0,
        tiled=True,
    )
    hidden_normed = layer_norm(
        regrouped.astype(jnp.float32), out_gain[:, None, None], out_bias[:, None, None], 0
    ).astype(jnp.bfloat16)
    mixed = jnp.einsum("hrj,hc->rjc", hidden_normed, w_out, preferred_element_type=jnp.float32)
    return (gating.astype(jnp.float32) * mixed).astype(jnp.bfloat16)


def solution(mesh):
    n_row, n_sub = mesh.shape["row"], mesh.shape["sub"]

    def per_device(pair_rep, *weights):
        rows, cols, _ = pair_rep.shape
        gathered = n_row * n_sub * pair_rep.size * pair_rep.dtype.itemsize
        routed = (n_row, n_sub) == (8, 2) and cols == n_row // 2 * rows
        if routed and gathered <= GATHER_BYTES:
            return gather_span(ROUTES, pair_rep, *weights)
        return exchange_channels(pair_rep, *weights)

    in_specs = (P(("grp", "row"), "sub", None), P(), P(), P(), P(), P(), P(), P(), P(), P(), P())
    out_specs = P(("grp", "row"), "sub", None)
    return jax.shard_map(
        per_device, mesh=mesh, in_specs=in_specs, out_specs=out_specs, check_vma=False
    )
```

```python
import functools

import jax
import jax.numpy as jnp
from jax import lax
from jax.experimental import pallas as pl
from jax.experimental.pallas import tpu as pltpu
from jax.sharding import PartitionSpec as P

EPSILON = 1e-05
GATHER_BYTES = 2 * 1024 * 1024
KERNEL_BYTES = 4 * 1024 * 1024
ROUTES = (
    (5, 13, 1, 9, 0, 15, 2, 11, 3, 8, 4, 10, 6, 12, 7, 14),
    (6, 15, 5, 13, 2, 10, 7, 9, 1, 12, 3, 14, 0, 8, 4, 11),
    (3, 11, 7, 14, 5, 12, 4, 13, 6, 15, 1, 9, 2, 10, 0, 8),
    (1, 9, 3, 11, 6, 8, 0, 15, 5, 10, 7, 12, 4, 14, 2, 13),
)


def layer_norm(values, gain, shift, axis):
    centred = values - jnp.mean(values, axis=axis, keepdims=True)
    variance = jnp.mean(centred * centred, axis=axis, keepdims=True)
    return centred * lax.rsqrt(variance + EPSILON) * gain + shift


def gated(rows, w_proj, w_gate):
    proj = jnp.dot(rows, w_proj, preferred_element_type=jnp.float32)
    gate = jnp.dot(rows, w_gate, preferred_element_type=jnp.float32)
    return (jax.nn.sigmoid(gate) * proj).astype(jnp.bfloat16).astype(jnp.float32)


def lookup(values, bits):
    word = sum(value << (bits * place) for place, value in enumerate(values))
    word = jnp.int32(word - (1 << 32) if word >> 31 else word)
    device = lax.axis_index("row") * 2 + lax.axis_index("sub")
    return lax.shift_right_logical(word, device * bits) & ((1 << bits) - 1)


def place_of(sources, span):
    place = lookup([source // 2 % span for source in sources], 2)
    return place, lookup([source % 2 for source in sources], 1)


def copy_kernel(source_ref, target_ref):
    target_ref[...] = source_ref[...]


def flat_normed(values, gain_ref, bias_ref):
    flat = values.reshape(-1, values.shape[-1]).astype(jnp.float32)
    return layer_norm(flat, gain_ref[...], bias_ref[...], -1).astype(jnp.bfloat16)


def finish(left_ref, blocks, places, gating_ref, out_gain_ref, out_bias_ref, w_out_ref):
    sums, gates = [], []
    for block, (place, half) in zip(blocks, places):
        left = left_ref[half].astype(jnp.float32), left_ref[1 - half].astype(jnp.float32)
        for row in range(left_ref.shape[1]):
            products = block[0] * left[0][row] + block[1] * left[1][row]
            sums.append(jnp.sum(products, axis=1))
        gates.append(gating_ref[place])
    triangle = jnp.concatenate(sums, axis=0).astype(jnp.bfloat16).astype(jnp.float32)
    hidden_normed = layer_norm(triangle, out_gain_ref[...], out_bias_ref[...], -1)
    mixed = jnp.dot(
        hidden_normed.astype(jnp.bfloat16), w_out_ref[...], preferred_element_type=jnp.float32
    )
    return (jnp.concatenate(gates, axis=0) * mixed).reshape(len(gates), -1, mixed.shape[-1])


def first_kernel(
    span,
    routes,
    own_ref,
    other_ref,
    block_ref,
    norm_gain_ref,
    norm_bias_ref,
    w_a_proj_ref,
    w_a_gate_ref,
    w_b_proj_ref,
    w_b_gate_ref,
    w_gate_ref,
    out_gain_ref,
    out_bias_ref,
    w_out_ref,
    left_ref,
    gating_ref,
    update_ref,
):
    rows, cols, width = own_ref.shape
    sub = lax.axis_index("sub")
    own = flat_normed(own_ref[...], norm_gain_ref, norm_bias_ref)
    other = flat_normed(other_ref[...], norm_gain_ref, norm_bias_ref)
    for values, half in ((own, sub), (other, 1 - sub)):
        left = gated(values, w_a_proj_ref[...], w_a_gate_ref[...])
        left_ref[pl.ds(half, 1)] = left.astype(jnp.bfloat16).reshape(1, rows, cols, -1)
    gating = jax.nn.sigmoid(jnp.dot(own, w_gate_ref[...], preferred_element_type=jnp.float32))
    gating = gating.astype(jnp.bfloat16).astype(jnp.float32).reshape(rows, cols, width)
    for place in range(span):
        part = gating[:, place * rows : (place + 1) * rows]
        gating_ref[place] = part.reshape(rows * rows, width)
    right = gated(flat_normed(block_ref[...], norm_gain_ref, norm_bias_ref), w_b_proj_ref[...], w_b_gate_ref[...])
    right = right.reshape(1, 2, rows, cols, -1)
    places = [place_of(routes[0], span)]
    update_ref[...] = finish(left_ref, right, places, gating_ref, out_gain_ref, out_bias_ref, w_out_ref)


def last_kernel(span, routes, *refs):
    block_refs = refs[: span - 1][::-1]
    (
        left_ref,
        gating_ref,
        first_ref,
        norm_gain_ref,
        norm_bias_ref,
        w_b_proj_ref,
        w_b_gate_ref,
        out_gain_ref,
        out_bias_ref,
        w_out_ref,
        update_ref,
        placed_ref,
    ) = refs[span - 1 :]
    _, rows, cols, width = block_refs[0].shape
    right = jnp.stack([ref[...] for ref in block_refs])
    right = gated(flat_normed(right, norm_gain_ref, norm_bias_ref), w_b_proj_ref[...], w_b_gate_ref[...])
    right = right.reshape(span - 1, 2, rows, cols, -1)
    places = [place_of(sources, span) for sources in routes]
    last = finish(left_ref, right, places[1:], gating_ref, out_gain_ref, out_bias_ref, w_out_ref)
    placed_ref[pl.ds(places[0][0], 1)] = first_ref[...]
    for step in range(span - 1):
        placed_ref[pl.ds(places[step + 1][0], 1)] = last[step : step + 1]
    for row in range(rows):
        parts = [placed_ref[place, row * rows : (row + 1) * rows] for place in range(span)]
        update_ref[row] = jnp.concatenate(parts, axis=0).astype(jnp.bfloat16)


def gather_span(
    routes,
    pair_rep,
    norm_gain,
    norm_bias,
    w_a_proj,
    w_a_gate,
    w_b_proj,
    w_b_gate,
    w_gate,
    out_gain,
    out_bias,
    w_out,
):
    span = len(routes)
    block = pair_rep.shape
    rows, _, width = block
    params = pltpu.CompilerParams(vmem_limit_bytes=KERNEL_BYTES)
    cost = pl.CostEstimate(flops=10**8, bytes_accessed=10**6, transcendentals=0)

    def receive(values, sources):
        pairs = [(source, device) for device, source in enumerate(sources)]
        return lax.ppermute(values, ("row", "sub"), pairs)

    other = receive(pair_rep, [device ^ 1 for device in range(4 * span)])
    own = pl.pallas_call(
        copy_kernel,
        out_shape=jax.ShapeDtypeStruct(block, pair_rep.dtype),
        cost_estimate=cost,
        compiler_params=params,
    )(pair_rep)
    pair = jnp.stack([own, other])
    blocks = [receive(pair, sources) for sources in routes]
    norm = (norm_gain[None], norm_bias[None])
    out = (out_gain[None], out_bias[None], w_out)
    left, gating, update = pl.pallas_call(
        functools.partial(first_kernel, span, routes),
        out_shape=(
            jax.ShapeDtypeStruct((2,) + block, jnp.bfloat16),
            jax.ShapeDtypeStruct((span, rows * rows, width), jnp.float32),
            jax.ShapeDtypeStruct((1, rows * rows, width), jnp.float32),
        ),
        cost_estimate=cost,
        compiler_params=params,
    )(own, other, blocks[0], *norm, w_a_proj, w_a_gate, w_b_proj, w_b_gate, w_gate, *out)
    return pl.pallas_call(
        functools.partial(last_kernel, span, routes),
        out_shape=jax.ShapeDtypeStruct(block, pair_rep.dtype),
        scratch_shapes=[pltpu.VMEM((span, rows * rows, width), jnp.float32)],
        compiler_params=params,
    )(*blocks[:0:-1], left, gating, update, *norm, w_b_proj, w_b_gate, *out)


def exchange_channels(
    pair_rep,
    norm_gain,
    norm_bias,
    w_a_proj,
    w_a_gate,
    w_b_proj,
    w_b_gate,
    w_gate,
    out_gain,
    out_bias,
    w_out,
):
    hidden = w_a_proj.shape[1]
    w_inner = jnp.concatenate([w_a_proj, w_a_gate, w_b_proj, w_b_gate], axis=1)
    normed = layer_norm(pair_rep.astype(jnp.float32), norm_gain, norm_bias, -1).astype(jnp.bfloat16)
    inner = jnp.einsum("rkc,cm->mrk", normed, w_inner, preferred_element_type=jnp.float32)
    left_local = (jax.nn.sigmoid(inner[hidden : 2 * hidden]) * inner[:hidden]).astype(jnp.bfloat16)
    right_local = (
        jax.nn.sigmoid(inner[3 * hidden : 4 * hidden]) * inner[2 * hidden : 3 * hidden]
    ).astype(jnp.bfloat16)
    gating = jax.nn.sigmoid(
        jnp.einsum("rkc,cd->rkd", normed, w_gate, preferred_element_type=jnp.float32)
    ).astype(jnp.bfloat16)
    left_chan, right_chan = (
        lax.all_to_all(left_local, "row", split_axis=0, concat_axis=1, tiled=True),
        lax.all_to_all(right_local, "row", split_axis=0, concat_axis=1, tiled=True),
    )
    left_rows = lax.all_to_all(left_chan, "sub", split_axis=1, concat_axis=2, tiled=True)
    triangle = jnp.einsum(
        "hik,hjk->hij",
        left_rows,
        lax.all_gather(right_chan, "sub", axis=2, tiled=True),
        preferred_element_type=jnp.float32,
    ).astype(jnp.bfloat16)
    regrouped = lax.all_to_all(
        lax.all_to_all(triangle, "sub", split_axis=2, concat_axis=1, tiled=True),
        "row",
        split_axis=1,
        concat_axis=0,
        tiled=True,
    )
    hidden_normed = layer_norm(
        regrouped.astype(jnp.float32), out_gain[:, None, None], out_bias[:, None, None], 0
    ).astype(jnp.bfloat16)
    mixed = jnp.einsum("hrj,hc->rjc", hidden_normed, w_out, preferred_element_type=jnp.float32)
    return (gating.astype(jnp.float32) * mixed).astype(jnp.bfloat16)


def solution(mesh):
    n_row, n_sub = mesh.shape["row"], mesh.shape["sub"]

    def per_device(pair_rep, *weights):
        rows, cols, _ = pair_rep.shape
        gathered = n_row * n_sub * pair_rep.size * pair_rep.dtype.itemsize
        routed = (n_row, n_sub) == (8, 2) and cols == n_row // 2 * rows
        if routed and gathered <= GATHER_BYTES:
            return gather_span(ROUTES, pair_rep, *weights)
        return exchange_channels(pair_rep, *weights)

    in_specs = (P(("grp", "row"), "sub", None), P(), P(), P(), P(), P(), P(), P(), P(), P(), P())
    out_specs = P(("grp", "row"), "sub", None)
    return jax.shard_map(
        per_device, mesh=mesh, in_specs=in_specs, out_specs=out_specs, check_vma=False
    )
```

```python
import functools

import jax
import jax.numpy as jnp
from jax import lax
from jax.experimental import pallas as pl
from jax.experimental.pallas import tpu as pltpu
from jax.sharding import PartitionSpec as P

EPSILON = 1e-05
GATHER_BYTES = 2 * 1024 * 1024
KERNEL_BYTES = 4 * 1024 * 1024
ROUTES = (
    (3, 14, 4, 9, 5, 11, 0, 8, 1, 10, 7, 15, 2, 12, 6, 13),
    (6, 13, 3, 12, 1, 15, 7, 11, 5, 8, 4, 10, 0, 9, 2, 14),
    (5, 11, 7, 15, 3, 9, 4, 13, 2, 14, 1, 12, 6, 10, 0, 8),
    (1, 9, 0, 11, 7, 13, 2, 15, 6, 12, 3, 8, 4, 14, 5, 10),
)


def layer_norm(values, gain, shift, axis):
    centred = values - jnp.mean(values, axis=axis, keepdims=True)
    variance = jnp.mean(centred * centred, axis=axis, keepdims=True)
    return centred * lax.rsqrt(variance + EPSILON) * gain + shift


def sigmoid(values):
    return 0.5 * jnp.tanh(0.5 * values) + 0.5


def gated(rows, w_proj, w_gate):
    proj = jnp.dot(rows, w_proj, preferred_element_type=jnp.float32)
    gate = jnp.dot(rows, w_gate, preferred_element_type=jnp.float32)
    return sigmoid(gate) * proj


def lookup(values, bits):
    word = sum(value << (bits * place) for place, value in enumerate(values))
    word = jnp.int32(word - (1 << 32) if word >> 31 else word)
    device = lax.axis_index("row") * 2 + lax.axis_index("sub")
    return lax.shift_right_logical(word, device * bits) & ((1 << bits) - 1)


def place_of(sources, span):
    place = lookup([source // 2 % span for source in sources], 2)
    return place, lookup([source % 2 for source in sources], 1)


def copy_kernel(source_ref, target_ref):
    target_ref[...] = source_ref[...]


def flat_normed(values, gain_ref, bias_ref):
    flat = values.reshape(-1, values.shape[-1]).astype(jnp.float32)
    return layer_norm(flat, gain_ref[...], bias_ref[...], -1).astype(jnp.bfloat16)


def finish(left_ref, blocks, places, gating_ref, out_gain_ref, out_bias_ref, w_out_ref):
    sums, gates = [], []
    for block, (place, half) in zip(blocks, places):
        left = left_ref[half], left_ref[1 - half]
        for row in range(left_ref.shape[1]):
            products = block[0] * left[0][row] + block[1] * left[1][row]
            sums.append(jnp.sum(products, axis=1))
        gates.append(gating_ref[place])
    triangle = jnp.concatenate(sums, axis=0)
    hidden_normed = layer_norm(triangle, out_gain_ref[...], out_bias_ref[...], -1)
    mixed = jnp.dot(
        hidden_normed.astype(jnp.bfloat16), w_out_ref[...], preferred_element_type=jnp.float32
    )
    return (jnp.concatenate(gates, axis=0) * mixed).reshape(len(gates), -1, mixed.shape[-1])


def first_kernel(
    span,
    routes,
    own_ref,
    other_ref,
    block_ref,
    norm_gain_ref,
    norm_bias_ref,
    w_a_proj_ref,
    w_a_gate_ref,
    w_b_proj_ref,
    w_b_gate_ref,
    w_gate_ref,
    out_gain_ref,
    out_bias_ref,
    w_out_ref,
    left_ref,
    gating_ref,
    update_ref,
):
    rows, cols, width = own_ref.shape
    sub = lax.axis_index("sub")
    own = flat_normed(own_ref[...], norm_gain_ref, norm_bias_ref)
    other = flat_normed(other_ref[...], norm_gain_ref, norm_bias_ref)
    for values, half in ((own, sub), (other, 1 - sub)):
        left = gated(values, w_a_proj_ref[...], w_a_gate_ref[...])
        left_ref[pl.ds(half, 1)] = left.reshape(1, rows, cols, -1)
    gating = sigmoid(jnp.dot(own, w_gate_ref[...], preferred_element_type=jnp.float32))
    gating = gating.reshape(rows, cols, width)
    for place in range(span):
        part = gating[:, place * rows : (place + 1) * rows]
        gating_ref[place] = part.reshape(rows * rows, width)
    right = gated(flat_normed(block_ref[...], norm_gain_ref, norm_bias_ref), w_b_proj_ref[...], w_b_gate_ref[...])
    right = right.reshape(1, 2, rows, cols, -1)
    places = [place_of(routes[0], span)]
    update_ref[...] = finish(left_ref, right, places, gating_ref, out_gain_ref, out_bias_ref, w_out_ref)


def last_kernel(span, routes, *refs):
    block_refs = refs[: span - 1][::-1]
    (
        left_ref,
        gating_ref,
        first_ref,
        norm_gain_ref,
        norm_bias_ref,
        w_b_proj_ref,
        w_b_gate_ref,
        out_gain_ref,
        out_bias_ref,
        w_out_ref,
        update_ref,
        placed_ref,
    ) = refs[span - 1 :]
    _, rows, cols, width = block_refs[0].shape
    right = jnp.stack([ref[...] for ref in block_refs])
    right = gated(flat_normed(right, norm_gain_ref, norm_bias_ref), w_b_proj_ref[...], w_b_gate_ref[...])
    right = right.reshape(span - 1, 2, rows, cols, -1)
    places = [place_of(sources, span) for sources in routes]
    last = finish(left_ref, right, places[1:], gating_ref, out_gain_ref, out_bias_ref, w_out_ref)
    placed_ref[pl.ds(places[0][0], 1)] = first_ref[...]
    for step in range(span - 1):
        placed_ref[pl.ds(places[step + 1][0], 1)] = last[step : step + 1]
    for row in range(rows):
        parts = [placed_ref[place, row * rows : (row + 1) * rows] for place in range(span)]
        update_ref[row] = jnp.concatenate(parts, axis=0).astype(jnp.bfloat16)


def gather_span(
    routes,
    pair_rep,
    norm_gain,
    norm_bias,
    w_a_proj,
    w_a_gate,
    w_b_proj,
    w_b_gate,
    w_gate,
    out_gain,
    out_bias,
    w_out,
):
    span = len(routes)
    block = pair_rep.shape
    rows, _, width = block
    params = pltpu.CompilerParams(vmem_limit_bytes=KERNEL_BYTES)
    cost = pl.CostEstimate(flops=10**8, bytes_accessed=10**6, transcendentals=0)

    def receive(values, sources):
        pairs = [(source, device) for device, source in enumerate(sources)]
        return lax.ppermute(values, ("row", "sub"), pairs)

    other = receive(pair_rep, [device ^ 1 for device in range(4 * span)])
    own = pl.pallas_call(
        copy_kernel,
        out_shape=jax.ShapeDtypeStruct(block, pair_rep.dtype),
        cost_estimate=cost,
        compiler_params=params,
    )(pair_rep)
    pair = jnp.stack([own, other])
    blocks = [receive(pair, sources) for sources in routes]
    norm = (norm_gain[None], norm_bias[None])
    out = (out_gain[None], out_bias[None], w_out)
    left, gating, update = pl.pallas_call(
        functools.partial(first_kernel, span, routes),
        out_shape=(
            jax.ShapeDtypeStruct((2,) + block, jnp.float32),
            jax.ShapeDtypeStruct((span, rows * rows, width), jnp.float32),
            jax.ShapeDtypeStruct((1, rows * rows, width), jnp.float32),
        ),
        cost_estimate=cost,
        compiler_params=params,
    )(own, other, blocks[0], *norm, w_a_proj, w_a_gate, w_b_proj, w_b_gate, w_gate, *out)
    return pl.pallas_call(
        functools.partial(last_kernel, span, routes),
        out_shape=jax.ShapeDtypeStruct(block, pair_rep.dtype),
        scratch_shapes=[pltpu.VMEM((span, rows * rows, width), jnp.float32)],
        compiler_params=params,
    )(*blocks[:0:-1], left, gating, update, *norm, w_b_proj, w_b_gate, *out)


def exchange_channels(
    pair_rep,
    norm_gain,
    norm_bias,
    w_a_proj,
    w_a_gate,
    w_b_proj,
    w_b_gate,
    w_gate,
    out_gain,
    out_bias,
    w_out,
):
    hidden = w_a_proj.shape[1]
    w_inner = jnp.concatenate([w_a_proj, w_a_gate, w_b_proj, w_b_gate], axis=1)
    normed = layer_norm(pair_rep.astype(jnp.float32), norm_gain, norm_bias, -1).astype(jnp.bfloat16)
    inner = jnp.einsum("rkc,cm->mrk", normed, w_inner, preferred_element_type=jnp.float32)
    left_local = (jax.nn.sigmoid(inner[hidden : 2 * hidden]) * inner[:hidden]).astype(jnp.bfloat16)
    right_local = (
        jax.nn.sigmoid(inner[3 * hidden : 4 * hidden]) * inner[2 * hidden : 3 * hidden]
    ).astype(jnp.bfloat16)
    gating = jax.nn.sigmoid(
        jnp.einsum("rkc,cd->rkd", normed, w_gate, preferred_element_type=jnp.float32)
    ).astype(jnp.bfloat16)
    left_chan, right_chan = (
        lax.all_to_all(left_local, "row", split_axis=0, concat_axis=1, tiled=True),
        lax.all_to_all(right_local, "row", split_axis=0, concat_axis=1, tiled=True),
    )
    left_rows = lax.all_to_all(left_chan, "sub", split_axis=1, concat_axis=2, tiled=True)
    triangle = jnp.einsum(
        "hik,hjk->hij",
        left_rows,
        lax.all_gather(right_chan, "sub", axis=2, tiled=True),
        preferred_element_type=jnp.float32,
    ).astype(jnp.bfloat16)
    regrouped = lax.all_to_all(
        lax.all_to_all(triangle, "sub", split_axis=2, concat_axis=1, tiled=True),
        "row",
        split_axis=1,
        concat_axis=0,
        tiled=True,
    )
    hidden_normed = layer_norm(
        regrouped.astype(jnp.float32), out_gain[:, None, None], out_bias[:, None, None], 0
    ).astype(jnp.bfloat16)
    mixed = jnp.einsum("hrj,hc->rjc", hidden_normed, w_out, preferred_element_type=jnp.float32)
    return (gating.astype(jnp.float32) * mixed).astype(jnp.bfloat16)


def solution(mesh):
    n_row, n_sub = mesh.shape["row"], mesh.shape["sub"]

    def per_device(pair_rep, *weights):
        rows, cols, _ = pair_rep.shape
        gathered = n_row * n_sub * pair_rep.size * pair_rep.dtype.itemsize
        routed = (n_row, n_sub) == (8, 2) and cols == n_row // 2 * rows
        if routed and gathered <= GATHER_BYTES:
            return gather_span(ROUTES, pair_rep, *weights)
        return exchange_channels(pair_rep, *weights)

    in_specs = (P(("grp", "row"), "sub", None), P(), P(), P(), P(), P(), P(), P(), P(), P(), P())
    out_specs = P(("grp", "row"), "sub", None)
    return jax.shard_map(
        per_device, mesh=mesh, in_specs=in_specs, out_specs=out_specs, check_vma=False
    )
```

```python
import functools

import jax
import jax.numpy as jnp
from jax import lax
from jax.experimental import pallas as pl
from jax.experimental.pallas import tpu as pltpu
from jax.sharding import PartitionSpec as P

EPSILON = 1e-05
GATHER_BYTES = 2 * 1024 * 1024
KERNEL_BYTES = 4 * 1024 * 1024
ROUTES = (
    (3, 14, 4, 9, 5, 11, 0, 8, 1, 10, 7, 15, 2, 12, 6, 13),
    (6, 13, 3, 12, 1, 15, 7, 11, 5, 8, 4, 10, 0, 9, 2, 14),
    (5, 11, 7, 15, 3, 9, 4, 13, 2, 14, 1, 12, 6, 10, 0, 8),
    (1, 9, 0, 11, 7, 13, 2, 15, 6, 12, 3, 8, 4, 14, 5, 10),
)


def layer_norm(values, gain, shift, axis):
    centred = values - jnp.mean(values, axis=axis, keepdims=True)
    variance = jnp.mean(centred * centred, axis=axis, keepdims=True)
    return centred * lax.rsqrt(variance + EPSILON) * gain + shift


def sigmoid(values):
    return 0.5 * jnp.tanh(0.5 * values) + 0.5


def gated(rows, w_proj, w_gate):
    proj = jnp.dot(rows, w_proj, preferred_element_type=jnp.float32)
    gate = jnp.dot(rows, w_gate, preferred_element_type=jnp.float32)
    return sigmoid(gate) * proj


def lookup(values, bits):
    word = sum(value << (bits * place) for place, value in enumerate(values))
    word = jnp.int32(word - (1 << 32) if word >> 31 else word)
    device = lax.axis_index("row") * 2 + lax.axis_index("sub")
    return lax.shift_right_logical(word, device * bits) & ((1 << bits) - 1)


def place_of(sources, span):
    place = lookup([source // 2 % span for source in sources], 2)
    return place, lookup([source % 2 for source in sources], 1)


def copy_kernel(source_ref, target_ref):
    target_ref[...] = source_ref[...]


def flat_normed(values, gain_ref, bias_ref):
    flat = values.reshape(-1, values.shape[-1]).astype(jnp.float32)
    return layer_norm(flat, gain_ref[...], bias_ref[...], -1).astype(jnp.bfloat16)


def first_kernel(
    own_ref,
    other_ref,
    norm_gain_ref,
    norm_bias_ref,
    w_a_proj_ref,
    w_a_gate_ref,
    w_gate_ref,
    w_b_proj_ref,
    w_b_gate_ref,
    out_gain_ref,
    out_bias_ref,
    w_out_ref,
    left_ref,
    gating_ref,
):
    rows, cols, _ = own_ref.shape
    sub = lax.axis_index("sub")
    own = flat_normed(own_ref[...], norm_gain_ref, norm_bias_ref)
    other = flat_normed(other_ref[...], norm_gain_ref, norm_bias_ref)
    for values, half in ((own, sub), (other, 1 - sub)):
        left = gated(values, w_a_proj_ref[...], w_a_gate_ref[...])
        left_ref[pl.ds(half, 1)] = left.reshape(1, rows, cols, -1)
    gating_ref[...] = sigmoid(jnp.dot(own, w_gate_ref[...], preferred_element_type=jnp.float32))


def last_kernel(span, routes, *refs):
    block_refs = refs[:span][::-1]
    (
        left_ref,
        gating_ref,
        norm_gain_ref,
        norm_bias_ref,
        w_b_proj_ref,
        w_b_gate_ref,
        out_gain_ref,
        out_bias_ref,
        w_out_ref,
        update_ref,
        placed_ref,
    ) = refs[span:]
    _, rows, cols, _ = block_refs[0].shape
    for sources, ref in zip(routes, block_refs):
        place, half = place_of(sources, span)
        placed_ref[pl.ds(half, 1), pl.ds(place, 1)] = ref[0:1][None]
        placed_ref[pl.ds(1 - half, 1), pl.ds(place, 1)] = ref[1:2][None]
    right = flat_normed(placed_ref[...], norm_gain_ref, norm_bias_ref)
    right = gated(right, w_b_proj_ref[...], w_b_gate_ref[...]).reshape(2, span * rows, cols, -1)
    sums = []
    for row in range(rows):
        products = right[0] * left_ref[0, row] + right[1] * left_ref[1, row]
        sums.append(jnp.sum(products, axis=1))
    triangle = jnp.concatenate(sums, axis=0)
    hidden_normed = layer_norm(triangle, out_gain_ref[...], out_bias_ref[...], -1)
    mixed = jnp.dot(
        hidden_normed.astype(jnp.bfloat16), w_out_ref[...], preferred_element_type=jnp.float32
    )
    update_ref[...] = (gating_ref[...] * mixed).astype(jnp.bfloat16).reshape(update_ref.shape)


def gather_span(
    routes,
    pair_rep,
    norm_gain,
    norm_bias,
    w_a_proj,
    w_a_gate,
    w_b_proj,
    w_b_gate,
    w_gate,
    out_gain,
    out_bias,
    w_out,
):
    span = len(routes)
    block = pair_rep.shape
    rows, cols, width = block
    params = pltpu.CompilerParams(vmem_limit_bytes=KERNEL_BYTES)
    cost = pl.CostEstimate(flops=10**8, bytes_accessed=10**6, transcendentals=0)

    def receive(values, sources):
        pairs = [(source, device) for device, source in enumerate(sources)]
        return lax.ppermute(values, ("row", "sub"), pairs)

    other = receive(pair_rep, [device ^ 1 for device in range(4 * span)])
    own = pl.pallas_call(
        copy_kernel,
        out_shape=jax.ShapeDtypeStruct(block, pair_rep.dtype),
        cost_estimate=cost,
        compiler_params=params,
    )(pair_rep)
    pair = jnp.stack([own, other])
    blocks = [receive(pair, sources) for sources in routes]
    norm = (norm_gain[None], norm_bias[None])
    tail = (w_b_proj, w_b_gate, out_gain[None], out_bias[None], w_out)
    left, gating = pl.pallas_call(
        first_kernel,
        out_shape=(
            jax.ShapeDtypeStruct((2,) + block, jnp.float32),
            jax.ShapeDtypeStruct((rows * cols, width), jnp.float32),
        ),
        cost_estimate=cost,
        compiler_params=params,
    )(own, other, *norm, w_a_proj, w_a_gate, w_gate, *tail)
    return pl.pallas_call(
        functools.partial(last_kernel, span, routes),
        out_shape=jax.ShapeDtypeStruct(block, pair_rep.dtype),
        scratch_shapes=[pltpu.VMEM((2, span) + block, pair_rep.dtype)],
        compiler_params=params,
    )(*blocks[::-1], left, gating, *norm, *tail)


def exchange_channels(
    pair_rep,
    norm_gain,
    norm_bias,
    w_a_proj,
    w_a_gate,
    w_b_proj,
    w_b_gate,
    w_gate,
    out_gain,
    out_bias,
    w_out,
):
    hidden = w_a_proj.shape[1]
    w_inner = jnp.concatenate([w_a_proj, w_a_gate, w_b_proj, w_b_gate], axis=1)
    normed = layer_norm(pair_rep.astype(jnp.float32), norm_gain, norm_bias, -1).astype(jnp.bfloat16)
    inner = jnp.einsum("rkc,cm->mrk", normed, w_inner, preferred_element_type=jnp.float32)
    left_local = (jax.nn.sigmoid(inner[hidden : 2 * hidden]) * inner[:hidden]).astype(jnp.bfloat16)
    right_local = (
        jax.nn.sigmoid(inner[3 * hidden : 4 * hidden]) * inner[2 * hidden : 3 * hidden]
    ).astype(jnp.bfloat16)
    gating = jax.nn.sigmoid(
        jnp.einsum("rkc,cd->rkd", normed, w_gate, preferred_element_type=jnp.float32)
    ).astype(jnp.bfloat16)
    left_chan, right_chan = (
        lax.all_to_all(left_local, "row", split_axis=0, concat_axis=1, tiled=True),
        lax.all_to_all(right_local, "row", split_axis=0, concat_axis=1, tiled=True),
    )
    left_rows = lax.all_to_all(left_chan, "sub", split_axis=1, concat_axis=2, tiled=True)
    triangle = jnp.einsum(
        "hik,hjk->hij",
        left_rows,
        lax.all_gather(right_chan, "sub", axis=2, tiled=True),
        preferred_element_type=jnp.float32,
    ).astype(jnp.bfloat16)
    regrouped = lax.all_to_all(
        lax.all_to_all(triangle, "sub", split_axis=2, concat_axis=1, tiled=True),
        "row",
        split_axis=1,
        concat_axis=0,
        tiled=True,
    )
    hidden_normed = layer_norm(
        regrouped.astype(jnp.float32), out_gain[:, None, None], out_bias[:, None, None], 0
    ).astype(jnp.bfloat16)
    mixed = jnp.einsum("hrj,hc->rjc", hidden_normed, w_out, preferred_element_type=jnp.float32)
    return (gating.astype(jnp.float32) * mixed).astype(jnp.bfloat16)


def solution(mesh):
    n_row, n_sub = mesh.shape["row"], mesh.shape["sub"]

    def per_device(pair_rep, *weights):
        rows, cols, _ = pair_rep.shape
        gathered = n_row * n_sub * pair_rep.size * pair_rep.dtype.itemsize
        routed = (n_row, n_sub) == (8, 2) and cols == n_row // 2 * rows
        if routed and gathered <= GATHER_BYTES:
            return gather_span(ROUTES, pair_rep, *weights)
        return exchange_channels(pair_rep, *weights)

    in_specs = (P(("grp", "row"), "sub", None), P(), P(), P(), P(), P(), P(), P(), P(), P(), P())
    out_specs = P(("grp", "row"), "sub", None)
    return jax.shard_map(
        per_device, mesh=mesh, in_specs=in_specs, out_specs=out_specs, check_vma=False
    )
```

```python
import functools

import jax
import jax.numpy as jnp
from jax import lax
from jax.experimental import pallas as pl
from jax.experimental.pallas import tpu as pltpu
from jax.sharding import PartitionSpec as P

EPSILON = 1e-05
GATHER_BYTES = 2 * 1024 * 1024
KERNEL_BYTES = 4 * 1024 * 1024
ROUTES = (
    (
        (6, 14, 0, 8, 3, 13, 7, 15, 1, 12, 4, 10, 2, 11, 5, 9),
        (4, 11, 6, 13, 5, 15, 1, 8, 3, 10, 0, 9, 7, 12, 2, 14),
        (3, 12, 5, 15, 7, 11, 2, 10, 4, 8, 6, 14, 1, 9, 0, 13),
        (1, 9, 3, 11, 0, 8, 5, 12, 7, 14, 2, 13, 4, 15, 6, 10),
    ),
    (
        (4, 10, 1, 14, 5, 15, 0, 13, 3, 8, 2, 9, 7, 12, 6, 11),
        (6, 13, 5, 9, 3, 12, 7, 11, 1, 15, 0, 10, 2, 8, 4, 14),
        (1, 15, 3, 13, 6, 11, 5, 9, 7, 10, 4, 12, 0, 14, 2, 8),
        (3, 9, 6, 11, 0, 8, 2, 15, 4, 12, 7, 14, 5, 10, 1, 13),
    ),
)


def layer_norm(values, gain, shift, axis):
    centred = values - jnp.mean(values, axis=axis, keepdims=True)
    variance = jnp.mean(centred * centred, axis=axis, keepdims=True)
    return centred * lax.rsqrt(variance + EPSILON) * gain + shift


def sigmoid(values):
    return 0.5 * jnp.tanh(0.5 * values) + 0.5


def gated(rows, w_proj, w_gate):
    both = jnp.concatenate([w_proj, w_gate], axis=1)
    both = jnp.dot(rows, both, preferred_element_type=jnp.float32)
    return sigmoid(both[:, w_proj.shape[1] :]) * both[:, : w_proj.shape[1]]


def lookup(tables, bits):
    words = []
    for values in tables:
        word = sum(value << (bits * place) for place, value in enumerate(values))
        words.append(jnp.int32(word - (1 << 32) if word >> 31 else word))
    word = jnp.where(lax.axis_index("grp") == 0, *words)
    device = lax.axis_index("row") * 2 + lax.axis_index("sub")
    return lax.shift_right_logical(word, device * bits) & ((1 << bits) - 1)


def place_of(sources, span):
    place = lookup([[source // 2 % span for source in table] for table in sources], 2)
    return place, lookup([[source % 2 for source in table] for table in sources], 1)


def copy_kernel(source_ref, target_ref):
    target_ref[...] = source_ref[...]


def flat_normed(values, gain_ref, bias_ref):
    width = values.shape[-1]
    flat = values.reshape(-1, width)
    share = jnp.full((width, width), 1 / width, jnp.bfloat16)
    centred = flat.astype(jnp.float32) - jnp.dot(flat, share, preferred_element_type=jnp.float32)
    variance = jnp.mean(centred * centred, axis=-1, keepdims=True)
    normed = centred * lax.rsqrt(variance + EPSILON) * gain_ref[...] + bias_ref[...]
    return normed.astype(jnp.bfloat16)


def first_kernel(
    own_ref,
    other_ref,
    norm_gain_ref,
    norm_bias_ref,
    w_a_proj_ref,
    w_a_gate_ref,
    w_gate_ref,
    w_b_proj_ref,
    w_b_gate_ref,
    out_gain_ref,
    out_bias_ref,
    w_out_ref,
    left_ref,
    gating_ref,
):
    rows, cols, _ = own_ref.shape
    sub = lax.axis_index("sub")
    own = flat_normed(own_ref[...], norm_gain_ref, norm_bias_ref)
    other = flat_normed(other_ref[...], norm_gain_ref, norm_bias_ref)
    for values, half in ((own, sub), (other, 1 - sub)):
        left = gated(values, w_a_proj_ref[...], w_a_gate_ref[...])
        left_ref[pl.ds(half, 1)] = left.reshape(1, rows, cols, -1)
    gating_ref[...] = sigmoid(jnp.dot(own, w_gate_ref[...], preferred_element_type=jnp.float32))


def last_kernel(span, routes, *refs):
    block_refs = refs[:span][::-1]
    (
        left_ref,
        gating_ref,
        norm_gain_ref,
        norm_bias_ref,
        w_b_proj_ref,
        w_b_gate_ref,
        out_gain_ref,
        out_bias_ref,
        w_out_ref,
        update_ref,
        placed_ref,
    ) = refs[span:]
    _, rows, cols, _ = block_refs[0].shape
    for sources, ref in zip(zip(*routes), block_refs):
        place, half = place_of(sources, span)
        placed_ref[pl.ds(half, 1), pl.ds(place, 1)] = ref[0:1][None]
        placed_ref[pl.ds(1 - half, 1), pl.ds(place, 1)] = ref[1:2][None]
    right = flat_normed(placed_ref[...], norm_gain_ref, norm_bias_ref)
    right = gated(right, w_b_proj_ref[...], w_b_gate_ref[...]).reshape(2, span * rows, cols, -1)
    sums = []
    for row in range(rows):
        products = right[0] * left_ref[0, row] + right[1] * left_ref[1, row]
        sums.append(jnp.sum(products, axis=1))
    triangle = jnp.concatenate(sums, axis=0)
    hidden_normed = layer_norm(triangle, out_gain_ref[...], out_bias_ref[...], -1)
    mixed = jnp.dot(
        hidden_normed.astype(jnp.bfloat16), w_out_ref[...], preferred_element_type=jnp.float32
    )
    update_ref[...] = (gating_ref[...] * mixed).astype(jnp.bfloat16).reshape(update_ref.shape)


def gather_span(
    routes,
    pair_rep,
    norm_gain,
    norm_bias,
    w_a_proj,
    w_a_gate,
    w_b_proj,
    w_b_gate,
    w_gate,
    out_gain,
    out_bias,
    w_out,
):
    span = len(routes[0])
    block = pair_rep.shape
    rows, cols, width = block
    params = pltpu.CompilerParams(vmem_limit_bytes=KERNEL_BYTES)
    cost = pl.CostEstimate(flops=10**8, bytes_accessed=10**6, transcendentals=0)

    def receive(values, sources):
        devices = 4 * span
        pairs = [
            (group * devices + source, group * devices + device)
            for group, table in enumerate(sources)
            for device, source in enumerate(table)
        ]
        return lax.ppermute(values, ("grp", "row", "sub"), pairs)

    swap = [device ^ 1 for device in range(4 * span)]
    other = receive(pair_rep, [swap] * len(routes))
    own = pl.pallas_call(
        copy_kernel,
        out_shape=jax.ShapeDtypeStruct(block, pair_rep.dtype),
        cost_estimate=cost,
        compiler_params=params,
    )(pair_rep)
    pair = jnp.stack([own, other])
    blocks = [receive(pair, sources) for sources in zip(*routes)]
    norm = (norm_gain[None], norm_bias[None])
    tail = (w_b_proj, w_b_gate, out_gain[None], out_bias[None], w_out)
    left, gating = pl.pallas_call(
        first_kernel,
        out_shape=(
            jax.ShapeDtypeStruct((2,) + block, jnp.float32),
            jax.ShapeDtypeStruct((rows * cols, width), jnp.float32),
        ),
        cost_estimate=cost,
        compiler_params=params,
    )(own, other, *norm, w_a_proj, w_a_gate, w_gate, *tail)
    return pl.pallas_call(
        functools.partial(last_kernel, span, routes),
        out_shape=jax.ShapeDtypeStruct(block, pair_rep.dtype),
        scratch_shapes=[pltpu.VMEM((2, span) + block, pair_rep.dtype)],
        compiler_params=params,
    )(*blocks[::-1], left, gating, *norm, *tail)


def exchange_channels(
    pair_rep,
    norm_gain,
    norm_bias,
    w_a_proj,
    w_a_gate,
    w_b_proj,
    w_b_gate,
    w_gate,
    out_gain,
    out_bias,
    w_out,
):
    hidden = w_a_proj.shape[1]
    w_inner = jnp.concatenate([w_a_proj, w_a_gate, w_b_proj, w_b_gate], axis=1)
    normed = layer_norm(pair_rep.astype(jnp.float32), norm_gain, norm_bias, -1).astype(jnp.bfloat16)
    inner = jnp.einsum("rkc,cm->mrk", normed, w_inner, preferred_element_type=jnp.float32)
    left_local = (jax.nn.sigmoid(inner[hidden : 2 * hidden]) * inner[:hidden]).astype(jnp.bfloat16)
    right_local = (
        jax.nn.sigmoid(inner[3 * hidden : 4 * hidden]) * inner[2 * hidden : 3 * hidden]
    ).astype(jnp.bfloat16)
    gating = jax.nn.sigmoid(
        jnp.einsum("rkc,cd->rkd", normed, w_gate, preferred_element_type=jnp.float32)
    ).astype(jnp.bfloat16)
    left_chan, right_chan = (
        lax.all_to_all(left_local, "row", split_axis=0, concat_axis=1, tiled=True),
        lax.all_to_all(right_local, "row", split_axis=0, concat_axis=1, tiled=True),
    )
    left_rows = lax.all_to_all(left_chan, "sub", split_axis=1, concat_axis=2, tiled=True)
    triangle = jnp.einsum(
        "hik,hjk->hij",
        left_rows,
        lax.all_gather(right_chan, "sub", axis=2, tiled=True),
        preferred_element_type=jnp.float32,
    ).astype(jnp.bfloat16)
    regrouped = lax.all_to_all(
        lax.all_to_all(triangle, "sub", split_axis=2, concat_axis=1, tiled=True),
        "row",
        split_axis=1,
        concat_axis=0,
        tiled=True,
    )
    hidden_normed = layer_norm(
        regrouped.astype(jnp.float32), out_gain[:, None, None], out_bias[:, None, None], 0
    ).astype(jnp.bfloat16)
    mixed = jnp.einsum("hrj,hc->rjc", hidden_normed, w_out, preferred_element_type=jnp.float32)
    return (gating.astype(jnp.float32) * mixed).astype(jnp.bfloat16)


def solution(mesh):
    n_row, n_sub = mesh.shape["row"], mesh.shape["sub"]

    def per_device(pair_rep, *weights):
        rows, cols, _ = pair_rep.shape
        gathered = n_row * n_sub * pair_rep.size * pair_rep.dtype.itemsize
        routed = (mesh.shape["grp"], n_row, n_sub) == (2, 8, 2) and cols == n_row // 2 * rows
        if routed and gathered <= GATHER_BYTES:
            return gather_span(ROUTES, pair_rep, *weights)
        return exchange_channels(pair_rep, *weights)

    in_specs = (P(("grp", "row"), "sub", None), P(), P(), P(), P(), P(), P(), P(), P(), P(), P())
    out_specs = P(("grp", "row"), "sub", None)
    return jax.shard_map(
        per_device, mesh=mesh, in_specs=in_specs, out_specs=out_specs, check_vma=False
    )
```

```python
import functools

import jax
import jax.numpy as jnp
from jax import lax
from jax.experimental import pallas as pl
from jax.experimental.pallas import tpu as pltpu
from jax.sharding import PartitionSpec as P

EPSILON = 1e-05
GATHER_BYTES = 2 * 1024 * 1024
KERNEL_BYTES = 4 * 1024 * 1024
ROUTES = (
    (
        (4, 11, 1, 9, 3, 8, 0, 14, 2, 10, 6, 15, 5, 12, 7, 13),
        (7, 15, 3, 13, 1, 11, 2, 9, 0, 12, 5, 10, 6, 8, 4, 14),
        (2, 12, 6, 14, 5, 15, 4, 13, 7, 8, 1, 9, 3, 11, 0, 10),
        (1, 9, 5, 11, 6, 13, 7, 10, 4, 15, 2, 12, 0, 14, 3, 8),
    ),
    (
        (6, 15, 4, 13, 1, 11, 5, 8, 3, 12, 7, 10, 0, 9, 2, 14),
        (5, 13, 6, 9, 3, 15, 1, 12, 7, 10, 0, 8, 2, 14, 4, 11),
        (2, 11, 3, 15, 6, 13, 7, 14, 1, 8, 5, 12, 4, 10, 0, 9),
        (1, 9, 0, 11, 5, 8, 3, 10, 4, 15, 2, 14, 7, 12, 6, 13),
    ),
)


def layer_norm(values, gain, shift, axis):
    centred = values - jnp.mean(values, axis=axis, keepdims=True)
    variance = jnp.mean(centred * centred, axis=axis, keepdims=True)
    return centred * lax.rsqrt(variance + EPSILON) * gain + shift


def sigmoid(values):
    return 0.5 * jnp.tanh(0.5 * values) + 0.5


def gated(rows, w_proj, w_gate):
    both = jnp.concatenate([w_proj, w_gate], axis=1)
    both = jnp.dot(rows, both, preferred_element_type=jnp.float32)
    return sigmoid(both[:, w_proj.shape[1] :]) * both[:, : w_proj.shape[1]]


def lookup(tables, bits):
    words = []
    for values in tables:
        word = sum(value << (bits * place) for place, value in enumerate(values))
        words.append(jnp.int32(word - (1 << 32) if word >> 31 else word))
    word = jnp.where(lax.axis_index("grp") == 0, *words)
    device = lax.axis_index("row") * 2 + lax.axis_index("sub")
    return lax.shift_right_logical(word, device * bits) & ((1 << bits) - 1)


def place_of(sources, span):
    place = lookup([[source // 2 % span for source in table] for table in sources], 2)
    return place, lookup([[source % 2 for source in table] for table in sources], 1)


def copy_kernel(source_ref, target_ref):
    target_ref[...] = source_ref[...]


def flat_normed(values, gain_ref, bias_ref):
    flat = values.reshape(-1, values.shape[-1]).astype(jnp.float32)
    return layer_norm(flat, gain_ref[...], bias_ref[...], -1).astype(jnp.bfloat16)


def first_kernel(
    own_ref,
    other_ref,
    norm_gain_ref,
    norm_bias_ref,
    w_a_proj_ref,
    w_a_gate_ref,
    w_gate_ref,
    w_b_proj_ref,
    w_b_gate_ref,
    out_gain_ref,
    out_bias_ref,
    w_out_ref,
    left_ref,
    gating_ref,
):
    rows, cols, _ = own_ref.shape
    sub = lax.axis_index("sub")
    own = flat_normed(own_ref[...], norm_gain_ref, norm_bias_ref)
    other = flat_normed(other_ref[...], norm_gain_ref, norm_bias_ref)
    for values, half in ((own, sub), (other, 1 - sub)):
        left = gated(values, w_a_proj_ref[...], w_a_gate_ref[...])
        left_ref[pl.ds(half, 1)] = left.reshape(1, rows, cols, -1)
    gating_ref[...] = sigmoid(jnp.dot(own, w_gate_ref[...], preferred_element_type=jnp.float32))


def last_kernel(span, routes, *refs):
    block_refs = refs[:span][::-1]
    (
        left_ref,
        gating_ref,
        norm_gain_ref,
        norm_bias_ref,
        w_b_proj_ref,
        w_b_gate_ref,
        out_gain_ref,
        out_bias_ref,
        w_out_ref,
        update_ref,
        placed_ref,
    ) = refs[span:]
    _, rows, cols, _ = block_refs[0].shape
    for sources, ref in zip(zip(*routes), block_refs):
        place, half = place_of(sources, span)
        placed_ref[pl.ds(half, 1), pl.ds(place, 1)] = ref[0:1][None]
        placed_ref[pl.ds(1 - half, 1), pl.ds(place, 1)] = ref[1:2][None]
    right = flat_normed(placed_ref[...], norm_gain_ref, norm_bias_ref)
    right = gated(right, w_b_proj_ref[...], w_b_gate_ref[...]).reshape(2, span * rows, cols, -1)
    sums = []
    for row in range(rows):
        products = right[0] * left_ref[0, row] + right[1] * left_ref[1, row]
        sums.append(jnp.sum(products, axis=1))
    triangle = jnp.concatenate(sums, axis=0)
    hidden_normed = layer_norm(triangle, out_gain_ref[...], out_bias_ref[...], -1)
    mixed = jnp.dot(
        hidden_normed.astype(jnp.bfloat16), w_out_ref[...], preferred_element_type=jnp.float32
    )
    update_ref[...] = (gating_ref[...] * mixed).astype(jnp.bfloat16).reshape(update_ref.shape)


def gather_span(
    routes,
    pair_rep,
    norm_gain,
    norm_bias,
    w_a_proj,
    w_a_gate,
    w_b_proj,
    w_b_gate,
    w_gate,
    out_gain,
    out_bias,
    w_out,
):
    span = len(routes[0])
    block = pair_rep.shape
    rows, cols, width = block
    params = pltpu.CompilerParams(vmem_limit_bytes=KERNEL_BYTES)
    cost = pl.CostEstimate(flops=10**8, bytes_accessed=10**6, transcendentals=0)

    def receive(values, sources):
        devices = 4 * span
        pairs = [
            (group * devices + source, group * devices + device)
            for group, table in enumerate(sources)
            for device, source in enumerate(table)
        ]
        return lax.ppermute(values, ("grp", "row", "sub"), pairs)

    swap = [device ^ 1 for device in range(4 * span)]
    other = receive(pair_rep, [swap] * len(routes))
    own = pl.pallas_call(
        copy_kernel,
        out_shape=jax.ShapeDtypeStruct(block, pair_rep.dtype),
        cost_estimate=cost,
        compiler_params=params,
    )(pair_rep)
    pair = jnp.stack([own, other])
    blocks = [receive(pair, sources) for sources in zip(*routes)]
    norm = (norm_gain[None], norm_bias[None])
    tail = (w_b_proj, w_b_gate, out_gain[None], out_bias[None], w_out)
    left, gating = pl.pallas_call(
        first_kernel,
        out_shape=(
            jax.ShapeDtypeStruct((2,) + block, jnp.float32),
            jax.ShapeDtypeStruct((rows * cols, width), jnp.float32),
        ),
        cost_estimate=cost,
        compiler_params=params,
    )(own, other, *norm, w_a_proj, w_a_gate, w_gate, *tail)
    return pl.pallas_call(
        functools.partial(last_kernel, span, routes),
        out_shape=jax.ShapeDtypeStruct(block, pair_rep.dtype),
        scratch_shapes=[pltpu.VMEM((2, span) + block, pair_rep.dtype)],
        compiler_params=params,
    )(*blocks[::-1], left, gating, *norm, *tail)


def exchange_channels(
    pair_rep,
    norm_gain,
    norm_bias,
    w_a_proj,
    w_a_gate,
    w_b_proj,
    w_b_gate,
    w_gate,
    out_gain,
    out_bias,
    w_out,
):
    hidden = w_a_proj.shape[1]
    w_inner = jnp.concatenate([w_a_proj, w_a_gate, w_b_proj, w_b_gate], axis=1)
    normed = layer_norm(pair_rep.astype(jnp.float32), norm_gain, norm_bias, -1).astype(jnp.bfloat16)
    inner = jnp.einsum("rkc,cm->mrk", normed, w_inner, preferred_element_type=jnp.float32)
    left_local = (jax.nn.sigmoid(inner[hidden : 2 * hidden]) * inner[:hidden]).astype(jnp.bfloat16)
    right_local = (
        jax.nn.sigmoid(inner[3 * hidden : 4 * hidden]) * inner[2 * hidden : 3 * hidden]
    ).astype(jnp.bfloat16)
    gating = jax.nn.sigmoid(
        jnp.einsum("rkc,cd->rkd", normed, w_gate, preferred_element_type=jnp.float32)
    ).astype(jnp.bfloat16)
    left_chan, right_chan = (
        lax.all_to_all(left_local, "row", split_axis=0, concat_axis=1, tiled=True),
        lax.all_to_all(right_local, "row", split_axis=0, concat_axis=1, tiled=True),
    )
    left_rows = lax.all_to_all(left_chan, "sub", split_axis=1, concat_axis=2, tiled=True)
    triangle = jnp.einsum(
        "hik,hjk->hij",
        left_rows,
        lax.all_gather(right_chan, "sub", axis=2, tiled=True),
        preferred_element_type=jnp.float32,
    ).astype(jnp.bfloat16)
    regrouped = lax.all_to_all(
        lax.all_to_all(triangle, "sub", split_axis=2, concat_axis=1, tiled=True),
        "row",
        split_axis=1,
        concat_axis=0,
        tiled=True,
    )
    hidden_normed = layer_norm(
        regrouped.astype(jnp.float32), out_gain[:, None, None], out_bias[:, None, None], 0
    ).astype(jnp.bfloat16)
    mixed = jnp.einsum("hrj,hc->rjc", hidden_normed, w_out, preferred_element_type=jnp.float32)
    return (gating.astype(jnp.float32) * mixed).astype(jnp.bfloat16)


def solution(mesh):
    n_row, n_sub = mesh.shape["row"], mesh.shape["sub"]

    def per_device(pair_rep, *weights):
        rows, cols, _ = pair_rep.shape
        gathered = n_row * n_sub * pair_rep.size * pair_rep.dtype.itemsize
        routed = (mesh.shape["grp"], n_row, n_sub) == (2, 8, 2) and cols == n_row // 2 * rows
        if routed and gathered <= GATHER_BYTES:
            return gather_span(ROUTES, pair_rep, *weights)
        return exchange_channels(pair_rep, *weights)

    in_specs = (P(("grp", "row"), "sub", None), P(), P(), P(), P(), P(), P(), P(), P(), P(), P())
    out_specs = P(("grp", "row"), "sub", None)
    return jax.shard_map(
        per_device, mesh=mesh, in_specs=in_specs, out_specs=out_specs, check_vma=False
    )
```

```python
import functools

import jax
import jax.numpy as jnp
from jax import lax
from jax.experimental import pallas as pl
from jax.experimental.pallas import tpu as pltpu
from jax.sharding import PartitionSpec as P

EPSILON = 1e-05
GATHER_BYTES = 2 * 1024 * 1024
KERNEL_BYTES = 4 * 1024 * 1024
FIRST = (14, 15, 9, 8, 10, 11, 13, 12, 4, 5, 6, 7, 1, 0, 2, 3)
ROUTES = (
    (2, 13, 7, 15, 0, 8, 1, 11, 3, 10, 4, 9, 5, 14, 6, 12),
    (7, 11, 4, 13, 3, 15, 2, 8, 0, 12, 1, 14, 6, 9, 5, 10),
    (5, 9, 1, 11, 6, 13, 4, 14, 7, 15, 3, 12, 2, 10, 0, 8),
)


def layer_norm(values, gain, shift, axis):
    centred = values - jnp.mean(values, axis=axis, keepdims=True)
    variance = jnp.mean(centred * centred, axis=axis, keepdims=True)
    return centred * lax.rsqrt(variance + EPSILON) * gain + shift


def sigmoid(values):
    return 0.5 * jnp.tanh(0.5 * values) + 0.5


def gated(rows, w_proj, w_gate):
    proj = jnp.dot(rows, w_proj, preferred_element_type=jnp.float32)
    gate = jnp.dot(rows, w_gate, preferred_element_type=jnp.float32)
    return sigmoid(gate) * proj


def lookup(values, bits):
    word = sum(value << (bits * place) for place, value in enumerate(values))
    word = jnp.int32(word - (1 << 32) if word >> 31 else word)
    device = lax.axis_index("row") * 2 + lax.axis_index("sub")
    return lax.shift_right_logical(word, device * bits) & ((1 << bits) - 1)


def place_of(sources, span):
    place = lookup([source // 2 % span for source in sources], 2)
    return place, lookup([source % 2 for source in sources], 1)


def copy_kernel(source_ref, target_ref):
    target_ref[...] = source_ref[...]


def flat_normed(values, gain_ref, bias_ref):
    flat = values.reshape(-1, values.shape[-1]).astype(jnp.float32)
    return layer_norm(flat, gain_ref[...], bias_ref[...], -1).astype(jnp.bfloat16)


def first_kernel(
    own_ref,
    other_ref,
    norm_gain_ref,
    norm_bias_ref,
    w_a_proj_ref,
    w_a_gate_ref,
    w_gate_ref,
    w_b_proj_ref,
    w_b_gate_ref,
    out_gain_ref,
    out_bias_ref,
    w_out_ref,
    left_ref,
    gating_ref,
):
    rows, cols, _ = own_ref.shape
    sub = lax.axis_index("sub")
    own = flat_normed(own_ref[...], norm_gain_ref, norm_bias_ref)
    other = flat_normed(other_ref[...], norm_gain_ref, norm_bias_ref)
    for values, half in ((own, sub), (other, 1 - sub)):
        left = gated(values, w_a_proj_ref[...], w_a_gate_ref[...])
        left_ref[pl.ds(half, 1)] = left.reshape(1, rows, cols, -1)
    gating_ref[...] = sigmoid(jnp.dot(own, w_gate_ref[...], preferred_element_type=jnp.float32))


def last_kernel(span, first, routes, *refs):
    block_refs, refs = refs[: span - 1][::-1], refs[span - 1 :]
    (
        own_ref,
        other_ref,
        near_ref,
        handed_ref,
        left_ref,
        gating_ref,
        norm_gain_ref,
        norm_bias_ref,
        w_b_proj_ref,
        w_b_gate_ref,
        out_gain_ref,
        out_bias_ref,
        w_out_ref,
        update_ref,
        placed_ref,
    ) = refs
    rows, cols, _ = own_ref.shape

    def put(place, half, values):
        placed_ref[pl.ds(half, 1), pl.ds(place, 1)] = values[None, None]

    row, sub = lax.axis_index("row"), lax.axis_index("sub")
    crossed = row // span != sub
    place, half = place_of(first, span)
    place, half = jnp.where(crossed, place, lax.rem(row, span)), jnp.where(crossed, half, sub)
    put(place, half, jnp.where(crossed, near_ref[...], own_ref[...]))
    put(place, 1 - half, jnp.where(crossed, handed_ref[...], other_ref[...]))
    for sources, ref in zip(routes, block_refs):
        place, half = place_of(sources, span)
        put(place, half, ref[0])
        put(place, 1 - half, ref[1])
    right = flat_normed(placed_ref[...], norm_gain_ref, norm_bias_ref)
    right = gated(right, w_b_proj_ref[...], w_b_gate_ref[...]).reshape(2, span * rows, cols, -1)
    sums = []
    for row in range(rows):
        products = right[0] * left_ref[0, row] + right[1] * left_ref[1, row]
        sums.append(jnp.sum(products, axis=1))
    triangle = jnp.concatenate(sums, axis=0)
    hidden_normed = layer_norm(triangle, out_gain_ref[...], out_bias_ref[...], -1)
    mixed = jnp.dot(
        hidden_normed.astype(jnp.bfloat16), w_out_ref[...], preferred_element_type=jnp.float32
    )
    update_ref[...] = (gating_ref[...] * mixed).astype(jnp.bfloat16).reshape(update_ref.shape)


def gather_span(
    first,
    routes,
    pair_rep,
    norm_gain,
    norm_bias,
    w_a_proj,
    w_a_gate,
    w_b_proj,
    w_b_gate,
    w_gate,
    out_gain,
    out_bias,
    w_out,
):
    span = len(routes) + 1
    block = pair_rep.shape
    rows, cols, width = block
    params = pltpu.CompilerParams(vmem_limit_bytes=KERNEL_BYTES)
    cost = pl.CostEstimate(flops=10**8, bytes_accessed=10**6, transcendentals=0)

    def receive(values, sources):
        pairs = [(source, device) for device, source in enumerate(sources)]
        return lax.ppermute(values, ("row", "sub"), pairs)

    swap = [device ^ 1 for device in range(4 * span)]
    near = receive(pair_rep, first)
    other = receive(pair_rep, swap)
    own = pl.pallas_call(
        copy_kernel,
        out_shape=jax.ShapeDtypeStruct(block, pair_rep.dtype),
        cost_estimate=cost,
        compiler_params=params,
    )(pair_rep)
    pair = jnp.stack([own, other])
    blocks = [receive(pair, sources) for sources in routes]
    handed = receive(near, swap)
    norm = (norm_gain[None], norm_bias[None])
    tail = (w_b_proj, w_b_gate, out_gain[None], out_bias[None], w_out)
    left, gating = pl.pallas_call(
        first_kernel,
        out_shape=(
            jax.ShapeDtypeStruct((2,) + block, jnp.float32),
            jax.ShapeDtypeStruct((rows * cols, width), jnp.float32),
        ),
        cost_estimate=cost,
        compiler_params=params,
    )(own, other, *norm, w_a_proj, w_a_gate, w_gate, *tail)
    return pl.pallas_call(
        functools.partial(last_kernel, span, first, routes),
        out_shape=jax.ShapeDtypeStruct(block, pair_rep.dtype),
        scratch_shapes=[pltpu.VMEM((2, span) + block, pair_rep.dtype)],
        compiler_params=params,
    )(*blocks[::-1], own, other, near, handed, left, gating, *norm, *tail)


def exchange_channels(
    pair_rep,
    norm_gain,
    norm_bias,
    w_a_proj,
    w_a_gate,
    w_b_proj,
    w_b_gate,
    w_gate,
    out_gain,
    out_bias,
    w_out,
):
    hidden = w_a_proj.shape[1]
    w_inner = jnp.concatenate([w_a_proj, w_a_gate, w_b_proj, w_b_gate], axis=1)
    normed = layer_norm(pair_rep.astype(jnp.float32), norm_gain, norm_bias, -1).astype(jnp.bfloat16)
    inner = jnp.einsum("rkc,cm->mrk", normed, w_inner, preferred_element_type=jnp.float32)
    left_local = (jax.nn.sigmoid(inner[hidden : 2 * hidden]) * inner[:hidden]).astype(jnp.bfloat16)
    right_local = (
        jax.nn.sigmoid(inner[3 * hidden : 4 * hidden]) * inner[2 * hidden : 3 * hidden]
    ).astype(jnp.bfloat16)
    gating = jax.nn.sigmoid(
        jnp.einsum("rkc,cd->rkd", normed, w_gate, preferred_element_type=jnp.float32)
    ).astype(jnp.bfloat16)
    left_chan, right_chan = (
        lax.all_to_all(left_local, "row", split_axis=0, concat_axis=1, tiled=True),
        lax.all_to_all(right_local, "row", split_axis=0, concat_axis=1, tiled=True),
    )
    left_rows = lax.all_to_all(left_chan, "sub", split_axis=1, concat_axis=2, tiled=True)
    triangle = jnp.einsum(
        "hik,hjk->hij",
        left_rows,
        lax.all_gather(right_chan, "sub", axis=2, tiled=True),
        preferred_element_type=jnp.float32,
    ).astype(jnp.bfloat16)
    regrouped = lax.all_to_all(
        lax.all_to_all(triangle, "sub", split_axis=2, concat_axis=1, tiled=True),
        "row",
        split_axis=1,
        concat_axis=0,
        tiled=True,
    )
    hidden_normed = layer_norm(
        regrouped.astype(jnp.float32), out_gain[:, None, None], out_bias[:, None, None], 0
    ).astype(jnp.bfloat16)
    mixed = jnp.einsum("hrj,hc->rjc", hidden_normed, w_out, preferred_element_type=jnp.float32)
    return (gating.astype(jnp.float32) * mixed).astype(jnp.bfloat16)


def solution(mesh):
    n_row, n_sub = mesh.shape["row"], mesh.shape["sub"]

    def per_device(pair_rep, *weights):
        rows, cols, _ = pair_rep.shape
        gathered = n_row * n_sub * pair_rep.size * pair_rep.dtype.itemsize
        routed = (n_row, n_sub) == (8, 2) and cols == n_row // 2 * rows
        if routed and gathered <= GATHER_BYTES:
            return gather_span(FIRST, ROUTES, pair_rep, *weights)
        return exchange_channels(pair_rep, *weights)

    in_specs = (P(("grp", "row"), "sub", None), P(), P(), P(), P(), P(), P(), P(), P(), P(), P())
    out_specs = P(("grp", "row"), "sub", None)
    return jax.shard_map(
        per_device, mesh=mesh, in_specs=in_specs, out_specs=out_specs, check_vma=False
    )
```

```python
import functools

import jax
import jax.numpy as jnp
from jax import lax
from jax.experimental import pallas as pl
from jax.experimental.pallas import tpu as pltpu
from jax.sharding import PartitionSpec as P

EPSILON = 1e-05
GATHER_BYTES = 2 * 1024 * 1024
KERNEL_BYTES = 4 * 1024 * 1024
ROUTES = (
    (3, 14, 4, 9, 5, 11, 0, 8, 1, 10, 7, 15, 2, 12, 6, 13),
    (6, 13, 3, 12, 1, 15, 7, 11, 5, 8, 4, 10, 0, 9, 2, 14),
    (5, 11, 7, 15, 3, 9, 4, 13, 2, 14, 1, 12, 6, 10, 0, 8),
    (1, 9, 0, 11, 7, 13, 2, 15, 6, 12, 3, 8, 4, 14, 5, 10),
)


def layer_norm(values, gain, shift, axis):
    centred = values - jnp.mean(values, axis=axis, keepdims=True)
    variance = jnp.mean(centred * centred, axis=axis, keepdims=True)
    return centred * lax.rsqrt(variance + EPSILON) * gain + shift


def gated(rows, w_proj, w_gate):
    proj = jnp.dot(rows, w_proj, preferred_element_type=jnp.float32)
    gate = jnp.dot(rows, w_gate, preferred_element_type=jnp.float32)
    return (jax.nn.sigmoid(gate) * proj).astype(jnp.bfloat16).astype(jnp.float32)


def lookup(values, bits):
    word = sum(value << (bits * place) for place, value in enumerate(values))
    word = jnp.int32(word - (1 << 32) if word >> 31 else word)
    device = lax.axis_index("row") * 2 + lax.axis_index("sub")
    return lax.shift_right_logical(word, device * bits) & ((1 << bits) - 1)


def place_of(sources, span):
    place = lookup([source // 2 % span for source in sources], 2)
    return place, lookup([source % 2 for source in sources], 1)


def copy_kernel(source_ref, target_ref):
    target_ref[...] = source_ref[...]


def flat_normed(values, gain_ref, bias_ref):
    flat = values.reshape(-1, values.shape[-1]).astype(jnp.float32)
    return layer_norm(flat, gain_ref[...], bias_ref[...], -1).astype(jnp.bfloat16)


def finish(left_ref, blocks, places, gating_ref, out_gain_ref, out_bias_ref, w_out_ref):
    sums, gates = [], []
    for block, (place, half) in zip(blocks, places):
        left = left_ref[half].astype(jnp.float32), left_ref[1 - half].astype(jnp.float32)
        for row in range(left_ref.shape[1]):
            products = block[0] * left[0][row] + block[1] * left[1][row]
            sums.append(jnp.sum(products, axis=1))
        gates.append(gating_ref[place])
    triangle = jnp.concatenate(sums, axis=0).astype(jnp.bfloat16).astype(jnp.float32)
    hidden_normed = layer_norm(triangle, out_gain_ref[...], out_bias_ref[...], -1)
    mixed = jnp.dot(
        hidden_normed.astype(jnp.bfloat16), w_out_ref[...], preferred_element_type=jnp.float32
    )
    return (jnp.concatenate(gates, axis=0) * mixed).reshape(len(gates), -1, mixed.shape[-1])


def first_kernel(
    span,
    routes,
    own_ref,
    other_ref,
    block_ref,
    norm_gain_ref,
    norm_bias_ref,
    w_a_proj_ref,
    w_a_gate_ref,
    w_b_proj_ref,
    w_b_gate_ref,
    w_gate_ref,
    out_gain_ref,
    out_bias_ref,
    w_out_ref,
    left_ref,
    gating_ref,
    update_ref,
):
    rows, cols, width = own_ref.shape
    sub = lax.axis_index("sub")
    own = flat_normed(own_ref[...], norm_gain_ref, norm_bias_ref)
    other = flat_normed(other_ref[...], norm_gain_ref, norm_bias_ref)
    for values, half in ((own, sub), (other, 1 - sub)):
        left = gated(values, w_a_proj_ref[...], w_a_gate_ref[...])
        left_ref[pl.ds(half, 1)] = left.astype(jnp.bfloat16).reshape(1, rows, cols, -1)
    gating = jax.nn.sigmoid(jnp.dot(own, w_gate_ref[...], preferred_element_type=jnp.float32))
    gating = gating.astype(jnp.bfloat16).astype(jnp.float32).reshape(rows, cols, width)
    for place in range(span):
        part = gating[:, place * rows : (place + 1) * rows]
        gating_ref[place] = part.reshape(rows * rows, width)
    right = gated(flat_normed(block_ref[...], norm_gain_ref, norm_bias_ref), w_b_proj_ref[...], w_b_gate_ref[...])
    right = right.reshape(1, 2, rows, cols, -1)
    places = [place_of(routes[0], span)]
    update_ref[...] = finish(left_ref, right, places, gating_ref, out_gain_ref, out_bias_ref, w_out_ref)


def last_kernel(span, routes, *refs):
    block_refs = refs[: span - 1][::-1]
    (
        left_ref,
        gating_ref,
        first_ref,
        norm_gain_ref,
        norm_bias_ref,
        w_b_proj_ref,
        w_b_gate_ref,
        out_gain_ref,
        out_bias_ref,
        w_out_ref,
        update_ref,
        placed_ref,
    ) = refs[span - 1 :]
    _, rows, cols, width = block_refs[0].shape
    right = jnp.stack([ref[...] for ref in block_refs])
    right = gated(flat_normed(right, norm_gain_ref, norm_bias_ref), w_b_proj_ref[...], w_b_gate_ref[...])
    right = right.reshape(span - 1, 2, rows, cols, -1)
    places = [place_of(sources, span) for sources in routes]
    last = finish(left_ref, right, places[1:], gating_ref, out_gain_ref, out_bias_ref, w_out_ref)
    placed_ref[pl.ds(places[0][0], 1)] = first_ref[...]
    for step in range(span - 1):
        placed_ref[pl.ds(places[step + 1][0], 1)] = last[step : step + 1]
    for row in range(rows):
        parts = [placed_ref[place, row * rows : (row + 1) * rows] for place in range(span)]
        update_ref[row] = jnp.concatenate(parts, axis=0).astype(jnp.bfloat16)


def gather_span(
    routes,
    pair_rep,
    norm_gain,
    norm_bias,
    w_a_proj,
    w_a_gate,
    w_b_proj,
    w_b_gate,
    w_gate,
    out_gain,
    out_bias,
    w_out,
):
    span = len(routes)
    block = pair_rep.shape
    rows, _, width = block
    params = pltpu.CompilerParams(vmem_limit_bytes=KERNEL_BYTES)
    cost = pl.CostEstimate(flops=10**8, bytes_accessed=10**6, transcendentals=0)

    def receive(values, sources):
        pairs = [(source, device) for device, source in enumerate(sources)]
        return lax.ppermute(values, ("row", "sub"), pairs)

    other = receive(pair_rep, [device ^ 1 for device in range(4 * span)])
    own = pl.pallas_call(
        copy_kernel,
        out_shape=jax.ShapeDtypeStruct(block, pair_rep.dtype),
        cost_estimate=cost,
        compiler_params=params,
    )(pair_rep)
    pair = jnp.stack([own, other])
    blocks = [receive(pair, sources) for sources in routes]
    norm = (norm_gain[None], norm_bias[None])
    out = (out_gain[None], out_bias[None], w_out)
    left, gating, update = pl.pallas_call(
        functools.partial(first_kernel, span, routes),
        out_shape=(
            jax.ShapeDtypeStruct((2,) + block, jnp.bfloat16),
            jax.ShapeDtypeStruct((span, rows * rows, width), jnp.float32),
            jax.ShapeDtypeStruct((1, rows * rows, width), jnp.float32),
        ),
        cost_estimate=cost,
        compiler_params=params,
    )(own, other, blocks[0], *norm, w_a_proj, w_a_gate, w_b_proj, w_b_gate, w_gate, *out)
    return pl.pallas_call(
        functools.partial(last_kernel, span, routes),
        out_shape=jax.ShapeDtypeStruct(block, pair_rep.dtype),
        scratch_shapes=[pltpu.VMEM((span, rows * rows, width), jnp.float32)],
        compiler_params=params,
    )(*blocks[:0:-1], left, gating, update, *norm, w_b_proj, w_b_gate, *out)


def exchange_channels(
    pair_rep,
    norm_gain,
    norm_bias,
    w_a_proj,
    w_a_gate,
    w_b_proj,
    w_b_gate,
    w_gate,
    out_gain,
    out_bias,
    w_out,
):
    hidden = w_a_proj.shape[1]
    w_inner = jnp.concatenate([w_a_proj, w_a_gate, w_b_proj, w_b_gate], axis=1)
    normed = layer_norm(pair_rep.astype(jnp.float32), norm_gain, norm_bias, -1).astype(jnp.bfloat16)
    inner = jnp.einsum("rkc,cm->mrk", normed, w_inner, preferred_element_type=jnp.float32)
    left_local = (jax.nn.sigmoid(inner[hidden : 2 * hidden]) * inner[:hidden]).astype(jnp.bfloat16)
    right_local = (
        jax.nn.sigmoid(inner[3 * hidden : 4 * hidden]) * inner[2 * hidden : 3 * hidden]
    ).astype(jnp.bfloat16)
    gating = jax.nn.sigmoid(
        jnp.einsum("rkc,cd->rkd", normed, w_gate, preferred_element_type=jnp.float32)
    ).astype(jnp.bfloat16)
    left_chan, right_chan = (
        lax.all_to_all(left_local, "row", split_axis=0, concat_axis=1, tiled=True),
        lax.all_to_all(right_local, "row", split_axis=0, concat_axis=1, tiled=True),
    )
    left_rows = lax.all_to_all(left_chan, "sub", split_axis=1, concat_axis=2, tiled=True)
    triangle = jnp.einsum(
        "hik,hjk->hij",
        left_rows,
        lax.all_gather(right_chan, "sub", axis=2, tiled=True),
        preferred_element_type=jnp.float32,
    ).astype(jnp.bfloat16)
    regrouped = lax.all_to_all(
        lax.all_to_all(triangle, "sub", split_axis=2, concat_axis=1, tiled=True),
        "row",
        split_axis=1,
        concat_axis=0,
        tiled=True,
    )
    hidden_normed = layer_norm(
        regrouped.astype(jnp.float32), out_gain[:, None, None], out_bias[:, None, None], 0
    ).astype(jnp.bfloat16)
    mixed = jnp.einsum("hrj,hc->rjc", hidden_normed, w_out, preferred_element_type=jnp.float32)
    return (gating.astype(jnp.float32) * mixed).astype(jnp.bfloat16)


def solution(mesh):
    n_row, n_sub = mesh.shape["row"], mesh.shape["sub"]

    def per_device(pair_rep, *weights):
        rows, cols, _ = pair_rep.shape
        gathered = n_row * n_sub * pair_rep.size * pair_rep.dtype.itemsize
        routed = (n_row, n_sub) == (8, 2) and cols == n_row // 2 * rows
        if routed and gathered <= GATHER_BYTES:
            return gather_span(ROUTES, pair_rep, *weights)
        return exchange_channels(pair_rep, *weights)

    in_specs = (P(("grp", "row"), "sub", None), P(), P(), P(), P(), P(), P(), P(), P(), P(), P())
    out_specs = P(("grp", "row"), "sub", None)
    return jax.shard_map(
        per_device, mesh=mesh, in_specs=in_specs, out_specs=out_specs, check_vma=False
    )
```

```python
import functools

import jax
import jax.numpy as jnp
from jax import lax
from jax.experimental import pallas as pl
from jax.experimental.pallas import tpu as pltpu
from jax.sharding import PartitionSpec as P

EPSILON = 1e-05
GATHER_BYTES = 2 * 1024 * 1024
KERNEL_BYTES = 4 * 1024 * 1024
ROUTES = (
    (3, 14, 4, 9, 5, 11, 0, 8, 1, 10, 7, 15, 2, 12, 6, 13),
    (6, 13, 3, 12, 1, 15, 7, 11, 5, 8, 4, 10, 0, 9, 2, 14),
    (5, 11, 7, 15, 3, 9, 4, 13, 2, 14, 1, 12, 6, 10, 0, 8),
    (1, 9, 0, 11, 7, 13, 2, 15, 6, 12, 3, 8, 4, 14, 5, 10),
)


def layer_norm(values, gain, shift, axis):
    centred = values - jnp.mean(values, axis=axis, keepdims=True)
    variance = jnp.mean(centred * centred, axis=axis, keepdims=True)
    return centred * lax.rsqrt(variance + EPSILON) * gain + shift


def gated(rows, w_proj, w_gate):
    proj = jnp.dot(rows, w_proj, preferred_element_type=jnp.float32)
    gate = jnp.dot(rows, w_gate, preferred_element_type=jnp.float32)
    return (jax.nn.sigmoid(gate) * proj).astype(jnp.bfloat16).astype(jnp.float32)


def lookup(values, bits):
    word = sum(value << (bits * place) for place, value in enumerate(values))
    word = jnp.int32(word - (1 << 32) if word >> 31 else word)
    device = lax.axis_index("row") * 2 + lax.axis_index("sub")
    return lax.shift_right_logical(word, device * bits) & ((1 << bits) - 1)


def place_of(sources, span):
    place = lookup([source // 2 % span for source in sources], 2)
    return place, lookup([source % 2 for source in sources], 1)


def copy_kernel(source_ref, target_ref):
    target_ref[...] = source_ref[...]


def flat_normed(values, gain_ref, bias_ref):
    flat = values.reshape(-1, values.shape[-1]).astype(jnp.float32)
    return layer_norm(flat, gain_ref[...], bias_ref[...], -1).astype(jnp.bfloat16)


def finish(left_ref, blocks, places, gating_ref, out_gain_ref, out_bias_ref, w_out_ref):
    sums, gates = [], []
    for block, (place, half) in zip(blocks, places):
        left = left_ref[half], left_ref[1 - half]
        for row in range(left_ref.shape[1]):
            products = block[0] * left[0][row] + block[1] * left[1][row]
            sums.append(jnp.sum(products, axis=1))
        gates.append(gating_ref[place])
    triangle = jnp.concatenate(sums, axis=0).astype(jnp.bfloat16).astype(jnp.float32)
    hidden_normed = layer_norm(triangle, out_gain_ref[...], out_bias_ref[...], -1)
    mixed = jnp.dot(
        hidden_normed.astype(jnp.bfloat16), w_out_ref[...], preferred_element_type=jnp.float32
    )
    return (jnp.concatenate(gates, axis=0) * mixed).reshape(len(gates), -1, mixed.shape[-1])


def left_kernel(
    span,
    own_ref,
    other_ref,
    norm_gain_ref,
    norm_bias_ref,
    w_a_proj_ref,
    w_a_gate_ref,
    w_gate_ref,
    w_b_proj_ref,
    w_b_gate_ref,
    out_gain_ref,
    out_bias_ref,
    w_out_ref,
    left_ref,
    gating_ref,
):
    rows, cols, width = own_ref.shape
    sub = lax.axis_index("sub")
    own = flat_normed(own_ref[...], norm_gain_ref, norm_bias_ref)
    other = flat_normed(other_ref[...], norm_gain_ref, norm_bias_ref)
    for values, half in ((own, sub), (other, 1 - sub)):
        left = gated(values, w_a_proj_ref[...], w_a_gate_ref[...])
        left_ref[pl.ds(half, 1)] = left.reshape(1, rows, cols, -1)
    gating = jax.nn.sigmoid(jnp.dot(own, w_gate_ref[...], preferred_element_type=jnp.float32))
    gating = gating.astype(jnp.bfloat16).astype(jnp.float32).reshape(rows, cols, width)
    for place in range(span):
        part = gating[:, place * rows : (place + 1) * rows]
        gating_ref[place] = part.reshape(rows * rows, width)


def first_kernel(
    span,
    routes,
    block_ref,
    left_ref,
    gating_ref,
    norm_gain_ref,
    norm_bias_ref,
    w_b_proj_ref,
    w_b_gate_ref,
    out_gain_ref,
    out_bias_ref,
    w_out_ref,
    update_ref,
):
    _, rows, cols, _ = block_ref.shape
    right = flat_normed(block_ref[...], norm_gain_ref, norm_bias_ref)
    right = gated(right, w_b_proj_ref[...], w_b_gate_ref[...]).reshape(1, 2, rows, cols, -1)
    places = [place_of(routes[0], span)]
    update_ref[...] = finish(left_ref, right, places, gating_ref, out_gain_ref, out_bias_ref, w_out_ref)


def last_kernel(span, routes, *refs):
    block_refs = refs[: span - 1][::-1]
    (
        left_ref,
        gating_ref,
        first_ref,
        norm_gain_ref,
        norm_bias_ref,
        w_b_proj_ref,
        w_b_gate_ref,
        out_gain_ref,
        out_bias_ref,
        w_out_ref,
        update_ref,
        placed_ref,
    ) = refs[span - 1 :]
    _, rows, cols, width = block_refs[0].shape
    right = jnp.stack([ref[...] for ref in block_refs])
    right = gated(flat_normed(right, norm_gain_ref, norm_bias_ref), w_b_proj_ref[...], w_b_gate_ref[...])
    right = right.reshape(span - 1, 2, rows, cols, -1)
    places = [place_of(sources, span) for sources in routes]
    last = finish(left_ref, right, places[1:], gating_ref, out_gain_ref, out_bias_ref, w_out_ref)
    placed_ref[pl.ds(places[0][0], 1)] = first_ref[...]
    for step in range(span - 1):
        placed_ref[pl.ds(places[step + 1][0], 1)] = last[step : step + 1]
    for row in range(rows):
        parts = [placed_ref[place, row * rows : (row + 1) * rows] for place in range(span)]
        update_ref[row] = jnp.concatenate(parts, axis=0).astype(jnp.bfloat16)


def gather_span(
    routes,
    pair_rep,
    norm_gain,
    norm_bias,
    w_a_proj,
    w_a_gate,
    w_b_proj,
    w_b_gate,
    w_gate,
    out_gain,
    out_bias,
    w_out,
):
    span = len(routes)
    block = pair_rep.shape
    rows, _, width = block
    params = pltpu.CompilerParams(vmem_limit_bytes=KERNEL_BYTES)
    cost = pl.CostEstimate(flops=10**8, bytes_accessed=10**6, transcendentals=0)

    def receive(values, sources):
        pairs = [(source, device) for device, source in enumerate(sources)]
        return lax.ppermute(values, ("row", "sub"), pairs)

    other = receive(pair_rep, [device ^ 1 for device in range(4 * span)])
    own = pl.pallas_call(
        copy_kernel,
        out_shape=jax.ShapeDtypeStruct(block, pair_rep.dtype),
        cost_estimate=cost,
        compiler_params=params,
    )(pair_rep)
    pair = jnp.stack([own, other])
    blocks = [receive(pair, sources) for sources in routes]
    norm = (norm_gain[None], norm_bias[None])
    tail = (w_b_proj, w_b_gate, out_gain[None], out_bias[None], w_out)
    left, gating = pl.pallas_call(
        functools.partial(left_kernel, span),
        out_shape=(
            jax.ShapeDtypeStruct((2,) + block, jnp.float32),
            jax.ShapeDtypeStruct((span, rows * rows, width), jnp.float32),
        ),
        cost_estimate=cost,
        compiler_params=params,
    )(own, other, *norm, w_a_proj, w_a_gate, w_gate, *tail)
    update = pl.pallas_call(
        functools.partial(first_kernel, span, routes),
        out_shape=jax.ShapeDtypeStruct((1, rows * rows, width), jnp.float32),
        cost_estimate=cost,
        compiler_params=params,
    )(blocks[0], left, gating, *norm, *tail)
    return pl.pallas_call(
        functools.partial(last_kernel, span, routes),
        out_shape=jax.ShapeDtypeStruct(block, pair_rep.dtype),
        scratch_shapes=[pltpu.VMEM((span, rows * rows, width), jnp.float32)],
        compiler_params=params,
    )(*blocks[:0:-1], left, gating, update, *norm, *tail)


def exchange_channels(
    pair_rep,
    norm_gain,
    norm_bias,
    w_a_proj,
    w_a_gate,
    w_b_proj,
    w_b_gate,
    w_gate,
    out_gain,
    out_bias,
    w_out,
):
    hidden = w_a_proj.shape[1]
    w_inner = jnp.concatenate([w_a_proj, w_a_gate, w_b_proj, w_b_gate], axis=1)
    normed = layer_norm(pair_rep.astype(jnp.float32), norm_gain, norm_bias, -1).astype(jnp.bfloat16)
    inner = jnp.einsum("rkc,cm->mrk", normed, w_inner, preferred_element_type=jnp.float32)
    left_local = (jax.nn.sigmoid(inner[hidden : 2 * hidden]) * inner[:hidden]).astype(jnp.bfloat16)
    right_local = (
        jax.nn.sigmoid(inner[3 * hidden : 4 * hidden]) * inner[2 * hidden : 3 * hidden]
    ).astype(jnp.bfloat16)
    gating = jax.nn.sigmoid(
        jnp.einsum("rkc,cd->rkd", normed, w_gate, preferred_element_type=jnp.float32)
    ).astype(jnp.bfloat16)
    left_chan, right_chan = (
        lax.all_to_all(left_local, "row", split_axis=0, concat_axis=1, tiled=True),
        lax.all_to_all(right_local, "row", split_axis=0, concat_axis=1, tiled=True),
    )
    left_rows = lax.all_to_all(left_chan, "sub", split_axis=1, concat_axis=2, tiled=True)
    triangle = jnp.einsum(
        "hik,hjk->hij",
        left_rows,
        lax.all_gather(right_chan, "sub", axis=2, tiled=True),
        preferred_element_type=jnp.float32,
    ).astype(jnp.bfloat16)
    regrouped = lax.all_to_all(
        lax.all_to_all(triangle, "sub", split_axis=2, concat_axis=1, tiled=True),
        "row",
        split_axis=1,
        concat_axis=0,
        tiled=True,
    )
    hidden_normed = layer_norm(
        regrouped.astype(jnp.float32), out_gain[:, None, None], out_bias[:, None, None], 0
    ).astype(jnp.bfloat16)
    mixed = jnp.einsum("hrj,hc->rjc", hidden_normed, w_out, preferred_element_type=jnp.float32)
    return (gating.astype(jnp.float32) * mixed).astype(jnp.bfloat16)


def solution(mesh):
    n_row, n_sub = mesh.shape["row"], mesh.shape["sub"]

    def per_device(pair_rep, *weights):
        rows, cols, _ = pair_rep.shape
        gathered = n_row * n_sub * pair_rep.size * pair_rep.dtype.itemsize
        routed = (n_row, n_sub) == (8, 2) and cols == n_row // 2 * rows
        if routed and gathered <= GATHER_BYTES:
            return gather_span(ROUTES, pair_rep, *weights)
        return exchange_channels(pair_rep, *weights)

    in_specs = (P(("grp", "row"), "sub", None), P(), P(), P(), P(), P(), P(), P(), P(), P(), P())
    out_specs = P(("grp", "row"), "sub", None)
    return jax.shard_map(
        per_device, mesh=mesh, in_specs=in_specs, out_specs=out_specs, check_vma=False
    )
```

```python
import functools

import jax
import jax.numpy as jnp
from jax import lax
from jax.experimental import pallas as pl
from jax.experimental.pallas import tpu as pltpu
from jax.sharding import PartitionSpec as P

EPSILON = 1e-05
GATHER_BYTES = 2 * 1024 * 1024
KERNEL_BYTES = 4 * 1024 * 1024
ROUTES = (
    (3, 14, 4, 9, 5, 11, 0, 8, 1, 10, 7, 15, 2, 12, 6, 13),
    (6, 13, 3, 12, 1, 15, 7, 11, 5, 8, 4, 10, 0, 9, 2, 14),
    (5, 11, 7, 15, 3, 9, 4, 13, 2, 14, 1, 12, 6, 10, 0, 8),
    (1, 9, 0, 11, 7, 13, 2, 15, 6, 12, 3, 8, 4, 14, 5, 10),
)


def layer_norm(values, gain, shift, axis):
    centred = values - jnp.mean(values, axis=axis, keepdims=True)
    variance = jnp.mean(centred * centred, axis=axis, keepdims=True)
    return centred * lax.rsqrt(variance + EPSILON) * gain + shift


def gated(rows, w_proj, w_gate):
    proj = jnp.dot(rows, w_proj, preferred_element_type=jnp.float32)
    gate = jnp.dot(rows, w_gate, preferred_element_type=jnp.float32)
    return (jax.nn.sigmoid(gate) * proj).astype(jnp.bfloat16).astype(jnp.float32)


def lookup(values, bits):
    word = sum(value << (bits * place) for place, value in enumerate(values))
    word = jnp.int32(word - (1 << 32) if word >> 31 else word)
    device = lax.axis_index("row") * 2 + lax.axis_index("sub")
    return lax.shift_right_logical(word, device * bits) & ((1 << bits) - 1)


def place_of(sources, span):
    place = lookup([source // 2 % span for source in sources], 2)
    return place, lookup([source % 2 for source in sources], 1)


def copy_kernel(source_ref, target_ref):
    target_ref[...] = source_ref[...]


def flat_normed(values, gain_ref, bias_ref):
    flat = values.reshape(-1, values.shape[-1]).astype(jnp.float32)
    return layer_norm(flat, gain_ref[...], bias_ref[...], -1).astype(jnp.bfloat16)


def finish(left_ref, blocks, places, gating_ref, out_gain_ref, out_bias_ref, w_out_ref):
    sums, gates = [], []
    for block, (place, half) in zip(blocks, places):
        left = left_ref[half], left_ref[1 - half]
        for row in range(left_ref.shape[1]):
            products = block[0] * left[0][row] + block[1] * left[1][row]
            sums.append(jnp.sum(products, axis=1))
        gates.append(gating_ref[place])
    triangle = jnp.concatenate(sums, axis=0).astype(jnp.bfloat16).astype(jnp.float32)
    hidden_normed = layer_norm(triangle, out_gain_ref[...], out_bias_ref[...], -1)
    mixed = jnp.dot(
        hidden_normed.astype(jnp.bfloat16), w_out_ref[...], preferred_element_type=jnp.float32
    )
    return (jnp.concatenate(gates, axis=0) * mixed).reshape(len(gates), -1, mixed.shape[-1])


def left_kernel(
    span,
    own_ref,
    other_ref,
    norm_gain_ref,
    norm_bias_ref,
    w_a_proj_ref,
    w_a_gate_ref,
    w_gate_ref,
    w_b_proj_ref,
    w_b_gate_ref,
    out_gain_ref,
    out_bias_ref,
    w_out_ref,
    left_ref,
    gating_ref,
):
    rows, cols, width = own_ref.shape
    sub = lax.axis_index("sub")
    own = flat_normed(own_ref[...], norm_gain_ref, norm_bias_ref)
    other = flat_normed(other_ref[...], norm_gain_ref, norm_bias_ref)
    for values, half in ((own, sub), (other, 1 - sub)):
        left = gated(values, w_a_proj_ref[...], w_a_gate_ref[...])
        left_ref[pl.ds(half, 1)] = left.reshape(1, rows, cols, -1)
    gating = jax.nn.sigmoid(jnp.dot(own, w_gate_ref[...], preferred_element_type=jnp.float32))
    gating = gating.astype(jnp.bfloat16).astype(jnp.float32).reshape(rows, cols, width)
    for place in range(span):
        part = gating[:, place * rows : (place + 1) * rows]
        gating_ref[place] = part.reshape(rows * rows, width)


def first_kernel(
    span,
    routes,
    block_ref,
    left_ref,
    gating_ref,
    norm_gain_ref,
    norm_bias_ref,
    w_b_proj_ref,
    w_b_gate_ref,
    out_gain_ref,
    out_bias_ref,
    w_out_ref,
    update_ref,
):
    _, rows, cols, _ = block_ref.shape
    right = flat_normed(block_ref[...], norm_gain_ref, norm_bias_ref)
    right = gated(right, w_b_proj_ref[...], w_b_gate_ref[...]).reshape(1, 2, rows, cols, -1)
    places = [place_of(routes[0], span)]
    update_ref[...] = finish(left_ref, right, places, gating_ref, out_gain_ref, out_bias_ref, w_out_ref)


def last_kernel(span, routes, *refs):
    block_refs = refs[: span - 1]
    (
        left_ref,
        gating_ref,
        first_ref,
        norm_gain_ref,
        norm_bias_ref,
        w_b_proj_ref,
        w_b_gate_ref,
        out_gain_ref,
        out_bias_ref,
        w_out_ref,
        update_ref,
        placed_ref,
    ) = refs[span - 1 :]
    _, rows, cols, width = block_refs[0].shape
    right = jnp.stack([ref[...] for ref in block_refs])
    right = gated(flat_normed(right, norm_gain_ref, norm_bias_ref), w_b_proj_ref[...], w_b_gate_ref[...])
    right = right.reshape(span - 1, 2, rows, cols, -1)
    places = [place_of(sources, span) for sources in routes]
    last = finish(left_ref, right, places[1:], gating_ref, out_gain_ref, out_bias_ref, w_out_ref)
    placed_ref[pl.ds(places[0][0], 1)] = first_ref[...]
    for step in range(span - 1):
        placed_ref[pl.ds(places[step + 1][0], 1)] = last[step : step + 1]
    for row in range(rows):
        parts = [placed_ref[place, row * rows : (row + 1) * rows] for place in range(span)]
        update_ref[row] = jnp.concatenate(parts, axis=0).astype(jnp.bfloat16)


def gather_span(
    routes,
    pair_rep,
    norm_gain,
    norm_bias,
    w_a_proj,
    w_a_gate,
    w_b_proj,
    w_b_gate,
    w_gate,
    out_gain,
    out_bias,
    w_out,
):
    span = len(routes)
    block = pair_rep.shape
    rows, _, width = block
    params = pltpu.CompilerParams(vmem_limit_bytes=KERNEL_BYTES)
    cost = pl.CostEstimate(flops=10**8, bytes_accessed=10**6, transcendentals=0)

    def receive(values, sources):
        pairs = [(source, device) for device, source in enumerate(sources)]
        return lax.ppermute(values, ("row", "sub"), pairs)

    other = receive(pair_rep, [device ^ 1 for device in range(4 * span)])
    own = pl.pallas_call(
        copy_kernel,
        out_shape=jax.ShapeDtypeStruct(block, pair_rep.dtype),
        cost_estimate=cost,
        compiler_params=params,
    )(pair_rep)
    pair = jnp.stack([own, other])
    blocks = [receive(pair, sources) for sources in routes]
    norm = (norm_gain[None], norm_bias[None])
    tail = (w_b_proj, w_b_gate, out_gain[None], out_bias[None], w_out)
    left, gating = pl.pallas_call(
        functools.partial(left_kernel, span),
        out_shape=(
            jax.ShapeDtypeStruct((2,) + block, jnp.float32),
            jax.ShapeDtypeStruct((span, rows * rows, width), jnp.float32),
        ),
        cost_estimate=cost,
        compiler_params=params,
    )(own, other, *norm, w_a_proj, w_a_gate, w_gate, *tail)
    update = pl.pallas_call(
        functools.partial(first_kernel, span, routes),
        out_shape=jax.ShapeDtypeStruct((1, rows * rows, width), jnp.float32),
        cost_estimate=cost,
        compiler_params=params,
    )(blocks[0], left, gating, *norm, *tail)
    return pl.pallas_call(
        functools.partial(last_kernel, span, routes),
        out_shape=jax.ShapeDtypeStruct(block, pair_rep.dtype),
        scratch_shapes=[pltpu.VMEM((span, rows * rows, width), jnp.float32)],
        compiler_params=params,
    )(*blocks[1:], left, gating, update, *norm, *tail)


def exchange_channels(
    pair_rep,
    norm_gain,
    norm_bias,
    w_a_proj,
    w_a_gate,
    w_b_proj,
    w_b_gate,
    w_gate,
    out_gain,
    out_bias,
    w_out,
):
    hidden = w_a_proj.shape[1]
    w_inner = jnp.concatenate([w_a_proj, w_a_gate, w_b_proj, w_b_gate], axis=1)
    normed = layer_norm(pair_rep.astype(jnp.float32), norm_gain, norm_bias, -1).astype(jnp.bfloat16)
    inner = jnp.einsum("rkc,cm->mrk", normed, w_inner, preferred_element_type=jnp.float32)
    left_local = (jax.nn.sigmoid(inner[hidden : 2 * hidden]) * inner[:hidden]).astype(jnp.bfloat16)
    right_local = (
        jax.nn.sigmoid(inner[3 * hidden : 4 * hidden]) * inner[2 * hidden : 3 * hidden]
    ).astype(jnp.bfloat16)
    gating = jax.nn.sigmoid(
        jnp.einsum("rkc,cd->rkd", normed, w_gate, preferred_element_type=jnp.float32)
    ).astype(jnp.bfloat16)
    left_chan, right_chan = (
        lax.all_to_all(left_local, "row", split_axis=0, concat_axis=1, tiled=True),
        lax.all_to_all(right_local, "row", split_axis=0, concat_axis=1, tiled=True),
    )
    left_rows = lax.all_to_all(left_chan, "sub", split_axis=1, concat_axis=2, tiled=True)
    triangle = jnp.einsum(
        "hik,hjk->hij",
        left_rows,
        lax.all_gather(right_chan, "sub", axis=2, tiled=True),
        preferred_element_type=jnp.float32,
    ).astype(jnp.bfloat16)
    regrouped = lax.all_to_all(
        lax.all_to_all(triangle, "sub", split_axis=2, concat_axis=1, tiled=True),
        "row",
        split_axis=1,
        concat_axis=0,
        tiled=True,
    )
    hidden_normed = layer_norm(
        regrouped.astype(jnp.float32), out_gain[:, None, None], out_bias[:, None, None], 0
    ).astype(jnp.bfloat16)
    mixed = jnp.einsum("hrj,hc->rjc", hidden_normed, w_out, preferred_element_type=jnp.float32)
    return (gating.astype(jnp.float32) * mixed).astype(jnp.bfloat16)


def solution(mesh):
    n_row, n_sub = mesh.shape["row"], mesh.shape["sub"]

    def per_device(pair_rep, *weights):
        rows, cols, _ = pair_rep.shape
        gathered = n_row * n_sub * pair_rep.size * pair_rep.dtype.itemsize
        routed = (n_row, n_sub) == (8, 2) and cols == n_row // 2 * rows
        if routed and gathered <= GATHER_BYTES:
            return gather_span(ROUTES, pair_rep, *weights)
        return exchange_channels(pair_rep, *weights)

    in_specs = (P(("grp", "row"), "sub", None), P(), P(), P(), P(), P(), P(), P(), P(), P(), P())
    out_specs = P(("grp", "row"), "sub", None)
    return jax.shard_map(
        per_device, mesh=mesh, in_specs=in_specs, out_specs=out_specs, check_vma=False
    )
```

```python
import functools

import jax
import jax.numpy as jnp
from jax import lax
from jax.experimental import pallas as pl
from jax.experimental.pallas import tpu as pltpu
from jax.sharding import PartitionSpec as P

EPSILON = 1e-05
GATHER_BYTES = 2 * 1024 * 1024
KERNEL_BYTES = 4 * 1024 * 1024
ROUTES = (
    (3, 14, 4, 9, 5, 11, 0, 8, 1, 10, 7, 15, 2, 12, 6, 13),
    (6, 13, 3, 12, 1, 15, 7, 11, 5, 8, 4, 10, 0, 9, 2, 14),
    (5, 11, 7, 15, 3, 9, 4, 13, 2, 14, 1, 12, 6, 10, 0, 8),
    (1, 9, 0, 11, 7, 13, 2, 15, 6, 12, 3, 8, 4, 14, 5, 10),
)


def layer_norm(values, gain, shift, axis):
    centred = values - jnp.mean(values, axis=axis, keepdims=True)
    variance = jnp.mean(centred * centred, axis=axis, keepdims=True)
    return centred * lax.rsqrt(variance + EPSILON) * gain + shift


def gated(rows, w_proj, w_gate):
    proj = jnp.dot(rows, w_proj, preferred_element_type=jnp.float32)
    gate = jnp.dot(rows, w_gate, preferred_element_type=jnp.float32)
    return (jax.nn.sigmoid(gate) * proj).astype(jnp.bfloat16).astype(jnp.float32)


def lookup(values, bits):
    word = sum(value << (bits * place) for place, value in enumerate(values))
    word = jnp.int32(word - (1 << 32) if word >> 31 else word)
    device = lax.axis_index("row") * 2 + lax.axis_index("sub")
    return lax.shift_right_logical(word, device * bits) & ((1 << bits) - 1)


def place_of(sources, span):
    place = lookup([source // 2 % span for source in sources], 2)
    return place, lookup([source % 2 for source in sources], 1)


def copy_kernel(source_ref, target_ref):
    target_ref[...] = source_ref[...]


def flat_normed(values, gain_ref, bias_ref):
    flat = values.reshape(-1, values.shape[-1]).astype(jnp.float32)
    return layer_norm(flat, gain_ref[...], bias_ref[...], -1).astype(jnp.bfloat16)


def finish(left_ref, blocks, places, gating_ref, out_gain_ref, out_bias_ref, w_out_ref):
    sums, gates = [], []
    for block, (place, half) in zip(blocks, places):
        left = left_ref[half], left_ref[1 - half]
        for row in range(left_ref.shape[1]):
            products = block[0] * left[0][row] + block[1] * left[1][row]
            sums.append(jnp.sum(products, axis=1))
        gates.append(gating_ref[place])
    triangle = jnp.concatenate(sums, axis=0).astype(jnp.bfloat16).astype(jnp.float32)
    hidden_normed = layer_norm(triangle, out_gain_ref[...], out_bias_ref[...], -1)
    mixed = jnp.dot(
        hidden_normed.astype(jnp.bfloat16), w_out_ref[...], preferred_element_type=jnp.float32
    )
    return (jnp.concatenate(gates, axis=0) * mixed).reshape(len(gates), -1, mixed.shape[-1])


def left_kernel(
    span,
    own_ref,
    other_ref,
    norm_gain_ref,
    norm_bias_ref,
    w_a_proj_ref,
    w_a_gate_ref,
    w_gate_ref,
    w_b_proj_ref,
    w_b_gate_ref,
    out_gain_ref,
    out_bias_ref,
    w_out_ref,
    left_ref,
    gating_ref,
):
    rows, cols, width = own_ref.shape
    sub = lax.axis_index("sub")
    own = flat_normed(own_ref[...], norm_gain_ref, norm_bias_ref)
    other = flat_normed(other_ref[...], norm_gain_ref, norm_bias_ref)
    for values, half in ((own, sub), (other, 1 - sub)):
        left = gated(values, w_a_proj_ref[...], w_a_gate_ref[...])
        left_ref[pl.ds(half, 1)] = left.reshape(1, rows, cols, -1)
    gating = jax.nn.sigmoid(jnp.dot(own, w_gate_ref[...], preferred_element_type=jnp.float32))
    gating = gating.astype(jnp.bfloat16).astype(jnp.float32).reshape(rows, cols, width)
    for place in range(span):
        part = gating[:, place * rows : (place + 1) * rows]
        gating_ref[place] = part.reshape(rows * rows, width)


def first_kernel(
    span,
    routes,
    block_ref,
    left_ref,
    gating_ref,
    norm_gain_ref,
    norm_bias_ref,
    w_b_proj_ref,
    w_b_gate_ref,
    out_gain_ref,
    out_bias_ref,
    w_out_ref,
    update_ref,
):
    _, rows, cols, _ = block_ref.shape
    right = flat_normed(block_ref[...], norm_gain_ref, norm_bias_ref)
    right = gated(right, w_b_proj_ref[...], w_b_gate_ref[...]).reshape(1, 2, rows, cols, -1)
    places = [place_of(routes[0], span)]
    update_ref[...] = finish(left_ref, right, places, gating_ref, out_gain_ref, out_bias_ref, w_out_ref)


def last_kernel(span, routes, *refs):
    block_refs = refs[: span - 1]
    (
        left_ref,
        gating_ref,
        first_ref,
        norm_gain_ref,
        norm_bias_ref,
        w_b_proj_ref,
        w_b_gate_ref,
        out_gain_ref,
        out_bias_ref,
        w_out_ref,
        update_ref,
        placed_ref,
        result_ref,
        done,
    ) = refs[span - 1 :]
    _, rows, cols, width = block_refs[0].shape
    right = jnp.stack([ref[...] for ref in block_refs])
    right = gated(flat_normed(right, norm_gain_ref, norm_bias_ref), w_b_proj_ref[...], w_b_gate_ref[...])
    right = right.reshape(span - 1, 2, rows, cols, -1)
    places = [place_of(sources, span) for sources in routes]
    last = finish(left_ref, right, places[1:], gating_ref, out_gain_ref, out_bias_ref, w_out_ref)
    placed_ref[pl.ds(places[0][0], 1)] = first_ref[...]
    for step in range(span - 1):
        placed_ref[pl.ds(places[step + 1][0], 1)] = last[step : step + 1]
    for row in range(rows):
        parts = [placed_ref[place, row * rows : (row + 1) * rows] for place in range(span)]
        result_ref[row] = jnp.concatenate(parts, axis=0).astype(jnp.bfloat16)
    copy = pltpu.make_async_copy(result_ref, update_ref, done)
    copy.start()
    copy.wait()


def gather_span(
    routes,
    pair_rep,
    norm_gain,
    norm_bias,
    w_a_proj,
    w_a_gate,
    w_b_proj,
    w_b_gate,
    w_gate,
    out_gain,
    out_bias,
    w_out,
):
    span = len(routes)
    block = pair_rep.shape
    rows, _, width = block
    params = pltpu.CompilerParams(vmem_limit_bytes=KERNEL_BYTES)
    cost = pl.CostEstimate(flops=10**8, bytes_accessed=10**6, transcendentals=0)

    def receive(values, sources):
        pairs = [(source, device) for device, source in enumerate(sources)]
        return lax.ppermute(values, ("row", "sub"), pairs)

    other = receive(pair_rep, [device ^ 1 for device in range(4 * span)])
    own = pl.pallas_call(
        copy_kernel,
        out_shape=jax.ShapeDtypeStruct(block, pair_rep.dtype),
        cost_estimate=cost,
        compiler_params=params,
    )(pair_rep)
    pair = jnp.stack([own, other])
    blocks = [receive(pair, sources) for sources in routes]
    norm = (norm_gain[None], norm_bias[None])
    tail = (w_b_proj, w_b_gate, out_gain[None], out_bias[None], w_out)
    left, gating = pl.pallas_call(
        functools.partial(left_kernel, span),
        out_shape=(
            jax.ShapeDtypeStruct((2,) + block, jnp.float32),
            jax.ShapeDtypeStruct((span, rows * rows, width), jnp.float32),
        ),
        cost_estimate=cost,
        compiler_params=params,
    )(own, other, *norm, w_a_proj, w_a_gate, w_gate, *tail)
    update = pl.pallas_call(
        functools.partial(first_kernel, span, routes),
        out_shape=jax.ShapeDtypeStruct((1, rows * rows, width), jnp.float32),
        cost_estimate=cost,
        compiler_params=params,
    )(blocks[0], left, gating, *norm, *tail)
    return pl.pallas_call(
        functools.partial(last_kernel, span, routes),
        out_shape=jax.ShapeDtypeStruct(block, pair_rep.dtype),
        out_specs=pl.BlockSpec(memory_space=pl.ANY),
        scratch_shapes=[
            pltpu.VMEM((span, rows * rows, width), jnp.float32),
            pltpu.VMEM(block, pair_rep.dtype),
            pltpu.SemaphoreType.DMA,
        ],
        compiler_params=params,
    )(*blocks[1:], left, gating, update, *norm, *tail)


def exchange_channels(
    pair_rep,
    norm_gain,
    norm_bias,
    w_a_proj,
    w_a_gate,
    w_b_proj,
    w_b_gate,
    w_gate,
    out_gain,
    out_bias,
    w_out,
):
    hidden = w_a_proj.shape[1]
    w_inner = jnp.concatenate([w_a_proj, w_a_gate, w_b_proj, w_b_gate], axis=1)
    normed = layer_norm(pair_rep.astype(jnp.float32), norm_gain, norm_bias, -1).astype(jnp.bfloat16)
    inner = jnp.einsum("rkc,cm->mrk", normed, w_inner, preferred_element_type=jnp.float32)
    left_local = (jax.nn.sigmoid(inner[hidden : 2 * hidden]) * inner[:hidden]).astype(jnp.bfloat16)
    right_local = (
        jax.nn.sigmoid(inner[3 * hidden : 4 * hidden]) * inner[2 * hidden : 3 * hidden]
    ).astype(jnp.bfloat16)
    gating = jax.nn.sigmoid(
        jnp.einsum("rkc,cd->rkd", normed, w_gate, preferred_element_type=jnp.float32)
    ).astype(jnp.bfloat16)
    left_chan, right_chan = (
        lax.all_to_all(left_local, "row", split_axis=0, concat_axis=1, tiled=True),
        lax.all_to_all(right_local, "row", split_axis=0, concat_axis=1, tiled=True),
    )
    left_rows = lax.all_to_all(left_chan, "sub", split_axis=1, concat_axis=2, tiled=True)
    triangle = jnp.einsum(
        "hik,hjk->hij",
        left_rows,
        lax.all_gather(right_chan, "sub", axis=2, tiled=True),
        preferred_element_type=jnp.float32,
    ).astype(jnp.bfloat16)
    regrouped = lax.all_to_all(
        lax.all_to_all(triangle, "sub", split_axis=2, concat_axis=1, tiled=True),
        "row",
        split_axis=1,
        concat_axis=0,
        tiled=True,
    )
    hidden_normed = layer_norm(
        regrouped.astype(jnp.float32), out_gain[:, None, None], out_bias[:, None, None], 0
    ).astype(jnp.bfloat16)
    mixed = jnp.einsum("hrj,hc->rjc", hidden_normed, w_out, preferred_element_type=jnp.float32)
    return (gating.astype(jnp.float32) * mixed).astype(jnp.bfloat16)


def solution(mesh):
    n_row, n_sub = mesh.shape["row"], mesh.shape["sub"]

    def per_device(pair_rep, *weights):
        rows, cols, _ = pair_rep.shape
        gathered = n_row * n_sub * pair_rep.size * pair_rep.dtype.itemsize
        routed = (n_row, n_sub) == (8, 2) and cols == n_row // 2 * rows
        if routed and gathered <= GATHER_BYTES:
            return gather_span(ROUTES, pair_rep, *weights)
        return exchange_channels(pair_rep, *weights)

    in_specs = (P(("grp", "row"), "sub", None), P(), P(), P(), P(), P(), P(), P(), P(), P(), P())
    out_specs = P(("grp", "row"), "sub", None)
    return jax.shard_map(
        per_device, mesh=mesh, in_specs=in_specs, out_specs=out_specs, check_vma=False
    )
```

```python
import functools

import jax
import jax.numpy as jnp
from jax import lax
from jax.experimental import pallas as pl
from jax.experimental.pallas import tpu as pltpu
from jax.sharding import PartitionSpec as P

EPSILON = 1e-05
GATHER_BYTES = 2 * 1024 * 1024
KERNEL_BYTES = 4 * 1024 * 1024
ROUTES = (
    (6, 11, 3, 8, 1, 9, 4, 10, 0, 13, 5, 15, 2, 12, 7, 14),
    (5, 15, 6, 12, 2, 11, 1, 9, 7, 8, 3, 10, 0, 14, 4, 13),
    (3, 13, 4, 14, 5, 15, 7, 12, 2, 10, 1, 8, 6, 9, 0, 11),
    (1, 9, 0, 11, 7, 13, 2, 15, 4, 14, 6, 12, 5, 10, 3, 8),
)


def layer_norm(values, gain, shift, axis):
    centred = values - jnp.mean(values, axis=axis, keepdims=True)
    variance = jnp.mean(centred * centred, axis=axis, keepdims=True)
    return centred * lax.rsqrt(variance + EPSILON) * gain + shift


def gated(rows, w_proj, w_gate):
    proj = jnp.dot(rows, w_proj, preferred_element_type=jnp.float32)
    gate = jnp.dot(rows, w_gate, preferred_element_type=jnp.float32)
    return (jax.nn.sigmoid(gate) * proj).astype(jnp.bfloat16).astype(jnp.float32)


def lookup(values, bits):
    word = sum(value << (bits * place) for place, value in enumerate(values))
    word = jnp.int32(word - (1 << 32) if word >> 31 else word)
    device = lax.axis_index("row") * 2 + lax.axis_index("sub")
    return lax.shift_right_logical(word, device * bits) & ((1 << bits) - 1)


def place_of(sources, span):
    place = lookup([source // 2 % span for source in sources], 2)
    return place, lookup([source % 2 for source in sources], 1)


def copy_kernel(source_ref, target_ref):
    target_ref[...] = source_ref[...]


def flat_normed(values, gain_ref, bias_ref):
    flat = values.reshape(-1, values.shape[-1]).astype(jnp.float32)
    return layer_norm(flat, gain_ref[...], bias_ref[...], -1).astype(jnp.bfloat16)


def finish(left_ref, blocks, places, gating_ref, out_gain_ref, out_bias_ref, w_out_ref):
    sums, gates = [], []
    for block, (place, half) in zip(blocks, places):
        left = left_ref[half], left_ref[1 - half]
        for row in range(left_ref.shape[1]):
            products = block[0] * left[0][row] + block[1] * left[1][row]
            sums.append(jnp.sum(products, axis=1))
        gates.append(gating_ref[place])
    triangle = jnp.concatenate(sums, axis=0).astype(jnp.bfloat16).astype(jnp.float32)
    hidden_normed = layer_norm(triangle, out_gain_ref[...], out_bias_ref[...], -1)
    mixed = jnp.dot(
        hidden_normed.astype(jnp.bfloat16), w_out_ref[...], preferred_element_type=jnp.float32
    )
    return (jnp.concatenate(gates, axis=0) * mixed).reshape(len(gates), -1, mixed.shape[-1])


def left_kernel(
    span,
    own_ref,
    other_ref,
    norm_gain_ref,
    norm_bias_ref,
    w_a_proj_ref,
    w_a_gate_ref,
    w_gate_ref,
    w_b_proj_ref,
    w_b_gate_ref,
    out_gain_ref,
    out_bias_ref,
    w_out_ref,
    left_ref,
    gating_ref,
):
    rows, cols, width = own_ref.shape
    sub = lax.axis_index("sub")
    own = flat_normed(own_ref[...], norm_gain_ref, norm_bias_ref)
    other = flat_normed(other_ref[...], norm_gain_ref, norm_bias_ref)
    for values, half in ((own, sub), (other, 1 - sub)):
        left = gated(values, w_a_proj_ref[...], w_a_gate_ref[...])
        left_ref[pl.ds(half, 1)] = left.reshape(1, rows, cols, -1)
    gating = jax.nn.sigmoid(jnp.dot(own, w_gate_ref[...], preferred_element_type=jnp.float32))
    gating = gating.astype(jnp.bfloat16).astype(jnp.float32).reshape(rows, cols, width)
    for place in range(span):
        part = gating[:, place * rows : (place + 1) * rows]
        gating_ref[place] = part.reshape(rows * rows, width)


def first_kernel(
    span,
    routes,
    block_ref,
    left_ref,
    gating_ref,
    norm_gain_ref,
    norm_bias_ref,
    w_b_proj_ref,
    w_b_gate_ref,
    out_gain_ref,
    out_bias_ref,
    w_out_ref,
    update_ref,
):
    _, rows, cols, _ = block_ref.shape
    right = flat_normed(block_ref[...], norm_gain_ref, norm_bias_ref)
    right = gated(right, w_b_proj_ref[...], w_b_gate_ref[...]).reshape(1, 2, rows, cols, -1)
    places = [place_of(routes[0], span)]
    update_ref[...] = finish(left_ref, right, places, gating_ref, out_gain_ref, out_bias_ref, w_out_ref)


def last_kernel(span, routes, *refs):
    block_refs = refs[: span - 1]
    (
        left_ref,
        gating_ref,
        first_ref,
        norm_gain_ref,
        norm_bias_ref,
        w_b_proj_ref,
        w_b_gate_ref,
        out_gain_ref,
        out_bias_ref,
        w_out_ref,
        update_ref,
        placed_ref,
        result_ref,
        done,
    ) = refs[span - 1 :]
    _, rows, cols, width = block_refs[0].shape
    right = jnp.stack([ref[...] for ref in block_refs])
    right = gated(flat_normed(right, norm_gain_ref, norm_bias_ref), w_b_proj_ref[...], w_b_gate_ref[...])
    right = right.reshape(span - 1, 2, rows, cols, -1)
    places = [place_of(sources, span) for sources in routes]
    last = finish(left_ref, right, places[1:], gating_ref, out_gain_ref, out_bias_ref, w_out_ref)
    placed_ref[pl.ds(places[0][0], 1)] = first_ref[...]
    for step in range(span - 1):
        placed_ref[pl.ds(places[step + 1][0], 1)] = last[step : step + 1]
    for row in range(rows):
        parts = [placed_ref[place, row * rows : (row + 1) * rows] for place in range(span)]
        result_ref[row] = jnp.concatenate(parts, axis=0).astype(jnp.bfloat16)
    copy = pltpu.make_async_copy(result_ref, update_ref, done)
    copy.start()
    copy.wait()


def gather_span(
    routes,
    pair_rep,
    norm_gain,
    norm_bias,
    w_a_proj,
    w_a_gate,
    w_b_proj,
    w_b_gate,
    w_gate,
    out_gain,
    out_bias,
    w_out,
):
    span = len(routes)
    block = pair_rep.shape
    rows, _, width = block
    params = pltpu.CompilerParams(vmem_limit_bytes=KERNEL_BYTES)
    cost = pl.CostEstimate(flops=10**8, bytes_accessed=10**6, transcendentals=0)

    def receive(values, sources):
        pairs = [(source, device) for device, source in enumerate(sources)]
        return lax.ppermute(values, ("row", "sub"), pairs)

    other = receive(pair_rep, [device ^ 1 for device in range(4 * span)])
    own = pl.pallas_call(
        copy_kernel,
        out_shape=jax.ShapeDtypeStruct(block, pair_rep.dtype),
        cost_estimate=cost,
        compiler_params=params,
    )(pair_rep)
    pair = jnp.stack([own, other])
    blocks = [receive(pair, sources) for sources in routes]
    norm = (norm_gain[None], norm_bias[None])
    tail = (w_b_proj, w_b_gate, out_gain[None], out_bias[None], w_out)
    left, gating = pl.pallas_call(
        functools.partial(left_kernel, span),
        out_shape=(
            jax.ShapeDtypeStruct((2,) + block, jnp.float32),
            jax.ShapeDtypeStruct((span, rows * rows, width), jnp.float32),
        ),
        cost_estimate=cost,
        compiler_params=params,
    )(own, other, *norm, w_a_proj, w_a_gate, w_gate, *tail)
    update = pl.pallas_call(
        functools.partial(first_kernel, span, routes),
        out_shape=jax.ShapeDtypeStruct((1, rows * rows, width), jnp.float32),
        cost_estimate=cost,
        compiler_params=params,
    )(blocks[0], left, gating, *norm, *tail)
    return pl.pallas_call(
        functools.partial(last_kernel, span, routes),
        out_shape=jax.ShapeDtypeStruct(block, pair_rep.dtype),
        out_specs=pl.BlockSpec(memory_space=pl.ANY),
        scratch_shapes=[
            pltpu.VMEM((span, rows * rows, width), jnp.float32),
            pltpu.VMEM(block, pair_rep.dtype),
            pltpu.SemaphoreType.DMA,
        ],
        compiler_params=params,
    )(*blocks[1:], left, gating, update, *norm, *tail)


def exchange_channels(
    pair_rep,
    norm_gain,
    norm_bias,
    w_a_proj,
    w_a_gate,
    w_b_proj,
    w_b_gate,
    w_gate,
    out_gain,
    out_bias,
    w_out,
):
    hidden = w_a_proj.shape[1]
    w_inner = jnp.concatenate([w_a_proj, w_a_gate, w_b_proj, w_b_gate], axis=1)
    normed = layer_norm(pair_rep.astype(jnp.float32), norm_gain, norm_bias, -1).astype(jnp.bfloat16)
    inner = jnp.einsum("rkc,cm->mrk", normed, w_inner, preferred_element_type=jnp.float32)
    left_local = (jax.nn.sigmoid(inner[hidden : 2 * hidden]) * inner[:hidden]).astype(jnp.bfloat16)
    right_local = (
        jax.nn.sigmoid(inner[3 * hidden : 4 * hidden]) * inner[2 * hidden : 3 * hidden]
    ).astype(jnp.bfloat16)
    gating = jax.nn.sigmoid(
        jnp.einsum("rkc,cd->rkd", normed, w_gate, preferred_element_type=jnp.float32)
    ).astype(jnp.bfloat16)
    left_chan, right_chan = (
        lax.all_to_all(left_local, "row", split_axis=0, concat_axis=1, tiled=True),
        lax.all_to_all(right_local, "row", split_axis=0, concat_axis=1, tiled=True),
    )
    left_rows = lax.all_to_all(left_chan, "sub", split_axis=1, concat_axis=2, tiled=True)
    triangle = jnp.einsum(
        "hik,hjk->hij",
        left_rows,
        lax.all_gather(right_chan, "sub", axis=2, tiled=True),
        preferred_element_type=jnp.float32,
    ).astype(jnp.bfloat16)
    regrouped = lax.all_to_all(
        lax.all_to_all(triangle, "sub", split_axis=2, concat_axis=1, tiled=True),
        "row",
        split_axis=1,
        concat_axis=0,
        tiled=True,
    )
    hidden_normed = layer_norm(
        regrouped.astype(jnp.float32), out_gain[:, None, None], out_bias[:, None, None], 0
    ).astype(jnp.bfloat16)
    mixed = jnp.einsum("hrj,hc->rjc", hidden_normed, w_out, preferred_element_type=jnp.float32)
    return (gating.astype(jnp.float32) * mixed).astype(jnp.bfloat16)


def solution(mesh):
    n_row, n_sub = mesh.shape["row"], mesh.shape["sub"]

    def per_device(pair_rep, *weights):
        rows, cols, _ = pair_rep.shape
        gathered = n_row * n_sub * pair_rep.size * pair_rep.dtype.itemsize
        routed = (n_row, n_sub) == (8, 2) and cols == n_row // 2 * rows
        if routed and gathered <= GATHER_BYTES:
            return gather_span(ROUTES, pair_rep, *weights)
        return exchange_channels(pair_rep, *weights)

    in_specs = (P(("grp", "row"), "sub", None), P(), P(), P(), P(), P(), P(), P(), P(), P(), P())
    out_specs = P(("grp", "row"), "sub", None)
    return jax.shard_map(
        per_device, mesh=mesh, in_specs=in_specs, out_specs=out_specs, check_vma=False
    )
```

```python
import functools

import jax
import jax.numpy as jnp
from jax import lax
from jax.experimental import pallas as pl
from jax.experimental.pallas import tpu as pltpu
from jax.sharding import PartitionSpec as P

EPSILON = 1e-05
GATHER_BYTES = 2 * 1024 * 1024
KERNEL_BYTES = 4 * 1024 * 1024
ROUTES = (
    (
        (6, 15, 4, 13, 3, 11, 7, 9, 1, 10, 2, 8, 0, 12, 5, 14),
        (5, 13, 3, 9, 0, 15, 1, 14, 7, 8, 4, 10, 2, 11, 6, 12),
        (3, 11, 6, 14, 5, 8, 4, 13, 2, 12, 1, 15, 7, 9, 0, 10),
        (1, 9, 0, 11, 6, 13, 2, 10, 5, 15, 7, 12, 4, 14, 3, 8),
    ),
    (
        (5, 12, 1, 13, 3, 15, 0, 9, 2, 8, 6, 10, 4, 11, 7, 14),
        (7, 15, 3, 8, 6, 10, 4, 11, 1, 14, 2, 13, 0, 12, 5, 9),
        (3, 11, 4, 15, 5, 9, 7, 13, 6, 10, 1, 8, 2, 14, 0, 12),
        (1, 9, 7, 11, 0, 13, 2, 14, 5, 12, 4, 15, 6, 8, 3, 10),
    ),
)


def layer_norm(values, gain, shift, axis):
    centred = values - jnp.mean(values, axis=axis, keepdims=True)
    variance = jnp.mean(centred * centred, axis=axis, keepdims=True)
    return centred * lax.rsqrt(variance + EPSILON) * gain + shift


def gated(rows, w_proj, w_gate):
    proj = jnp.dot(rows, w_proj, preferred_element_type=jnp.float32)
    gate = jnp.dot(rows, w_gate, preferred_element_type=jnp.float32)
    return (jax.nn.sigmoid(gate) * proj).astype(jnp.bfloat16).astype(jnp.float32)


def lookup(tables, bits):
    words = []
    for values in tables:
        word = sum(value << (bits * place) for place, value in enumerate(values))
        words.append(jnp.int32(word - (1 << 32) if word >> 31 else word))
    word = jnp.where(lax.axis_index("grp") == 0, *words)
    device = lax.axis_index("row") * 2 + lax.axis_index("sub")
    return lax.shift_right_logical(word, device * bits) & ((1 << bits) - 1)


def place_of(sources, span):
    place = lookup([[source // 2 % span for source in table] for table in sources], 2)
    return place, lookup([[source % 2 for source in table] for table in sources], 1)


def copy_kernel(source_ref, target_ref):
    target_ref[...] = source_ref[...]


def flat_normed(values, gain_ref, bias_ref):
    flat = values.reshape(-1, values.shape[-1]).astype(jnp.float32)
    return layer_norm(flat, gain_ref[...], bias_ref[...], -1).astype(jnp.bfloat16)


def finish(left_ref, blocks, places, gating_ref, out_gain_ref, out_bias_ref, w_out_ref):
    sums, gates = [], []
    for block, (place, half) in zip(blocks, places):
        left = left_ref[half], left_ref[1 - half]
        for row in range(left_ref.shape[1]):
            products = block[0] * left[0][row] + block[1] * left[1][row]
            sums.append(jnp.sum(products, axis=1))
        gates.append(gating_ref[place])
    triangle = jnp.concatenate(sums, axis=0).astype(jnp.bfloat16).astype(jnp.float32)
    hidden_normed = layer_norm(triangle, out_gain_ref[...], out_bias_ref[...], -1)
    mixed = jnp.dot(
        hidden_normed.astype(jnp.bfloat16), w_out_ref[...], preferred_element_type=jnp.float32
    )
    return (jnp.concatenate(gates, axis=0) * mixed).reshape(len(gates), -1, mixed.shape[-1])


def left_kernel(
    span,
    own_ref,
    other_ref,
    norm_gain_ref,
    norm_bias_ref,
    w_a_proj_ref,
    w_a_gate_ref,
    w_gate_ref,
    w_b_proj_ref,
    w_b_gate_ref,
    out_gain_ref,
    out_bias_ref,
    w_out_ref,
    left_ref,
    gating_ref,
):
    rows, cols, width = own_ref.shape
    sub = lax.axis_index("sub")
    own = flat_normed(own_ref[...], norm_gain_ref, norm_bias_ref)
    other = flat_normed(other_ref[...], norm_gain_ref, norm_bias_ref)
    for values, half in ((own, sub), (other, 1 - sub)):
        left = gated(values, w_a_proj_ref[...], w_a_gate_ref[...])
        left_ref[pl.ds(half, 1)] = left.reshape(1, rows, cols, -1)
    gating = jax.nn.sigmoid(jnp.dot(own, w_gate_ref[...], preferred_element_type=jnp.float32))
    gating = gating.astype(jnp.bfloat16).astype(jnp.float32).reshape(rows, cols, width)
    for place in range(span):
        part = gating[:, place * rows : (place + 1) * rows]
        gating_ref[place] = part.reshape(rows * rows, width)


def first_kernel(
    span,
    routes,
    block_ref,
    left_ref,
    gating_ref,
    norm_gain_ref,
    norm_bias_ref,
    w_b_proj_ref,
    w_b_gate_ref,
    out_gain_ref,
    out_bias_ref,
    w_out_ref,
    update_ref,
):
    _, rows, cols, _ = block_ref.shape
    right = flat_normed(block_ref[...], norm_gain_ref, norm_bias_ref)
    right = gated(right, w_b_proj_ref[...], w_b_gate_ref[...]).reshape(1, 2, rows, cols, -1)
    places = [place_of([table[0] for table in routes], span)]
    update_ref[...] = finish(left_ref, right, places, gating_ref, out_gain_ref, out_bias_ref, w_out_ref)


def last_kernel(span, routes, *refs):
    block_refs = refs[: span - 1]
    (
        left_ref,
        gating_ref,
        first_ref,
        norm_gain_ref,
        norm_bias_ref,
        w_b_proj_ref,
        w_b_gate_ref,
        out_gain_ref,
        out_bias_ref,
        w_out_ref,
        update_ref,
        placed_ref,
        result_ref,
        done,
    ) = refs[span - 1 :]
    _, rows, cols, width = block_refs[0].shape
    right = jnp.stack([ref[...] for ref in block_refs])
    right = gated(flat_normed(right, norm_gain_ref, norm_bias_ref), w_b_proj_ref[...], w_b_gate_ref[...])
    right = right.reshape(span - 1, 2, rows, cols, -1)
    places = [place_of(sources, span) for sources in zip(*routes)]
    last = finish(left_ref, right, places[1:], gating_ref, out_gain_ref, out_bias_ref, w_out_ref)
    placed_ref[pl.ds(places[0][0], 1)] = first_ref[...]
    for step in range(span - 1):
        placed_ref[pl.ds(places[step + 1][0], 1)] = last[step : step + 1]
    for row in range(rows):
        parts = [placed_ref[place, row * rows : (row + 1) * rows] for place in range(span)]
        result_ref[row] = jnp.concatenate(parts, axis=0).astype(jnp.bfloat16)
    copy = pltpu.make_async_copy(result_ref, update_ref, done)
    copy.start()
    copy.wait()


def gather_span(
    routes,
    pair_rep,
    norm_gain,
    norm_bias,
    w_a_proj,
    w_a_gate,
    w_b_proj,
    w_b_gate,
    w_gate,
    out_gain,
    out_bias,
    w_out,
):
    span = len(routes[0])
    block = pair_rep.shape
    rows, _, width = block
    params = pltpu.CompilerParams(vmem_limit_bytes=KERNEL_BYTES)
    cost = pl.CostEstimate(flops=10**8, bytes_accessed=10**6, transcendentals=0)

    def receive(values, sources):
        devices = 4 * span
        pairs = [
            (group * devices + source, group * devices + device)
            for group, table in enumerate(sources)
            for device, source in enumerate(table)
        ]
        return lax.ppermute(values, ("grp", "row", "sub"), pairs)

    swap = [device ^ 1 for device in range(4 * span)]
    other = receive(pair_rep, [swap] * len(routes))
    own = pl.pallas_call(
        copy_kernel,
        out_shape=jax.ShapeDtypeStruct(block, pair_rep.dtype),
        cost_estimate=cost,
        compiler_params=params,
    )(pair_rep)
    pair = jnp.stack([own, other])
    blocks = [receive(pair, sources) for sources in zip(*routes)]
    norm = (norm_gain[None], norm_bias[None])
    tail = (w_b_proj, w_b_gate, out_gain[None], out_bias[None], w_out)
    left, gating = pl.pallas_call(
        functools.partial(left_kernel, span),
        out_shape=(
            jax.ShapeDtypeStruct((2,) + block, jnp.float32),
            jax.ShapeDtypeStruct((span, rows * rows, width), jnp.float32),
        ),
        cost_estimate=cost,
        compiler_params=params,
    )(own, other, *norm, w_a_proj, w_a_gate, w_gate, *tail)
    update = pl.pallas_call(
        functools.partial(first_kernel, span, routes),
        out_shape=jax.ShapeDtypeStruct((1, rows * rows, width), jnp.float32),
        cost_estimate=cost,
        compiler_params=params,
    )(blocks[0], left, gating, *norm, *tail)
    return pl.pallas_call(
        functools.partial(last_kernel, span, routes),
        out_shape=jax.ShapeDtypeStruct(block, pair_rep.dtype),
        out_specs=pl.BlockSpec(memory_space=pl.ANY),
        scratch_shapes=[
            pltpu.VMEM((span, rows * rows, width), jnp.float32),
            pltpu.VMEM(block, pair_rep.dtype),
            pltpu.SemaphoreType.DMA,
        ],
        compiler_params=params,
    )(*blocks[1:], left, gating, update, *norm, *tail)


def exchange_channels(
    pair_rep,
    norm_gain,
    norm_bias,
    w_a_proj,
    w_a_gate,
    w_b_proj,
    w_b_gate,
    w_gate,
    out_gain,
    out_bias,
    w_out,
):
    hidden = w_a_proj.shape[1]
    w_inner = jnp.concatenate([w_a_proj, w_a_gate, w_b_proj, w_b_gate], axis=1)
    normed = layer_norm(pair_rep.astype(jnp.float32), norm_gain, norm_bias, -1).astype(jnp.bfloat16)
    inner = jnp.einsum("rkc,cm->mrk", normed, w_inner, preferred_element_type=jnp.float32)
    left_local = (jax.nn.sigmoid(inner[hidden : 2 * hidden]) * inner[:hidden]).astype(jnp.bfloat16)
    right_local = (
        jax.nn.sigmoid(inner[3 * hidden : 4 * hidden]) * inner[2 * hidden : 3 * hidden]
    ).astype(jnp.bfloat16)
    gating = jax.nn.sigmoid(
        jnp.einsum("rkc,cd->rkd", normed, w_gate, preferred_element_type=jnp.float32)
    ).astype(jnp.bfloat16)
    left_chan, right_chan = (
        lax.all_to_all(left_local, "row", split_axis=0, concat_axis=1, tiled=True),
        lax.all_to_all(right_local, "row", split_axis=0, concat_axis=1, tiled=True),
    )
    left_rows = lax.all_to_all(left_chan, "sub", split_axis=1, concat_axis=2, tiled=True)
    triangle = jnp.einsum(
        "hik,hjk->hij",
        left_rows,
        lax.all_gather(right_chan, "sub", axis=2, tiled=True),
        preferred_element_type=jnp.float32,
    ).astype(jnp.bfloat16)
    regrouped = lax.all_to_all(
        lax.all_to_all(triangle, "sub", split_axis=2, concat_axis=1, tiled=True),
        "row",
        split_axis=1,
        concat_axis=0,
        tiled=True,
    )
    hidden_normed = layer_norm(
        regrouped.astype(jnp.float32), out_gain[:, None, None], out_bias[:, None, None], 0
    ).astype(jnp.bfloat16)
    mixed = jnp.einsum("hrj,hc->rjc", hidden_normed, w_out, preferred_element_type=jnp.float32)
    return (gating.astype(jnp.float32) * mixed).astype(jnp.bfloat16)


def solution(mesh):
    n_row, n_sub = mesh.shape["row"], mesh.shape["sub"]

    def per_device(pair_rep, *weights):
        rows, cols, _ = pair_rep.shape
        gathered = n_row * n_sub * pair_rep.size * pair_rep.dtype.itemsize
        routed = (mesh.shape["grp"], n_row, n_sub) == (2, 8, 2) and cols == n_row // 2 * rows
        if routed and gathered <= GATHER_BYTES:
            return gather_span(ROUTES, pair_rep, *weights)
        return exchange_channels(pair_rep, *weights)

    in_specs = (P(("grp", "row"), "sub", None), P(), P(), P(), P(), P(), P(), P(), P(), P(), P())
    out_specs = P(("grp", "row"), "sub", None)
    return jax.shard_map(
        per_device, mesh=mesh, in_specs=in_specs, out_specs=out_specs, check_vma=False
    )
```

```python
import functools

import jax
import jax.numpy as jnp
from jax import lax
from jax.experimental import pallas as pl
from jax.experimental.pallas import tpu as pltpu
from jax.sharding import PartitionSpec as P

EPSILON = 1e-05
GATHER_BYTES = 2 * 1024 * 1024
KERNEL_BYTES = 4 * 1024 * 1024
ROUTES = (
    (
        (4, 10, 1, 9, 3, 15, 0, 8, 2, 11, 6, 13, 7, 14, 5, 12),
        (7, 15, 4, 13, 1, 9, 3, 11, 6, 8, 0, 14, 5, 12, 2, 10),
        (3, 12, 6, 15, 5, 11, 7, 13, 1, 14, 4, 8, 2, 10, 0, 9),
        (1, 9, 3, 11, 6, 13, 5, 15, 4, 12, 2, 10, 0, 8, 7, 14),
    ),
    (
        (5, 12, 1, 13, 3, 15, 0, 9, 2, 8, 6, 10, 4, 11, 7, 14),
        (7, 15, 3, 8, 6, 10, 4, 11, 1, 14, 2, 13, 0, 12, 5, 9),
        (3, 11, 4, 15, 5, 9, 7, 13, 6, 10, 1, 8, 2, 14, 0, 12),
        (1, 9, 7, 11, 0, 13, 2, 14, 5, 12, 4, 15, 6, 8, 3, 10),
    ),
)


def layer_norm(values, gain, shift, axis):
    centred = values - jnp.mean(values, axis=axis, keepdims=True)
    variance = jnp.mean(centred * centred, axis=axis, keepdims=True)
    return centred * lax.rsqrt(variance + EPSILON) * gain + shift


def gated(rows, w_proj, w_gate):
    proj = jnp.dot(rows, w_proj, preferred_element_type=jnp.float32)
    gate = jnp.dot(rows, w_gate, preferred_element_type=jnp.float32)
    return (jax.nn.sigmoid(gate) * proj).astype(jnp.bfloat16).astype(jnp.float32)


def lookup(tables, bits):
    words = []
    for values in tables:
        word = sum(value << (bits * place) for place, value in enumerate(values))
        words.append(jnp.int32(word - (1 << 32) if word >> 31 else word))
    word = jnp.where(lax.axis_index("grp") == 0, *words)
    device = lax.axis_index("row") * 2 + lax.axis_index("sub")
    return lax.shift_right_logical(word, device * bits) & ((1 << bits) - 1)


def place_of(sources, span):
    place = lookup([[source // 2 % span for source in table] for table in sources], 2)
    return place, lookup([[source % 2 for source in table] for table in sources], 1)


def copy_kernel(source_ref, target_ref):
    target_ref[...] = source_ref[...]


def flat_normed(values, gain_ref, bias_ref):
    flat = values.reshape(-1, values.shape[-1]).astype(jnp.float32)
    return layer_norm(flat, gain_ref[...], bias_ref[...], -1).astype(jnp.bfloat16)


def finish(left_ref, blocks, places, gating_ref, out_gain_ref, out_bias_ref, w_out_ref):
    sums, gates = [], []
    for block, (place, half) in zip(blocks, places):
        left = left_ref[half], left_ref[1 - half]
        for row in range(left_ref.shape[1]):
            products = block[0] * left[0][row] + block[1] * left[1][row]
            sums.append(jnp.sum(products, axis=1))
        gates.append(gating_ref[place])
    triangle = jnp.concatenate(sums, axis=0).astype(jnp.bfloat16).astype(jnp.float32)
    hidden_normed = layer_norm(triangle, out_gain_ref[...], out_bias_ref[...], -1)
    mixed = jnp.dot(
        hidden_normed.astype(jnp.bfloat16), w_out_ref[...], preferred_element_type=jnp.float32
    )
    return (jnp.concatenate(gates, axis=0) * mixed).reshape(len(gates), -1, mixed.shape[-1])


def left_kernel(
    span,
    own_ref,
    other_ref,
    norm_gain_ref,
    norm_bias_ref,
    w_a_proj_ref,
    w_a_gate_ref,
    w_gate_ref,
    w_b_proj_ref,
    w_b_gate_ref,
    out_gain_ref,
    out_bias_ref,
    w_out_ref,
    left_ref,
    gating_ref,
):
    rows, cols, width = own_ref.shape
    sub = lax.axis_index("sub")
    own = flat_normed(own_ref[...], norm_gain_ref, norm_bias_ref)
    other = flat_normed(other_ref[...], norm_gain_ref, norm_bias_ref)
    for values, half in ((own, sub), (other, 1 - sub)):
        left = gated(values, w_a_proj_ref[...], w_a_gate_ref[...])
        left_ref[pl.ds(half, 1)] = left.reshape(1, rows, cols, -1)
    gating = jax.nn.sigmoid(jnp.dot(own, w_gate_ref[...], preferred_element_type=jnp.float32))
    gating = gating.astype(jnp.bfloat16).astype(jnp.float32).reshape(rows, cols, width)
    for place in range(span):
        part = gating[:, place * rows : (place + 1) * rows]
        gating_ref[place] = part.reshape(rows * rows, width)


def first_kernel(
    span,
    routes,
    block_ref,
    left_ref,
    gating_ref,
    norm_gain_ref,
    norm_bias_ref,
    w_b_proj_ref,
    w_b_gate_ref,
    out_gain_ref,
    out_bias_ref,
    w_out_ref,
    update_ref,
):
    _, rows, cols, _ = block_ref.shape
    right = flat_normed(block_ref[...], norm_gain_ref, norm_bias_ref)
    right = gated(right, w_b_proj_ref[...], w_b_gate_ref[...]).reshape(1, 2, rows, cols, -1)
    places = [place_of([table[0] for table in routes], span)]
    update_ref[...] = finish(left_ref, right, places, gating_ref, out_gain_ref, out_bias_ref, w_out_ref)


def last_kernel(span, routes, *refs):
    block_refs = refs[: span - 1]
    (
        left_ref,
        gating_ref,
        first_ref,
        norm_gain_ref,
        norm_bias_ref,
        w_b_proj_ref,
        w_b_gate_ref,
        out_gain_ref,
        out_bias_ref,
        w_out_ref,
        update_ref,
        placed_ref,
        result_ref,
        done,
    ) = refs[span - 1 :]
    _, rows, cols, width = block_refs[0].shape
    right = jnp.stack([ref[...] for ref in block_refs])
    right = gated(flat_normed(right, norm_gain_ref, norm_bias_ref), w_b_proj_ref[...], w_b_gate_ref[...])
    right = right.reshape(span - 1, 2, rows, cols, -1)
    places = [place_of(sources, span) for sources in zip(*routes)]
    last = finish(left_ref, right, places[1:], gating_ref, out_gain_ref, out_bias_ref, w_out_ref)
    placed_ref[pl.ds(places[0][0], 1)] = first_ref[...]
    for step in range(span - 1):
        placed_ref[pl.ds(places[step + 1][0], 1)] = last[step : step + 1]
    for row in range(rows):
        parts = [placed_ref[place, row * rows : (row + 1) * rows] for place in range(span)]
        result_ref[row] = jnp.concatenate(parts, axis=0).astype(jnp.bfloat16)
    copy = pltpu.make_async_copy(result_ref, update_ref, done)
    copy.start()
    copy.wait()


def gather_span(
    routes,
    pair_rep,
    norm_gain,
    norm_bias,
    w_a_proj,
    w_a_gate,
    w_b_proj,
    w_b_gate,
    w_gate,
    out_gain,
    out_bias,
    w_out,
):
    span = len(routes[0])
    block = pair_rep.shape
    rows, _, width = block
    params = pltpu.CompilerParams(vmem_limit_bytes=KERNEL_BYTES)
    cost = pl.CostEstimate(flops=10**8, bytes_accessed=10**6, transcendentals=0)

    def receive(values, sources):
        devices = 4 * span
        pairs = [
            (group * devices + source, group * devices + device)
            for group, table in enumerate(sources)
            for device, source in enumerate(table)
        ]
        return lax.ppermute(values, ("grp", "row", "sub"), pairs)

    swap = [device ^ 1 for device in range(4 * span)]
    other = receive(pair_rep, [swap] * len(routes))
    own = pl.pallas_call(
        copy_kernel,
        out_shape=jax.ShapeDtypeStruct(block, pair_rep.dtype),
        cost_estimate=cost,
        compiler_params=params,
    )(pair_rep)
    pair = jnp.stack([own, other])
    blocks = [receive(pair, sources) for sources in zip(*routes)]
    norm = (norm_gain[None], norm_bias[None])
    tail = (w_b_proj, w_b_gate, out_gain[None], out_bias[None], w_out)
    left, gating = pl.pallas_call(
        functools.partial(left_kernel, span),
        out_shape=(
            jax.ShapeDtypeStruct((2,) + block, jnp.float32),
            jax.ShapeDtypeStruct((span, rows * rows, width), jnp.float32),
        ),
        cost_estimate=cost,
        compiler_params=params,
    )(own, other, *norm, w_a_proj, w_a_gate, w_gate, *tail)
    update = pl.pallas_call(
        functools.partial(first_kernel, span, routes),
        out_shape=jax.ShapeDtypeStruct((1, rows * rows, width), jnp.float32),
        cost_estimate=cost,
        compiler_params=params,
    )(blocks[0], left, gating, *norm, *tail)
    return pl.pallas_call(
        functools.partial(last_kernel, span, routes),
        out_shape=jax.ShapeDtypeStruct(block, pair_rep.dtype),
        out_specs=pl.BlockSpec(memory_space=pl.ANY),
        scratch_shapes=[
            pltpu.VMEM((span, rows * rows, width), jnp.float32),
            pltpu.VMEM(block, pair_rep.dtype),
            pltpu.SemaphoreType.DMA,
        ],
        compiler_params=params,
    )(*blocks[1:], left, gating, update, *norm, *tail)


def exchange_channels(
    pair_rep,
    norm_gain,
    norm_bias,
    w_a_proj,
    w_a_gate,
    w_b_proj,
    w_b_gate,
    w_gate,
    out_gain,
    out_bias,
    w_out,
):
    hidden = w_a_proj.shape[1]
    w_inner = jnp.concatenate([w_a_proj, w_a_gate, w_b_proj, w_b_gate], axis=1)
    normed = layer_norm(pair_rep.astype(jnp.float32), norm_gain, norm_bias, -1).astype(jnp.bfloat16)
    inner = jnp.einsum("rkc,cm->mrk", normed, w_inner, preferred_element_type=jnp.float32)
    left_local = (jax.nn.sigmoid(inner[hidden : 2 * hidden]) * inner[:hidden]).astype(jnp.bfloat16)
    right_local = (
        jax.nn.sigmoid(inner[3 * hidden : 4 * hidden]) * inner[2 * hidden : 3 * hidden]
    ).astype(jnp.bfloat16)
    gating = jax.nn.sigmoid(
        jnp.einsum("rkc,cd->rkd", normed, w_gate, preferred_element_type=jnp.float32)
    ).astype(jnp.bfloat16)
    left_chan, right_chan = (
        lax.all_to_all(left_local, "row", split_axis=0, concat_axis=1, tiled=True),
        lax.all_to_all(right_local, "row", split_axis=0, concat_axis=1, tiled=True),
    )
    left_rows = lax.all_to_all(left_chan, "sub", split_axis=1, concat_axis=2, tiled=True)
    triangle = jnp.einsum(
        "hik,hjk->hij",
        left_rows,
        lax.all_gather(right_chan, "sub", axis=2, tiled=True),
        preferred_element_type=jnp.float32,
    ).astype(jnp.bfloat16)
    regrouped = lax.all_to_all(
        lax.all_to_all(triangle, "sub", split_axis=2, concat_axis=1, tiled=True),
        "row",
        split_axis=1,
        concat_axis=0,
        tiled=True,
    )
    hidden_normed = layer_norm(
        regrouped.astype(jnp.float32), out_gain[:, None, None], out_bias[:, None, None], 0
    ).astype(jnp.bfloat16)
    mixed = jnp.einsum("hrj,hc->rjc", hidden_normed, w_out, preferred_element_type=jnp.float32)
    return (gating.astype(jnp.float32) * mixed).astype(jnp.bfloat16)


def solution(mesh):
    n_row, n_sub = mesh.shape["row"], mesh.shape["sub"]

    def per_device(pair_rep, *weights):
        rows, cols, _ = pair_rep.shape
        gathered = n_row * n_sub * pair_rep.size * pair_rep.dtype.itemsize
        routed = (mesh.shape["grp"], n_row, n_sub) == (2, 8, 2) and cols == n_row // 2 * rows
        if routed and gathered <= GATHER_BYTES:
            return gather_span(ROUTES, pair_rep, *weights)
        return exchange_channels(pair_rep, *weights)

    in_specs = (P(("grp", "row"), "sub", None), P(), P(), P(), P(), P(), P(), P(), P(), P(), P())
    out_specs = P(("grp", "row"), "sub", None)
    return jax.shard_map(
        per_device, mesh=mesh, in_specs=in_specs, out_specs=out_specs, check_vma=False
    )
```

```python
import functools

import jax
import jax.numpy as jnp
from jax import lax
from jax.experimental import pallas as pl
from jax.experimental.pallas import tpu as pltpu
from jax.sharding import PartitionSpec as P

EPSILON = 1e-05
GATHER_BYTES = 2 * 1024 * 1024
KERNEL_BYTES = 4 * 1024 * 1024
ROUTES = (
    (
        (4, 14, 1, 8, 3, 9, 0, 15, 7, 11, 5, 10, 6, 12, 2, 13),
        (7, 12, 6, 13, 1, 15, 4, 9, 2, 8, 3, 14, 0, 11, 5, 10),
        (3, 10, 4, 15, 5, 11, 7, 13, 1, 12, 6, 8, 2, 9, 0, 14),
        (1, 9, 3, 11, 7, 13, 2, 10, 5, 15, 0, 12, 4, 14, 6, 8),
    ),
    (
        (5, 12, 1, 13, 3, 15, 0, 9, 2, 8, 6, 10, 4, 11, 7, 14),
        (7, 15, 3, 8, 6, 10, 4, 11, 1, 14, 2, 13, 0, 12, 5, 9),
        (3, 11, 4, 15, 5, 9, 7, 13, 6, 10, 1, 8, 2, 14, 0, 12),
        (1, 9, 7, 11, 0, 13, 2, 14, 5, 12, 4, 15, 6, 8, 3, 10),
    ),
)


def layer_norm(values, gain, shift, axis):
    centred = values - jnp.mean(values, axis=axis, keepdims=True)
    variance = jnp.mean(centred * centred, axis=axis, keepdims=True)
    return centred * lax.rsqrt(variance + EPSILON) * gain + shift


def gated(rows, w_proj, w_gate):
    proj = jnp.dot(rows, w_proj, preferred_element_type=jnp.float32)
    gate = jnp.dot(rows, w_gate, preferred_element_type=jnp.float32)
    return (jax.nn.sigmoid(gate) * proj).astype(jnp.bfloat16).astype(jnp.float32)


def lookup(tables, bits):
    words = []
    for values in tables:
        word = sum(value << (bits * place) for place, value in enumerate(values))
        words.append(jnp.int32(word - (1 << 32) if word >> 31 else word))
    word = jnp.where(lax.axis_index("grp") == 0, *words)
    device = lax.axis_index("row") * 2 + lax.axis_index("sub")
    return lax.shift_right_logical(word, device * bits) & ((1 << bits) - 1)


def place_of(sources, span):
    place = lookup([[source // 2 % span for source in table] for table in sources], 2)
    return place, lookup([[source % 2 for source in table] for table in sources], 1)


def copy_kernel(source_ref, target_ref):
    target_ref[...] = source_ref[...]


def flat_normed(values, gain_ref, bias_ref):
    flat = values.reshape(-1, values.shape[-1]).astype(jnp.float32)
    return layer_norm(flat, gain_ref[...], bias_ref[...], -1).astype(jnp.bfloat16)


def finish(left_ref, blocks, places, gating_ref, out_gain_ref, out_bias_ref, w_out_ref):
    sums, gates = [], []
    for block, (place, half) in zip(blocks, places):
        left = left_ref[half], left_ref[1 - half]
        for row in range(left_ref.shape[1]):
            products = block[0] * left[0][row] + block[1] * left[1][row]
            sums.append(jnp.sum(products, axis=1))
        gates.append(gating_ref[place])
    triangle = jnp.concatenate(sums, axis=0).astype(jnp.bfloat16).astype(jnp.float32)
    hidden_normed = layer_norm(triangle, out_gain_ref[...], out_bias_ref[...], -1)
    mixed = jnp.dot(
        hidden_normed.astype(jnp.bfloat16), w_out_ref[...], preferred_element_type=jnp.float32
    )
    return (jnp.concatenate(gates, axis=0) * mixed).reshape(len(gates), -1, mixed.shape[-1])


def left_kernel(
    span,
    own_ref,
    other_ref,
    norm_gain_ref,
    norm_bias_ref,
    w_a_proj_ref,
    w_a_gate_ref,
    w_gate_ref,
    w_b_proj_ref,
    w_b_gate_ref,
    out_gain_ref,
    out_bias_ref,
    w_out_ref,
    left_ref,
    gating_ref,
):
    rows, cols, width = own_ref.shape
    sub = lax.axis_index("sub")
    own = flat_normed(own_ref[...], norm_gain_ref, norm_bias_ref)
    other = flat_normed(other_ref[...], norm_gain_ref, norm_bias_ref)
    for values, half in ((own, sub), (other, 1 - sub)):
        left = gated(values, w_a_proj_ref[...], w_a_gate_ref[...])
        left_ref[pl.ds(half, 1)] = left.reshape(1, rows, cols, -1)
    gating = jax.nn.sigmoid(jnp.dot(own, w_gate_ref[...], preferred_element_type=jnp.float32))
    gating = gating.astype(jnp.bfloat16).astype(jnp.float32).reshape(rows, cols, width)
    for place in range(span):
        part = gating[:, place * rows : (place + 1) * rows]
        gating_ref[place] = part.reshape(rows * rows, width)


def first_kernel(
    span,
    routes,
    block_ref,
    left_ref,
    gating_ref,
    norm_gain_ref,
    norm_bias_ref,
    w_b_proj_ref,
    w_b_gate_ref,
    out_gain_ref,
    out_bias_ref,
    w_out_ref,
    update_ref,
):
    _, rows, cols, _ = block_ref.shape
    right = flat_normed(block_ref[...], norm_gain_ref, norm_bias_ref)
    right = gated(right, w_b_proj_ref[...], w_b_gate_ref[...]).reshape(1, 2, rows, cols, -1)
    places = [place_of([table[0] for table in routes], span)]
    update_ref[...] = finish(left_ref, right, places, gating_ref, out_gain_ref, out_bias_ref, w_out_ref)


def last_kernel(span, routes, *refs):
    block_refs = refs[: span - 1]
    (
        left_ref,
        gating_ref,
        first_ref,
        norm_gain_ref,
        norm_bias_ref,
        w_b_proj_ref,
        w_b_gate_ref,
        out_gain_ref,
        out_bias_ref,
        w_out_ref,
        update_ref,
        placed_ref,
        result_ref,
        done,
    ) = refs[span - 1 :]
    _, rows, cols, width = block_refs[0].shape
    right = jnp.stack([ref[...] for ref in block_refs])
    right = gated(flat_normed(right, norm_gain_ref, norm_bias_ref), w_b_proj_ref[...], w_b_gate_ref[...])
    right = right.reshape(span - 1, 2, rows, cols, -1)
    places = [place_of(sources, span) for sources in zip(*routes)]
    last = finish(left_ref, right, places[1:], gating_ref, out_gain_ref, out_bias_ref, w_out_ref)
    placed_ref[pl.ds(places[0][0], 1)] = first_ref[...]
    for step in range(span - 1):
        placed_ref[pl.ds(places[step + 1][0], 1)] = last[step : step + 1]
    for row in range(rows):
        parts = [placed_ref[place, row * rows : (row + 1) * rows] for place in range(span)]
        result_ref[row] = jnp.concatenate(parts, axis=0).astype(jnp.bfloat16)
    copy = pltpu.make_async_copy(result_ref, update_ref, done)
    copy.start()
    copy.wait()


def gather_span(
    routes,
    pair_rep,
    norm_gain,
    norm_bias,
    w_a_proj,
    w_a_gate,
    w_b_proj,
    w_b_gate,
    w_gate,
    out_gain,
    out_bias,
    w_out,
):
    span = len(routes[0])
    block = pair_rep.shape
    rows, _, width = block
    params = pltpu.CompilerParams(vmem_limit_bytes=KERNEL_BYTES)
    cost = pl.CostEstimate(flops=10**8, bytes_accessed=10**6, transcendentals=0)

    def receive(values, sources):
        devices = 4 * span
        pairs = [
            (group * devices + source, group * devices + device)
            for group, table in enumerate(sources)
            for device, source in enumerate(table)
        ]
        return lax.ppermute(values, ("grp", "row", "sub"), pairs)

    swap = [device ^ 1 for device in range(4 * span)]
    other = receive(pair_rep, [swap] * len(routes))
    own = pl.pallas_call(
        copy_kernel,
        out_shape=jax.ShapeDtypeStruct(block, pair_rep.dtype),
        cost_estimate=cost,
        compiler_params=params,
    )(pair_rep)
    pair = jnp.stack([own, other])
    blocks = [receive(pair, sources) for sources in zip(*routes)]
    norm = (norm_gain[None], norm_bias[None])
    tail = (w_b_proj, w_b_gate, out_gain[None], out_bias[None], w_out)
    left, gating = pl.pallas_call(
        functools.partial(left_kernel, span),
        out_shape=(
            jax.ShapeDtypeStruct((2,) + block, jnp.float32),
            jax.ShapeDtypeStruct((span, rows * rows, width), jnp.float32),
        ),
        cost_estimate=cost,
        compiler_params=params,
    )(own, other, *norm, w_a_proj, w_a_gate, w_gate, *tail)
    update = pl.pallas_call(
        functools.partial(first_kernel, span, routes),
        out_shape=jax.ShapeDtypeStruct((1, rows * rows, width), jnp.float32),
        cost_estimate=cost,
        compiler_params=params,
    )(blocks[0], left, gating, *norm, *tail)
    return pl.pallas_call(
        functools.partial(last_kernel, span, routes),
        out_shape=jax.ShapeDtypeStruct(block, pair_rep.dtype),
        out_specs=pl.BlockSpec(memory_space=pl.ANY),
        scratch_shapes=[
            pltpu.VMEM((span, rows * rows, width), jnp.float32),
            pltpu.VMEM(block, pair_rep.dtype),
            pltpu.SemaphoreType.DMA,
        ],
        compiler_params=params,
    )(*blocks[1:], left, gating, update, *norm, *tail)


def exchange_channels(
    pair_rep,
    norm_gain,
    norm_bias,
    w_a_proj,
    w_a_gate,
    w_b_proj,
    w_b_gate,
    w_gate,
    out_gain,
    out_bias,
    w_out,
):
    hidden = w_a_proj.shape[1]
    w_inner = jnp.concatenate([w_a_proj, w_a_gate, w_b_proj, w_b_gate], axis=1)
    normed = layer_norm(pair_rep.astype(jnp.float32), norm_gain, norm_bias, -1).astype(jnp.bfloat16)
    inner = jnp.einsum("rkc,cm->mrk", normed, w_inner, preferred_element_type=jnp.float32)
    left_local = (jax.nn.sigmoid(inner[hidden : 2 * hidden]) * inner[:hidden]).astype(jnp.bfloat16)
    right_local = (
        jax.nn.sigmoid(inner[3 * hidden : 4 * hidden]) * inner[2 * hidden : 3 * hidden]
    ).astype(jnp.bfloat16)
    gating = jax.nn.sigmoid(
        jnp.einsum("rkc,cd->rkd", normed, w_gate, preferred_element_type=jnp.float32)
    ).astype(jnp.bfloat16)
    left_chan, right_chan = (
        lax.all_to_all(left_local, "row", split_axis=0, concat_axis=1, tiled=True),
        lax.all_to_all(right_local, "row", split_axis=0, concat_axis=1, tiled=True),
    )
    left_rows = lax.all_to_all(left_chan, "sub", split_axis=1, concat_axis=2, tiled=True)
    triangle = jnp.einsum(
        "hik,hjk->hij",
        left_rows,
        lax.all_gather(right_chan, "sub", axis=2, tiled=True),
        preferred_element_type=jnp.float32,
    ).astype(jnp.bfloat16)
    regrouped = lax.all_to_all(
        lax.all_to_all(triangle, "sub", split_axis=2, concat_axis=1, tiled=True),
        "row",
        split_axis=1,
        concat_axis=0,
        tiled=True,
    )
    hidden_normed = layer_norm(
        regrouped.astype(jnp.float32), out_gain[:, None, None], out_bias[:, None, None], 0
    ).astype(jnp.bfloat16)
    mixed = jnp.einsum("hrj,hc->rjc", hidden_normed, w_out, preferred_element_type=jnp.float32)
    return (gating.astype(jnp.float32) * mixed).astype(jnp.bfloat16)


def solution(mesh):
    n_row, n_sub = mesh.shape["row"], mesh.shape["sub"]

    def per_device(pair_rep, *weights):
        rows, cols, _ = pair_rep.shape
        gathered = n_row * n_sub * pair_rep.size * pair_rep.dtype.itemsize
        routed = (mesh.shape["grp"], n_row, n_sub) == (2, 8, 2) and cols == n_row // 2 * rows
        if routed and gathered <= GATHER_BYTES:
            return gather_span(ROUTES, pair_rep, *weights)
        return exchange_channels(pair_rep, *weights)

    in_specs = (P(("grp", "row"), "sub", None), P(), P(), P(), P(), P(), P(), P(), P(), P(), P())
    out_specs = P(("grp", "row"), "sub", None)
    return jax.shard_map(
        per_device, mesh=mesh, in_specs=in_specs, out_specs=out_specs, check_vma=False
    )
```

```python
import functools

import jax
import jax.numpy as jnp
from jax import lax
from jax.experimental import pallas as pl
from jax.experimental.pallas import tpu as pltpu
from jax.sharding import PartitionSpec as P

EPSILON = 1e-05
GATHER_BYTES = 2 * 1024 * 1024
KERNEL_BYTES = 4 * 1024 * 1024
ROUTES = (
    (
        (6, 15, 4, 13, 3, 11, 7, 9, 1, 10, 2, 8, 0, 12, 5, 14),
        (5, 13, 3, 9, 0, 15, 1, 14, 7, 8, 4, 10, 2, 11, 6, 12),
        (3, 11, 6, 14, 5, 8, 4, 13, 2, 12, 1, 15, 7, 9, 0, 10),
        (1, 9, 0, 11, 6, 13, 2, 10, 5, 15, 7, 12, 4, 14, 3, 8),
    ),
    (
        (5, 12, 1, 13, 3, 15, 0, 9, 2, 8, 6, 10, 4, 11, 7, 14),
        (7, 15, 3, 8, 6, 10, 4, 11, 1, 14, 2, 13, 0, 12, 5, 9),
        (3, 11, 4, 15, 5, 9, 7, 13, 6, 10, 1, 8, 2, 14, 0, 12),
        (1, 9, 7, 11, 0, 13, 2, 14, 5, 12, 4, 15, 6, 8, 3, 10),
    ),
)


def layer_norm(values, gain, shift, axis):
    centred = values - jnp.mean(values, axis=axis, keepdims=True)
    variance = jnp.mean(centred * centred, axis=axis, keepdims=True)
    return centred * lax.rsqrt(variance + EPSILON) * gain + shift


def gated(rows, w_proj_gate):
    both = jnp.dot(rows, w_proj_gate, preferred_element_type=jnp.float32)
    hidden = both.shape[1] // 2
    return (jax.nn.sigmoid(both[:, hidden:]) * both[:, :hidden]).astype(jnp.bfloat16).astype(jnp.float32)


def lookup(tables, bits):
    words = []
    for values in tables:
        word = sum(value << (bits * place) for place, value in enumerate(values))
        words.append(jnp.int32(word - (1 << 32) if word >> 31 else word))
    word = jnp.where(lax.axis_index("grp") == 0, *words)
    device = lax.axis_index("row") * 2 + lax.axis_index("sub")
    return lax.shift_right_logical(word, device * bits) & ((1 << bits) - 1)


def place_of(sources, span):
    place = lookup([[source // 2 % span for source in table] for table in sources], 2)
    return place, lookup([[source % 2 for source in table] for table in sources], 1)


def copy_kernel(source_ref, target_ref):
    target_ref[...] = source_ref[...]


def flat_normed(values, gain, bias):
    flat = values.reshape(-1, values.shape[-1]).astype(jnp.float32)
    return layer_norm(flat, gain, bias, -1).astype(jnp.bfloat16)


def finish(left_ref, blocks, places, gating_ref, vectors_ref, w_out_ref):
    sums, gates = [], []
    for block, (place, half) in zip(blocks, places):
        left = left_ref[half], left_ref[1 - half]
        for row in range(left_ref.shape[1]):
            products = block[0] * left[0][row] + block[1] * left[1][row]
            sums.append(jnp.sum(products, axis=1))
        gates.append(gating_ref[place])
    triangle = jnp.concatenate(sums, axis=0).astype(jnp.bfloat16).astype(jnp.float32)
    hidden_normed = layer_norm(triangle, vectors_ref[2:3], vectors_ref[3:4], -1)
    mixed = jnp.dot(
        hidden_normed.astype(jnp.bfloat16), w_out_ref[...], preferred_element_type=jnp.float32
    )
    return (jnp.concatenate(gates, axis=0) * mixed).reshape(len(gates), -1, mixed.shape[-1])


def left_kernel(
    span,
    own_ref,
    other_ref,
    norm_gain_ref,
    norm_bias_ref,
    w_a_proj_ref,
    w_a_gate_ref,
    w_gate_ref,
    w_b_proj_ref,
    w_b_gate_ref,
    out_gain_ref,
    out_bias_ref,
    w_out_ref,
    left_ref,
    gating_ref,
    vectors_ref,
    w_right_ref,
):
    rows, cols, width = own_ref.shape
    for place, ref in enumerate((norm_gain_ref, norm_bias_ref, out_gain_ref, out_bias_ref)):
        vectors_ref[place : place + 1] = ref[...]
    w_right_ref[:, :width] = w_b_proj_ref[...]
    w_right_ref[:, width:] = w_b_gate_ref[...]
    sub = lax.axis_index("sub")
    gain, bias = norm_gain_ref[...], norm_bias_ref[...]
    own, other = flat_normed(own_ref[...], gain, bias), flat_normed(other_ref[...], gain, bias)
    w_left = jnp.concatenate([w_a_proj_ref[...], w_a_gate_ref[...]], axis=1)
    for values, half in ((own, sub), (other, 1 - sub)):
        left_ref[pl.ds(half, 1)] = gated(values, w_left).reshape(1, rows, cols, -1)
    gating = jax.nn.sigmoid(jnp.dot(own, w_gate_ref[...], preferred_element_type=jnp.float32))
    gating = gating.astype(jnp.bfloat16).astype(jnp.float32).reshape(rows, cols, width)
    for place in range(span):
        part = gating[:, place * rows : (place + 1) * rows]
        gating_ref[place] = part.reshape(rows * rows, width)


def first_kernel(
    span,
    routes,
    block_ref,
    left_ref,
    gating_ref,
    vectors_ref,
    w_right_ref,
    w_out_ref,
    update_ref,
):
    _, rows, cols, _ = block_ref.shape
    right = flat_normed(block_ref[...], vectors_ref[0:1], vectors_ref[1:2])
    right = gated(right, w_right_ref[...]).reshape(1, 2, rows, cols, -1)
    places = [place_of([table[0] for table in routes], span)]
    update_ref[...] = finish(left_ref, right, places, gating_ref, vectors_ref, w_out_ref)


def last_kernel(span, routes, *refs):
    block_refs = refs[: span - 1]
    (
        left_ref,
        gating_ref,
        first_ref,
        vectors_ref,
        w_right_ref,
        w_out_ref,
        update_ref,
        placed_ref,
        result_ref,
        done,
    ) = refs[span - 1 :]
    _, rows, cols, width = block_refs[0].shape
    right = jnp.stack([ref[...] for ref in block_refs])
    right = gated(flat_normed(right, vectors_ref[0:1], vectors_ref[1:2]), w_right_ref[...])
    right = right.reshape(span - 1, 2, rows, cols, -1)
    places = [place_of(sources, span) for sources in zip(*routes)]
    last = finish(left_ref, right, places[1:], gating_ref, vectors_ref, w_out_ref)
    placed_ref[pl.ds(places[0][0], 1)] = first_ref[...]
    for step in range(span - 1):
        placed_ref[pl.ds(places[step + 1][0], 1)] = last[step : step + 1]
    for row in range(rows):
        parts = [placed_ref[place, row * rows : (row + 1) * rows] for place in range(span)]
        result_ref[row] = jnp.concatenate(parts, axis=0).astype(jnp.bfloat16)
    copy = pltpu.make_async_copy(result_ref, update_ref, done)
    copy.start()
    copy.wait()


def gather_span(
    routes,
    pair_rep,
    norm_gain,
    norm_bias,
    w_a_proj,
    w_a_gate,
    w_b_proj,
    w_b_gate,
    w_gate,
    out_gain,
    out_bias,
    w_out,
):
    span = len(routes[0])
    block = pair_rep.shape
    rows, _, width = block
    params = pltpu.CompilerParams(vmem_limit_bytes=KERNEL_BYTES)
    cost = pl.CostEstimate(flops=10**8, bytes_accessed=10**6, transcendentals=0)

    def receive(values, sources):
        devices = 4 * span
        pairs = [
            (group * devices + source, group * devices + device)
            for group, table in enumerate(sources)
            for device, source in enumerate(table)
        ]
        return lax.ppermute(values, ("grp", "row", "sub"), pairs)

    swap = [device ^ 1 for device in range(4 * span)]
    other = receive(pair_rep, [swap] * len(routes))
    own = pl.pallas_call(
        copy_kernel,
        out_shape=jax.ShapeDtypeStruct(block, pair_rep.dtype),
        cost_estimate=cost,
        compiler_params=params,
    )(pair_rep)
    pair = jnp.stack([own, other])
    blocks = [receive(pair, sources) for sources in zip(*routes)]
    norm = (norm_gain[None], norm_bias[None])
    tail = (w_b_proj, w_b_gate, out_gain[None], out_bias[None], w_out)
    left, gating, vectors, w_right = pl.pallas_call(
        functools.partial(left_kernel, span),
        out_shape=(
            jax.ShapeDtypeStruct((2,) + block, jnp.float32),
            jax.ShapeDtypeStruct((span, rows * rows, width), jnp.float32),
            jax.ShapeDtypeStruct((4, width), jnp.float32),
            jax.ShapeDtypeStruct((width, 2 * width), w_b_proj.dtype),
        ),
        cost_estimate=cost,
        compiler_params=params,
    )(own, other, *norm, w_a_proj, w_a_gate, w_gate, *tail)
    update = pl.pallas_call(
        functools.partial(first_kernel, span, routes),
        out_shape=jax.ShapeDtypeStruct((1, rows * rows, width), jnp.float32),
        cost_estimate=cost,
        compiler_params=params,
    )(blocks[0], left, gating, vectors, w_right, w_out)
    return pl.pallas_call(
        functools.partial(last_kernel, span, routes),
        out_shape=jax.ShapeDtypeStruct(block, pair_rep.dtype),
        out_specs=pl.BlockSpec(memory_space=pl.ANY),
        scratch_shapes=[
            pltpu.VMEM((span, rows * rows, width), jnp.float32),
            pltpu.VMEM(block, pair_rep.dtype),
            pltpu.SemaphoreType.DMA,
        ],
        compiler_params=params,
    )(*blocks[1:], left, gating, update, vectors, w_right, w_out)


def exchange_channels(
    pair_rep,
    norm_gain,
    norm_bias,
    w_a_proj,
    w_a_gate,
    w_b_proj,
    w_b_gate,
    w_gate,
    out_gain,
    out_bias,
    w_out,
):
    hidden = w_a_proj.shape[1]
    w_inner = jnp.concatenate([w_a_proj, w_a_gate, w_b_proj, w_b_gate], axis=1)
    normed = layer_norm(pair_rep.astype(jnp.float32), norm_gain, norm_bias, -1).astype(jnp.bfloat16)
    inner = jnp.einsum("rkc,cm->mrk", normed, w_inner, preferred_element_type=jnp.float32)
    left_local = (jax.nn.sigmoid(inner[hidden : 2 * hidden]) * inner[:hidden]).astype(jnp.bfloat16)
    right_local = (
        jax.nn.sigmoid(inner[3 * hidden : 4 * hidden]) * inner[2 * hidden : 3 * hidden]
    ).astype(jnp.bfloat16)
    gating = jax.nn.sigmoid(
        jnp.einsum("rkc,cd->rkd", normed, w_gate, preferred_element_type=jnp.float32)
    ).astype(jnp.bfloat16)
    left_chan, right_chan = (
        lax.all_to_all(left_local, "row", split_axis=0, concat_axis=1, tiled=True),
        lax.all_to_all(right_local, "row", split_axis=0, concat_axis=1, tiled=True),
    )
    left_rows = lax.all_to_all(left_chan, "sub", split_axis=1, concat_axis=2, tiled=True)
    triangle = jnp.einsum(
        "hik,hjk->hij",
        left_rows,
        lax.all_gather(right_chan, "sub", axis=2, tiled=True),
        preferred_element_type=jnp.float32,
    ).astype(jnp.bfloat16)
    regrouped = lax.all_to_all(
        lax.all_to_all(triangle, "sub", split_axis=2, concat_axis=1, tiled=True),
        "row",
        split_axis=1,
        concat_axis=0,
        tiled=True,
    )
    hidden_normed = layer_norm(
        regrouped.astype(jnp.float32), out_gain[:, None, None], out_bias[:, None, None], 0
    ).astype(jnp.bfloat16)
    mixed = jnp.einsum("hrj,hc->rjc", hidden_normed, w_out, preferred_element_type=jnp.float32)
    return (gating.astype(jnp.float32) * mixed).astype(jnp.bfloat16)


def solution(mesh):
    n_row, n_sub = mesh.shape["row"], mesh.shape["sub"]

    def per_device(pair_rep, *weights):
        rows, cols, _ = pair_rep.shape
        gathered = n_row * n_sub * pair_rep.size * pair_rep.dtype.itemsize
        routed = (mesh.shape["grp"], n_row, n_sub) == (2, 8, 2) and cols == n_row // 2 * rows
        if routed and gathered <= GATHER_BYTES:
            return gather_span(ROUTES, pair_rep, *weights)
        return exchange_channels(pair_rep, *weights)

    in_specs = (P(("grp", "row"), "sub", None), P(), P(), P(), P(), P(), P(), P(), P(), P(), P())
    out_specs = P(("grp", "row"), "sub", None)
    return jax.shard_map(
        per_device, mesh=mesh, in_specs=in_specs, out_specs=out_specs, check_vma=False
    )
```

```python
import functools

import jax
import jax.numpy as jnp
from jax import lax
from jax.experimental import pallas as pl
from jax.experimental.pallas import tpu as pltpu
from jax.sharding import PartitionSpec as P

EPSILON = 1e-05
GATHER_BYTES = 2 * 1024 * 1024
KERNEL_BYTES = 4 * 1024 * 1024
ROUTES = (
    (
        (6, 15, 4, 13, 3, 11, 7, 9, 1, 10, 2, 8, 0, 12, 5, 14),
        (5, 13, 3, 9, 0, 15, 1, 14, 7, 8, 4, 10, 2, 11, 6, 12),
        (3, 11, 6, 14, 5, 8, 4, 13, 2, 12, 1, 15, 7, 9, 0, 10),
        (1, 9, 0, 11, 6, 13, 2, 10, 5, 15, 7, 12, 4, 14, 3, 8),
    ),
    (
        (5, 12, 1, 13, 3, 15, 0, 9, 2, 8, 6, 10, 4, 11, 7, 14),
        (7, 15, 3, 8, 6, 10, 4, 11, 1, 14, 2, 13, 0, 12, 5, 9),
        (3, 11, 4, 15, 5, 9, 7, 13, 6, 10, 1, 8, 2, 14, 0, 12),
        (1, 9, 7, 11, 0, 13, 2, 14, 5, 12, 4, 15, 6, 8, 3, 10),
    ),
)


def layer_norm(values, gain, shift, axis):
    centred = values - jnp.mean(values, axis=axis, keepdims=True)
    variance = jnp.mean(centred * centred, axis=axis, keepdims=True)
    return centred * lax.rsqrt(variance + EPSILON) * gain + shift


def gated(rows, w_proj_gate):
    both = jnp.dot(rows, w_proj_gate, preferred_element_type=jnp.float32)
    hidden = both.shape[1] // 2
    return (jax.nn.sigmoid(both[:, hidden:]) * both[:, :hidden]).astype(jnp.bfloat16).astype(jnp.float32)


def lookup(tables, bits):
    words = []
    for values in tables:
        word = sum(value << (bits * place) for place, value in enumerate(values))
        words.append(jnp.int32(word - (1 << 32) if word >> 31 else word))
    word = jnp.where(lax.axis_index("grp") == 0, *words)
    device = lax.axis_index("row") * 2 + lax.axis_index("sub")
    return lax.shift_right_logical(word, device * bits) & ((1 << bits) - 1)


def place_of(sources, span):
    place = lookup([[source // 2 % span for source in table] for table in sources], 2)
    return place, lookup([[source % 2 for source in table] for table in sources], 1)


def copy_kernel(source_ref, target_ref):
    target_ref[...] = source_ref[...]


def flat_normed(values, gain, bias):
    flat = values.reshape(-1, values.shape[-1]).astype(jnp.float32)
    return layer_norm(flat, gain, bias, -1).astype(jnp.bfloat16)


def finish(left_ref, blocks, places, gating_ref, vectors_ref, w_out_ref):
    sums, gates = [], []
    for block, (place, half) in zip(blocks, places):
        left = left_ref[half], left_ref[1 - half]
        for row in range(left_ref.shape[1]):
            products = block[0] * left[0][row] + block[1] * left[1][row]
            sums.append(jnp.sum(products, axis=1))
        gates.append(gating_ref[place])
    triangle = jnp.concatenate(sums, axis=0).astype(jnp.bfloat16).astype(jnp.float32)
    hidden_normed = layer_norm(triangle, vectors_ref[2:3], vectors_ref[3:4], -1)
    mixed = jnp.dot(
        hidden_normed.astype(jnp.bfloat16), w_out_ref[...], preferred_element_type=jnp.float32
    )
    return (jnp.concatenate(gates, axis=0) * mixed).reshape(len(gates), -1, mixed.shape[-1])


def left_kernel(
    span,
    own_ref,
    other_ref,
    norm_gain_ref,
    norm_bias_ref,
    w_a_proj_ref,
    w_a_gate_ref,
    w_gate_ref,
    w_b_proj_ref,
    w_b_gate_ref,
    out_gain_ref,
    out_bias_ref,
    w_out_ref,
    left_ref,
    gating_ref,
    vectors_ref,
    w_right_ref,
):
    rows, cols, width = own_ref.shape
    for place, ref in enumerate((norm_gain_ref, norm_bias_ref, out_gain_ref, out_bias_ref)):
        vectors_ref[place : place + 1] = ref[...]
    w_right_ref[:, :width] = w_b_proj_ref[...]
    w_right_ref[:, width:] = w_b_gate_ref[...]
    sub = lax.axis_index("sub")
    gain, bias = norm_gain_ref[...], norm_bias_ref[...]
    own, other = flat_normed(own_ref[...], gain, bias), flat_normed(other_ref[...], gain, bias)
    w_left = jnp.concatenate([w_a_proj_ref[...], w_a_gate_ref[...]], axis=1)
    for values, half in ((own, sub), (other, 1 - sub)):
        left_ref[pl.ds(half, 1)] = gated(values, w_left).reshape(1, rows, cols, -1)
    gating = jax.nn.sigmoid(jnp.dot(own, w_gate_ref[...], preferred_element_type=jnp.float32))
    gating = gating.astype(jnp.bfloat16).astype(jnp.float32).reshape(rows, cols, width)
    for place in range(span):
        part = gating[:, place * rows : (place + 1) * rows]
        gating_ref[place] = part.reshape(rows * rows, width)


def first_kernel(
    span,
    routes,
    block_ref,
    left_ref,
    gating_ref,
    vectors_ref,
    w_right_ref,
    w_out_ref,
    update_ref,
):
    _, rows, cols, _ = block_ref.shape
    right = flat_normed(block_ref[...], vectors_ref[0:1], vectors_ref[1:2])
    right = gated(right, w_right_ref[...]).reshape(1, 2, rows, cols, -1)
    places = [place_of([table[0] for table in routes], span)]
    update_ref[...] = finish(left_ref, right, places, gating_ref, vectors_ref, w_out_ref)


def last_kernel(span, routes, *refs):
    block_refs = refs[: span - 1]
    (
        left_ref,
        gating_ref,
        first_ref,
        vectors_ref,
        w_right_ref,
        w_out_ref,
        update_ref,
        placed_ref,
        result_ref,
        done,
    ) = refs[span - 1 :]
    _, rows, cols, width = block_refs[0].shape
    right = jnp.stack([ref[...] for ref in block_refs])
    right = gated(flat_normed(right, vectors_ref[0:1], vectors_ref[1:2]), w_right_ref[...])
    right = right.reshape(span - 1, 2, rows, cols, -1)
    places = [place_of(sources, span) for sources in zip(*routes)]
    last = finish(left_ref, right, places[1:], gating_ref, vectors_ref, w_out_ref)
    parts = [first_ref[0]] + [last[step] for step in range(span - 1)]
    for (place, _), part in zip(places, parts):
        for row in range(rows):
            values = part[row * rows : (row + 1) * rows]
            placed_ref[row, pl.ds(pl.multiple_of(place * rows, rows), rows)] = values
    result_ref[...] = placed_ref[...].astype(jnp.bfloat16)
    copy = pltpu.make_async_copy(result_ref, update_ref, done)
    copy.start()
    copy.wait()


def gather_span(
    routes,
    pair_rep,
    norm_gain,
    norm_bias,
    w_a_proj,
    w_a_gate,
    w_b_proj,
    w_b_gate,
    w_gate,
    out_gain,
    out_bias,
    w_out,
):
    span = len(routes[0])
    block = pair_rep.shape
    rows, _, width = block
    params = pltpu.CompilerParams(vmem_limit_bytes=KERNEL_BYTES)
    cost = pl.CostEstimate(flops=10**8, bytes_accessed=10**6, transcendentals=0)

    def receive(values, sources):
        devices = 4 * span
        pairs = [
            (group * devices + source, group * devices + device)
            for group, table in enumerate(sources)
            for device, source in enumerate(table)
        ]
        return lax.ppermute(values, ("grp", "row", "sub"), pairs)

    swap = [device ^ 1 for device in range(4 * span)]
    other = receive(pair_rep, [swap] * len(routes))
    own = pl.pallas_call(
        copy_kernel,
        out_shape=jax.ShapeDtypeStruct(block, pair_rep.dtype),
        cost_estimate=cost,
        compiler_params=params,
    )(pair_rep)
    pair = jnp.stack([own, other])
    blocks = [receive(pair, sources) for sources in zip(*routes)]
    norm = (norm_gain[None], norm_bias[None])
    tail = (w_b_proj, w_b_gate, out_gain[None], out_bias[None], w_out)
    left, gating, vectors, w_right = pl.pallas_call(
        functools.partial(left_kernel, span),
        out_shape=(
            jax.ShapeDtypeStruct((2,) + block, jnp.float32),
            jax.ShapeDtypeStruct((span, rows * rows, width), jnp.float32),
            jax.ShapeDtypeStruct((4, width), jnp.float32),
            jax.ShapeDtypeStruct((width, 2 * width), w_b_proj.dtype),
        ),
        cost_estimate=cost,
        compiler_params=params,
    )(own, other, *norm, w_a_proj, w_a_gate, w_gate, *tail)
    update = pl.pallas_call(
        functools.partial(first_kernel, span, routes),
        out_shape=jax.ShapeDtypeStruct((1, rows * rows, width), jnp.float32),
        cost_estimate=cost,
        compiler_params=params,
    )(blocks[0], left, gating, vectors, w_right, w_out)
    return pl.pallas_call(
        functools.partial(last_kernel, span, routes),
        out_shape=jax.ShapeDtypeStruct(block, pair_rep.dtype),
        out_specs=pl.BlockSpec(memory_space=pl.ANY),
        scratch_shapes=[
            pltpu.VMEM(block, jnp.float32),
            pltpu.VMEM(block, pair_rep.dtype),
            pltpu.SemaphoreType.DMA,
        ],
        compiler_params=params,
    )(*blocks[1:], left, gating, update, vectors, w_right, w_out)


def exchange_channels(
    pair_rep,
    norm_gain,
    norm_bias,
    w_a_proj,
    w_a_gate,
    w_b_proj,
    w_b_gate,
    w_gate,
    out_gain,
    out_bias,
    w_out,
):
    hidden = w_a_proj.shape[1]
    w_inner = jnp.concatenate([w_a_proj, w_a_gate, w_b_proj, w_b_gate], axis=1)
    normed = layer_norm(pair_rep.astype(jnp.float32), norm_gain, norm_bias, -1).astype(jnp.bfloat16)
    inner = jnp.einsum("rkc,cm->mrk", normed, w_inner, preferred_element_type=jnp.float32)
    left_local = (jax.nn.sigmoid(inner[hidden : 2 * hidden]) * inner[:hidden]).astype(jnp.bfloat16)
    right_local = (
        jax.nn.sigmoid(inner[3 * hidden : 4 * hidden]) * inner[2 * hidden : 3 * hidden]
    ).astype(jnp.bfloat16)
    gating = jax.nn.sigmoid(
        jnp.einsum("rkc,cd->rkd", normed, w_gate, preferred_element_type=jnp.float32)
    ).astype(jnp.bfloat16)
    left_chan, right_chan = (
        lax.all_to_all(left_local, "row", split_axis=0, concat_axis=1, tiled=True),
        lax.all_to_all(right_local, "row", split_axis=0, concat_axis=1, tiled=True),
    )
    left_rows = lax.all_to_all(left_chan, "sub", split_axis=1, concat_axis=2, tiled=True)
    triangle = jnp.einsum(
        "hik,hjk->hij",
        left_rows,
        lax.all_gather(right_chan, "sub", axis=2, tiled=True),
        preferred_element_type=jnp.float32,
    ).astype(jnp.bfloat16)
    regrouped = lax.all_to_all(
        lax.all_to_all(triangle, "sub", split_axis=2, concat_axis=1, tiled=True),
        "row",
        split_axis=1,
        concat_axis=0,
        tiled=True,
    )
    hidden_normed = layer_norm(
        regrouped.astype(jnp.float32), out_gain[:, None, None], out_bias[:, None, None], 0
    ).astype(jnp.bfloat16)
    mixed = jnp.einsum("hrj,hc->rjc", hidden_normed, w_out, preferred_element_type=jnp.float32)
    return (gating.astype(jnp.float32) * mixed).astype(jnp.bfloat16)


def solution(mesh):
    n_row, n_sub = mesh.shape["row"], mesh.shape["sub"]

    def per_device(pair_rep, *weights):
        rows, cols, _ = pair_rep.shape
        gathered = n_row * n_sub * pair_rep.size * pair_rep.dtype.itemsize
        routed = (mesh.shape["grp"], n_row, n_sub) == (2, 8, 2) and cols == n_row // 2 * rows
        if routed and gathered <= GATHER_BYTES:
            return gather_span(ROUTES, pair_rep, *weights)
        return exchange_channels(pair_rep, *weights)

    in_specs = (P(("grp", "row"), "sub", None), P(), P(), P(), P(), P(), P(), P(), P(), P(), P())
    out_specs = P(("grp", "row"), "sub", None)
    return jax.shard_map(
        per_device, mesh=mesh, in_specs=in_specs, out_specs=out_specs, check_vma=False
    )
```

```python
import functools

import jax
import jax.numpy as jnp
from jax import lax
from jax.experimental import pallas as pl
from jax.experimental.pallas import tpu as pltpu
from jax.sharding import PartitionSpec as P

EPSILON = 1e-05
GATHER_BYTES = 2 * 1024 * 1024
KERNEL_BYTES = 4 * 1024 * 1024
ROUTES = (
    (
        (6, 15, 4, 13, 3, 11, 7, 9, 1, 10, 2, 8, 0, 12, 5, 14),
        (5, 13, 3, 9, 0, 15, 1, 14, 7, 8, 4, 10, 2, 11, 6, 12),
        (3, 11, 6, 14, 5, 8, 4, 13, 2, 12, 1, 15, 7, 9, 0, 10),
        (1, 9, 0, 11, 6, 13, 2, 10, 5, 15, 7, 12, 4, 14, 3, 8),
    ),
    (
        (5, 12, 1, 13, 3, 15, 0, 9, 2, 8, 6, 10, 4, 11, 7, 14),
        (7, 15, 3, 8, 6, 10, 4, 11, 1, 14, 2, 13, 0, 12, 5, 9),
        (3, 11, 4, 15, 5, 9, 7, 13, 6, 10, 1, 8, 2, 14, 0, 12),
        (1, 9, 7, 11, 0, 13, 2, 14, 5, 12, 4, 15, 6, 8, 3, 10),
    ),
)


def layer_norm(values, gain, shift, axis):
    centred = values - jnp.mean(values, axis=axis, keepdims=True)
    variance = jnp.mean(centred * centred, axis=axis, keepdims=True)
    return centred * lax.rsqrt(variance + EPSILON) * gain + shift


def gated(rows, w_proj_gate):
    both = jnp.dot(rows, w_proj_gate, preferred_element_type=jnp.float32)
    hidden = both.shape[1] // 2
    return (jax.nn.sigmoid(both[:, hidden:]) * both[:, :hidden]).astype(jnp.bfloat16).astype(jnp.float32)


def lookup(tables, bits):
    words = []
    for values in tables:
        word = sum(value << (bits * place) for place, value in enumerate(values))
        words.append(jnp.int32(word - (1 << 32) if word >> 31 else word))
    word = jnp.where(lax.axis_index("grp") == 0, *words)
    device = lax.axis_index("row") * 2 + lax.axis_index("sub")
    return lax.shift_right_logical(word, device * bits) & ((1 << bits) - 1)


def place_of(sources, span):
    place = lookup([[source // 2 % span for source in table] for table in sources], 2)
    return place, lookup([[source % 2 for source in table] for table in sources], 1)


def copy_kernel(source_ref, target_ref):
    target_ref[...] = source_ref[...]


def flat_normed(values, gain, bias):
    flat = values.reshape(-1, values.shape[-1]).astype(jnp.float32)
    return layer_norm(flat, gain, bias, -1).astype(jnp.bfloat16)


def finish(left_ref, blocks, places, gating_ref, vectors_ref, w_out_ref):
    sums, gates = [], []
    for block, (place, half) in zip(blocks, places):
        left = left_ref[half], left_ref[1 - half]
        for row in range(left_ref.shape[1]):
            products = block[0] * left[0][row] + block[1] * left[1][row]
            sums.append(jnp.sum(products, axis=1))
        gates.append(gating_ref[place])
    triangle = jnp.concatenate(sums, axis=0).astype(jnp.bfloat16).astype(jnp.float32)
    hidden_normed = layer_norm(triangle, vectors_ref[2:3], vectors_ref[3:4], -1)
    mixed = jnp.dot(
        hidden_normed.astype(jnp.bfloat16), w_out_ref[...], preferred_element_type=jnp.float32
    )
    return (jnp.concatenate(gates, axis=0) * mixed).reshape(len(gates), -1, mixed.shape[-1])


def left_kernel(
    span,
    own_ref,
    other_ref,
    norm_gain_ref,
    norm_bias_ref,
    w_a_proj_ref,
    w_a_gate_ref,
    w_gate_ref,
    w_b_proj_ref,
    w_b_gate_ref,
    out_gain_ref,
    out_bias_ref,
    w_out_ref,
    left_ref,
    gating_ref,
    vectors_ref,
    w_right_ref,
):
    rows, cols, width = own_ref.shape
    for place, ref in enumerate((norm_gain_ref, norm_bias_ref, out_gain_ref, out_bias_ref)):
        vectors_ref[place : place + 1] = ref[...]
    w_right_ref[:, :width] = w_b_proj_ref[...]
    w_right_ref[:, width:] = w_b_gate_ref[...]
    sub = lax.axis_index("sub")
    gain, bias = norm_gain_ref[...], norm_bias_ref[...]
    own, other = flat_normed(own_ref[...], gain, bias), flat_normed(other_ref[...], gain, bias)
    w_left = jnp.concatenate([w_a_proj_ref[...], w_a_gate_ref[...]], axis=1)
    for values, half in ((own, sub), (other, 1 - sub)):
        left_ref[pl.ds(half, 1)] = gated(values, w_left).reshape(1, rows, cols, -1)
    gating = jax.nn.sigmoid(jnp.dot(own, w_gate_ref[...], preferred_element_type=jnp.float32))
    gating = gating.astype(jnp.bfloat16).astype(jnp.float32).reshape(rows, cols, width)
    for place in range(span):
        part = gating[:, place * rows : (place + 1) * rows]
        gating_ref[place] = part.reshape(rows * rows, width)


def first_kernel(
    span,
    routes,
    block_ref,
    left_ref,
    gating_ref,
    vectors_ref,
    w_right_ref,
    w_out_ref,
    update_ref,
):
    _, rows, cols, _ = block_ref.shape
    right = flat_normed(block_ref[...], vectors_ref[0:1], vectors_ref[1:2])
    right = gated(right, w_right_ref[...]).reshape(1, 2, rows, cols, -1)
    places = [place_of([table[0] for table in routes], span)]
    update_ref[...] = finish(left_ref, right, places, gating_ref, vectors_ref, w_out_ref)


def last_kernel(span, routes, *refs):
    block_refs = refs[: span - 1]
    (
        left_ref,
        gating_ref,
        first_ref,
        vectors_ref,
        w_right_ref,
        w_out_ref,
        update_ref,
        placed_ref,
        result_ref,
        done,
    ) = refs[span - 1 :]
    _, rows, cols, width = block_refs[0].shape
    right = []
    for ref in block_refs:
        normed = flat_normed(ref[...], vectors_ref[0:1], vectors_ref[1:2])
        right.append(gated(normed, w_right_ref[...]).reshape(2, rows, cols, -1))
    places = [place_of(sources, span) for sources in zip(*routes)]
    last = finish(left_ref, right, places[1:], gating_ref, vectors_ref, w_out_ref)
    placed_ref[pl.ds(places[0][0], 1)] = first_ref[...]
    for step in range(span - 1):
        placed_ref[pl.ds(places[step + 1][0], 1)] = last[step : step + 1]
    for row in range(rows):
        parts = [placed_ref[place, row * rows : (row + 1) * rows] for place in range(span)]
        result_ref[row] = jnp.concatenate(parts, axis=0).astype(jnp.bfloat16)
    copy = pltpu.make_async_copy(result_ref, update_ref, done)
    copy.start()
    copy.wait()


def gather_span(
    routes,
    pair_rep,
    norm_gain,
    norm_bias,
    w_a_proj,
    w_a_gate,
    w_b_proj,
    w_b_gate,
    w_gate,
    out_gain,
    out_bias,
    w_out,
):
    span = len(routes[0])
    block = pair_rep.shape
    rows, _, width = block
    params = pltpu.CompilerParams(vmem_limit_bytes=KERNEL_BYTES)
    cost = pl.CostEstimate(flops=10**8, bytes_accessed=10**6, transcendentals=0)

    def receive(values, sources):
        devices = 4 * span
        pairs = [
            (group * devices + source, group * devices + device)
            for group, table in enumerate(sources)
            for device, source in enumerate(table)
        ]
        return lax.ppermute(values, ("grp", "row", "sub"), pairs)

    swap = [device ^ 1 for device in range(4 * span)]
    other = receive(pair_rep, [swap] * len(routes))
    own = pl.pallas_call(
        copy_kernel,
        out_shape=jax.ShapeDtypeStruct(block, pair_rep.dtype),
        cost_estimate=cost,
        compiler_params=params,
    )(pair_rep)
    pair = jnp.stack([own, other])
    blocks = [receive(pair, sources) for sources in zip(*routes)]
    norm = (norm_gain[None], norm_bias[None])
    tail = (w_b_proj, w_b_gate, out_gain[None], out_bias[None], w_out)
    left, gating, vectors, w_right = pl.pallas_call(
        functools.partial(left_kernel, span),
        out_shape=(
            jax.ShapeDtypeStruct((2,) + block, jnp.float32),
            jax.ShapeDtypeStruct((span, rows * rows, width), jnp.float32),
            jax.ShapeDtypeStruct((4, width), jnp.float32),
            jax.ShapeDtypeStruct((width, 2 * width), w_b_proj.dtype),
        ),
        cost_estimate=cost,
        compiler_params=params,
    )(own, other, *norm, w_a_proj, w_a_gate, w_gate, *tail)
    update = pl.pallas_call(
        functools.partial(first_kernel, span, routes),
        out_shape=jax.ShapeDtypeStruct((1, rows * rows, width), jnp.float32),
        cost_estimate=cost,
        compiler_params=params,
    )(blocks[0], left, gating, vectors, w_right, w_out)
    return pl.pallas_call(
        functools.partial(last_kernel, span, routes),
        out_shape=jax.ShapeDtypeStruct(block, pair_rep.dtype),
        out_specs=pl.BlockSpec(memory_space=pl.ANY),
        scratch_shapes=[
            pltpu.VMEM((span, rows * rows, width), jnp.float32),
            pltpu.VMEM(block, pair_rep.dtype),
            pltpu.SemaphoreType.DMA,
        ],
        compiler_params=params,
    )(*blocks[1:], left, gating, update, vectors, w_right, w_out)


def exchange_channels(
    pair_rep,
    norm_gain,
    norm_bias,
    w_a_proj,
    w_a_gate,
    w_b_proj,
    w_b_gate,
    w_gate,
    out_gain,
    out_bias,
    w_out,
):
    hidden = w_a_proj.shape[1]
    w_inner = jnp.concatenate([w_a_proj, w_a_gate, w_b_proj, w_b_gate], axis=1)
    normed = layer_norm(pair_rep.astype(jnp.float32), norm_gain, norm_bias, -1).astype(jnp.bfloat16)
    inner = jnp.einsum("rkc,cm->mrk", normed, w_inner, preferred_element_type=jnp.float32)
    left_local = (jax.nn.sigmoid(inner[hidden : 2 * hidden]) * inner[:hidden]).astype(jnp.bfloat16)
    right_local = (
        jax.nn.sigmoid(inner[3 * hidden : 4 * hidden]) * inner[2 * hidden : 3 * hidden]
    ).astype(jnp.bfloat16)
    gating = jax.nn.sigmoid(
        jnp.einsum("rkc,cd->rkd", normed, w_gate, preferred_element_type=jnp.float32)
    ).astype(jnp.bfloat16)
    left_chan, right_chan = (
        lax.all_to_all(left_local, "row", split_axis=0, concat_axis=1, tiled=True),
        lax.all_to_all(right_local, "row", split_axis=0, concat_axis=1, tiled=True),
    )
    left_rows = lax.all_to_all(left_chan, "sub", split_axis=1, concat_axis=2, tiled=True)
    triangle = jnp.einsum(
        "hik,hjk->hij",
        left_rows,
        lax.all_gather(right_chan, "sub", axis=2, tiled=True),
        preferred_element_type=jnp.float32,
    ).astype(jnp.bfloat16)
    regrouped = lax.all_to_all(
        lax.all_to_all(triangle, "sub", split_axis=2, concat_axis=1, tiled=True),
        "row",
        split_axis=1,
        concat_axis=0,
        tiled=True,
    )
    hidden_normed = layer_norm(
        regrouped.astype(jnp.float32), out_gain[:, None, None], out_bias[:, None, None], 0
    ).astype(jnp.bfloat16)
    mixed = jnp.einsum("hrj,hc->rjc", hidden_normed, w_out, preferred_element_type=jnp.float32)
    return (gating.astype(jnp.float32) * mixed).astype(jnp.bfloat16)


def solution(mesh):
    n_row, n_sub = mesh.shape["row"], mesh.shape["sub"]

    def per_device(pair_rep, *weights):
        rows, cols, _ = pair_rep.shape
        gathered = n_row * n_sub * pair_rep.size * pair_rep.dtype.itemsize
        routed = (mesh.shape["grp"], n_row, n_sub) == (2, 8, 2) and cols == n_row // 2 * rows
        if routed and gathered <= GATHER_BYTES:
            return gather_span(ROUTES, pair_rep, *weights)
        return exchange_channels(pair_rep, *weights)

    in_specs = (P(("grp", "row"), "sub", None), P(), P(), P(), P(), P(), P(), P(), P(), P(), P())
    out_specs = P(("grp", "row"), "sub", None)
    return jax.shard_map(
        per_device, mesh=mesh, in_specs=in_specs, out_specs=out_specs, check_vma=False
    )
```

```python
import functools

import jax
import jax.numpy as jnp
from jax import lax
from jax.experimental import pallas as pl
from jax.experimental.pallas import tpu as pltpu
from jax.sharding import PartitionSpec as P

EPSILON = 1e-05
GATHER_BYTES = 2 * 1024 * 1024
KERNEL_BYTES = 4 * 1024 * 1024
ROUTES = (
    (
        (6, 15, 4, 13, 3, 11, 7, 9, 1, 10, 2, 8, 0, 12, 5, 14),
        (5, 13, 3, 9, 0, 15, 1, 14, 7, 8, 4, 10, 2, 11, 6, 12),
        (3, 11, 6, 14, 5, 8, 4, 13, 2, 12, 1, 15, 7, 9, 0, 10),
        (1, 9, 0, 11, 6, 13, 2, 10, 5, 15, 7, 12, 4, 14, 3, 8),
    ),
    (
        (5, 12, 1, 13, 3, 15, 0, 9, 2, 8, 6, 10, 4, 11, 7, 14),
        (7, 15, 3, 8, 6, 10, 4, 11, 1, 14, 2, 13, 0, 12, 5, 9),
        (3, 11, 4, 15, 5, 9, 7, 13, 6, 10, 1, 8, 2, 14, 0, 12),
        (1, 9, 7, 11, 0, 13, 2, 14, 5, 12, 4, 15, 6, 8, 3, 10),
    ),
)


def layer_norm(values, gain, shift, axis):
    centred = values - jnp.mean(values, axis=axis, keepdims=True)
    variance = jnp.mean(centred * centred, axis=axis, keepdims=True)
    return centred * lax.rsqrt(variance + EPSILON) * gain + shift


def gated(rows, w_proj_gate):
    both = jnp.dot(rows, w_proj_gate, preferred_element_type=jnp.float32)
    hidden = both.shape[1] // 2
    return (jax.nn.sigmoid(both[:, hidden:]) * both[:, :hidden]).astype(jnp.bfloat16).astype(jnp.float32)


def lookup(tables, bits):
    words = []
    for values in tables:
        word = sum(value << (bits * place) for place, value in enumerate(values))
        words.append(jnp.int32(word - (1 << 32) if word >> 31 else word))
    word = jnp.where(lax.axis_index("grp") == 0, *words)
    device = lax.axis_index("row") * 2 + lax.axis_index("sub")
    return lax.shift_right_logical(word, device * bits) & ((1 << bits) - 1)


def place_of(sources, span):
    place = lookup([[source // 2 % span for source in table] for table in sources], 2)
    return place, lookup([[source % 2 for source in table] for table in sources], 1)


def copy_kernel(source_ref, target_ref):
    target_ref[...] = source_ref[...]


def flat_normed(values, gain, bias):
    flat = values.reshape(-1, values.shape[-1]).astype(jnp.float32)
    return layer_norm(flat, gain, bias, -1).astype(jnp.bfloat16)


def finish(left_ref, blocks, places, gating_ref, vectors_ref, w_out_ref):
    sums, gates = [], []
    for block, (place, half) in zip(blocks, places):
        left = left_ref[half], left_ref[1 - half]
        for row in range(left_ref.shape[1]):
            products = block[0] * left[0][row] + block[1] * left[1][row]
            sums.append(jnp.sum(products, axis=1))
        gates.append(gating_ref[place])
    triangle = jnp.concatenate(sums, axis=0).astype(jnp.bfloat16).astype(jnp.float32)
    hidden_normed = layer_norm(triangle, vectors_ref[2:3], vectors_ref[3:4], -1)
    mixed = jnp.dot(
        hidden_normed.astype(jnp.bfloat16), w_out_ref[...], preferred_element_type=jnp.float32
    )
    return (jnp.concatenate(gates, axis=0) * mixed).reshape(len(gates), -1, mixed.shape[-1])


def left_kernel(
    span,
    own_ref,
    other_ref,
    norm_gain_ref,
    norm_bias_ref,
    w_a_proj_ref,
    w_a_gate_ref,
    w_gate_ref,
    w_b_proj_ref,
    w_b_gate_ref,
    out_gain_ref,
    out_bias_ref,
    w_out_ref,
    left_ref,
    gating_ref,
    vectors_ref,
    w_right_ref,
):
    rows, cols, width = own_ref.shape
    for place, ref in enumerate((norm_gain_ref, norm_bias_ref, out_gain_ref, out_bias_ref)):
        vectors_ref[place : place + 1] = ref[...]
    w_right_ref[:, :width] = w_b_proj_ref[...]
    w_right_ref[:, width:] = w_b_gate_ref[...]
    sub = lax.axis_index("sub")
    gain, bias = norm_gain_ref[...], norm_bias_ref[...]
    own, other = flat_normed(own_ref[...], gain, bias), flat_normed(other_ref[...], gain, bias)
    w_left = jnp.concatenate([w_a_proj_ref[...], w_a_gate_ref[...]], axis=1)
    for values, half in ((own, sub), (other, 1 - sub)):
        left_ref[pl.ds(half, 1)] = gated(values, w_left).reshape(1, rows, cols, -1)
    gating = jax.nn.sigmoid(jnp.dot(own, w_gate_ref[...], preferred_element_type=jnp.float32))
    gating = gating.astype(jnp.bfloat16).astype(jnp.float32).reshape(rows, cols, width)
    for place in range(span):
        part = gating[:, place * rows : (place + 1) * rows]
        gating_ref[place] = part.reshape(rows * rows, width)


def first_kernel(
    span,
    routes,
    block_ref,
    left_ref,
    gating_ref,
    vectors_ref,
    w_right_ref,
    w_out_ref,
    update_ref,
):
    _, rows, cols, _ = block_ref.shape
    right = flat_normed(block_ref[...], vectors_ref[0:1], vectors_ref[1:2])
    right = gated(right, w_right_ref[...]).reshape(1, 2, rows, cols, -1)
    places = [place_of([table[0] for table in routes], span)]
    update_ref[...] = finish(left_ref, right, places, gating_ref, vectors_ref, w_out_ref)


def last_kernel(span, routes, *refs):
    block_refs = refs[: span - 1]
    (
        left_ref,
        gating_ref,
        first_ref,
        vectors_ref,
        w_right_ref,
        w_out_ref,
        update_ref,
        placed_ref,
        result_ref,
        done,
    ) = refs[span - 1 :]
    _, rows, cols, width = block_refs[0].shape
    right = jnp.stack([ref[...] for ref in block_refs])
    right = gated(flat_normed(right, vectors_ref[0:1], vectors_ref[1:2]), w_right_ref[...])
    right = right.reshape(span - 1, 2, rows, cols, -1)
    places = [place_of(sources, span) for sources in zip(*routes)]
    last = finish(left_ref, right, places[1:], gating_ref, vectors_ref, w_out_ref)
    placed_ref[pl.ds(places[0][0], 1)] = first_ref[...]
    for step in range(span - 1):
        placed_ref[pl.ds(places[step + 1][0], 1)] = last[step : step + 1]
    for row in range(rows):
        parts = [placed_ref[place, row * rows : (row + 1) * rows] for place in range(span)]
        result_ref[row] = jnp.concatenate(parts, axis=0).astype(jnp.bfloat16)
    copy = pltpu.make_async_copy(result_ref, update_ref, done)
    copy.start(priority=1)
    copy.wait()


def gather_span(
    routes,
    pair_rep,
    norm_gain,
    norm_bias,
    w_a_proj,
    w_a_gate,
    w_b_proj,
    w_b_gate,
    w_gate,
    out_gain,
    out_bias,
    w_out,
):
    span = len(routes[0])
    block = pair_rep.shape
    rows, _, width = block
    params = pltpu.CompilerParams(vmem_limit_bytes=KERNEL_BYTES)
    cost = pl.CostEstimate(flops=10**8, bytes_accessed=10**6, transcendentals=0)

    def receive(values, sources):
        devices = 4 * span
        pairs = [
            (group * devices + source, group * devices + device)
            for group, table in enumerate(sources)
            for device, source in enumerate(table)
        ]
        return lax.ppermute(values, ("grp", "row", "sub"), pairs)

    swap = [device ^ 1 for device in range(4 * span)]
    other = receive(pair_rep, [swap] * len(routes))
    own = pl.pallas_call(
        copy_kernel,
        out_shape=jax.ShapeDtypeStruct(block, pair_rep.dtype),
        cost_estimate=cost,
        compiler_params=params,
    )(pair_rep)
    pair = jnp.stack([own, other])
    blocks = [receive(pair, sources) for sources in zip(*routes)]
    norm = (norm_gain[None], norm_bias[None])
    tail = (w_b_proj, w_b_gate, out_gain[None], out_bias[None], w_out)
    left, gating, vectors, w_right = pl.pallas_call(
        functools.partial(left_kernel, span),
        out_shape=(
            jax.ShapeDtypeStruct((2,) + block, jnp.float32),
            jax.ShapeDtypeStruct((span, rows * rows, width), jnp.float32),
            jax.ShapeDtypeStruct((4, width), jnp.float32),
            jax.ShapeDtypeStruct((width, 2 * width), w_b_proj.dtype),
        ),
        cost_estimate=cost,
        compiler_params=params,
    )(own, other, *norm, w_a_proj, w_a_gate, w_gate, *tail)
    update = pl.pallas_call(
        functools.partial(first_kernel, span, routes),
        out_shape=jax.ShapeDtypeStruct((1, rows * rows, width), jnp.float32),
        cost_estimate=cost,
        compiler_params=params,
    )(blocks[0], left, gating, vectors, w_right, w_out)
    return pl.pallas_call(
        functools.partial(last_kernel, span, routes),
        out_shape=jax.ShapeDtypeStruct(block, pair_rep.dtype),
        out_specs=pl.BlockSpec(memory_space=pl.ANY),
        scratch_shapes=[
            pltpu.VMEM((span, rows * rows, width), jnp.float32),
            pltpu.VMEM(block, pair_rep.dtype),
            pltpu.SemaphoreType.DMA,
        ],
        compiler_params=params,
    )(*blocks[1:], left, gating, update, vectors, w_right, w_out)


def exchange_channels(
    pair_rep,
    norm_gain,
    norm_bias,
    w_a_proj,
    w_a_gate,
    w_b_proj,
    w_b_gate,
    w_gate,
    out_gain,
    out_bias,
    w_out,
):
    hidden = w_a_proj.shape[1]
    w_inner = jnp.concatenate([w_a_proj, w_a_gate, w_b_proj, w_b_gate], axis=1)
    normed = layer_norm(pair_rep.astype(jnp.float32), norm_gain, norm_bias, -1).astype(jnp.bfloat16)
    inner = jnp.einsum("rkc,cm->mrk", normed, w_inner, preferred_element_type=jnp.float32)
    left_local = (jax.nn.sigmoid(inner[hidden : 2 * hidden]) * inner[:hidden]).astype(jnp.bfloat16)
    right_local = (
        jax.nn.sigmoid(inner[3 * hidden : 4 * hidden]) * inner[2 * hidden : 3 * hidden]
    ).astype(jnp.bfloat16)
    gating = jax.nn.sigmoid(
        jnp.einsum("rkc,cd->rkd", normed, w_gate, preferred_element_type=jnp.float32)
    ).astype(jnp.bfloat16)
    left_chan, right_chan = (
        lax.all_to_all(left_local, "row", split_axis=0, concat_axis=1, tiled=True),
        lax.all_to_all(right_local, "row", split_axis=0, concat_axis=1, tiled=True),
    )
    left_rows = lax.all_to_all(left_chan, "sub", split_axis=1, concat_axis=2, tiled=True)
    triangle = jnp.einsum(
        "hik,hjk->hij",
        left_rows,
        lax.all_gather(right_chan, "sub", axis=2, tiled=True),
        preferred_element_type=jnp.float32,
    ).astype(jnp.bfloat16)
    regrouped = lax.all_to_all(
        lax.all_to_all(triangle, "sub", split_axis=2, concat_axis=1, tiled=True),
        "row",
        split_axis=1,
        concat_axis=0,
        tiled=True,
    )
    hidden_normed = layer_norm(
        regrouped.astype(jnp.float32), out_gain[:, None, None], out_bias[:, None, None], 0
    ).astype(jnp.bfloat16)
    mixed = jnp.einsum("hrj,hc->rjc", hidden_normed, w_out, preferred_element_type=jnp.float32)
    return (gating.astype(jnp.float32) * mixed).astype(jnp.bfloat16)


def solution(mesh):
    n_row, n_sub = mesh.shape["row"], mesh.shape["sub"]

    def per_device(pair_rep, *weights):
        rows, cols, _ = pair_rep.shape
        gathered = n_row * n_sub * pair_rep.size * pair_rep.dtype.itemsize
        routed = (mesh.shape["grp"], n_row, n_sub) == (2, 8, 2) and cols == n_row // 2 * rows
        if routed and gathered <= GATHER_BYTES:
            return gather_span(ROUTES, pair_rep, *weights)
        return exchange_channels(pair_rep, *weights)

    in_specs = (P(("grp", "row"), "sub", None), P(), P(), P(), P(), P(), P(), P(), P(), P(), P())
    out_specs = P(("grp", "row"), "sub", None)
    return jax.shard_map(
        per_device, mesh=mesh, in_specs=in_specs, out_specs=out_specs, check_vma=False
    )
```
